32 devices in a mesh: cells: 16 (over z, y, x), snaps: 2 (over core).
Axes of the slice: x: 2, y: 2, z: 4, core: 2. Of those that a mesh axis runs over, the one named last changes fastest.
Arguments:
- snapshots: float32 [65536, 512], P('cells', 'snaps'), may hold values from -6 to 6
- sketch: float32 [512, 32], P('snaps'), may hold values from -6 to 6
Outputs:
- basis: float32 [32, 65536], P(None, 'cells')
- coefficients: float32 [32, 512], P(None, 'snaps')
The draws below stay inside these ranges and needn't reach their ends.
All inputs are finite; a program needn't handle non-finite values.
Results may differ from the reference program's by a relative error of at most 0.0003.
Values sent between devices are 32-bit elements; how exact they have to be, the bound alone decides.
No kernel may reach another device: no remote copies, remote signals or barrier semaphores. Data moves between devices by JAX's collectives and lax.ppermute only.
A program may use at most 64 MiB of HBM per device.

```python
import math
import jax
import jax.numpy as jnp
from jax import lax

RANK = 32
CELLS = 65536
SNAPS = 512


def shard_levels(rng, shape, shards, least, top_value):
    def one(axis_at, shards_of):
        heights = jax.random.uniform(jax.random.fold_in(jax.random.fold_in(rng, 6), axis_at), (shards_of,), jnp.float32, least / len(shards), top_value / len(shards))
        return jnp.repeat(jnp.exp(heights), shape[axis_at] // shards_of).reshape((-1,) + (1,) * (len(shape) - axis_at - 1))

    level = one(*shards[0])
    for cut in shards[1:]:
        level = level * one(*cut)
    return level


def centred(key, dims, deviation, most, split=(), kind=jnp.bfloat16):
    result = deviation * jax.random.normal(key, dims, jnp.float32)
    if split:
        result = result * shard_levels(key, dims, split, -0.22, 0.18)
    return jnp.clip(result, -most, most).astype(kind)


def setup_inputs(seed: int = 0) -> dict:
    streams_of = jax.random.split(jax.random.key(seed), 3)
    return {
        "snapshots": centred(streams_of[0], (CELLS, SNAPS), 1.0, 6.0, ((0, 16), (1, 2)), jnp.float32),
        "sketch": centred(streams_of[1], (SNAPS, RANK), 1.0, 6.0, ((0, 2),), jnp.float32),
    }


def reference(snapshots, sketch):
    sketched = jnp.einsum('sk,ms->km', sketch, snapshots, precision=lax.Precision.HIGHEST)
    factor_q, factor_r = jnp.linalg.qr(sketched.T)
    diagonal = jnp.diagonal(factor_r)
    sense = jnp.where(diagonal < 0, -1.0, 1.0).astype(factor_q.dtype)
    orth = (factor_q * sense[None, :]).T
    coefficients = jnp.dot(orth, snapshots, precision=lax.Precision.HIGHEST)
    basis = orth * math.sqrt(CELLS)
    return (basis, coefficients)
```

```python
import math

import jax
import jax.numpy as jnp
from jax import lax
from jax.experimental import pallas as pl
from jax.experimental.pallas import tpu as pltpu
from jax.sharding import PartitionSpec as P

HIGHEST = lax.Precision.HIGHEST
LANES = 128


def swap(block, axis, offset):
    count = lax.axis_size(axis)
    return lax.ppermute(block, axis, [(at, at ^ offset) for at in range(count)])


def tree_sum(parts):
    while len(parts) > 1:
        parts = [parts[at] + parts[at + 1] for at in range(0, len(parts), 2)]
    return parts[0]


def contract(left, right, left_dim, right_dim):
    dims = (((left_dim,), (right_dim,)), ((), ()))
    return lax.dot_general(left, right, dims, precision=HIGHEST, preferred_element_type=jnp.float32)


def sketch_kernel(sketch_ref, snapshots_ref, out_ref):
    out_ref[...] = contract(sketch_ref[...], snapshots_ref[...], 0, 1)


def sketch_rows(snapshots, sketch):
    cells, snaps = snapshots.shape
    rank = sketch.shape[1]
    tile = min(cells, 1024)
    return pl.pallas_call(
        sketch_kernel,
        grid=(cells // tile,),
        in_specs=[
            pl.BlockSpec((snaps, rank), lambda at: (0, 0)),
            pl.BlockSpec((tile, snaps), lambda at: (at, 0)),
        ],
        out_specs=pl.BlockSpec((rank, tile), lambda at: (0, at)),
        out_shape=jax.ShapeDtypeStruct((rank, cells), jnp.float32),
        name="sketch_rows",
    )(sketch, snapshots)


def project_kernel(parts, *refs):
    snapshots_ref = refs[parts]
    rows_ref, sums_ref = refs[parts + 1:]
    rank = rows_ref.shape[0]
    snaps = snapshots_ref.shape[1]
    rows = tree_sum([ref[...] for ref in refs[:parts]])
    rows_ref[...] = rows

    @pl.when(pl.program_id(0) == 0)
    def _():
        sums_ref[...] = jnp.zeros_like(sums_ref)

    sums_ref[:, :snaps] += contract(rows, snapshots_ref[...], 1, 0)
    sums_ref[:, snaps:snaps + rank] += contract(rows, rows, 1, 1)


def project(parts, snapshots):
    cells, snaps = snapshots.shape
    rank = parts[0].shape[0]
    tile = min(cells, 1024)
    width = snaps + -(-rank // LANES) * LANES
    return pl.pallas_call(
        lambda *refs: project_kernel(len(parts), *refs),
        grid=(cells // tile,),
        in_specs=[pl.BlockSpec((rank, tile), lambda at: (0, at))] * len(parts)
        + [pl.BlockSpec((tile, snaps), lambda at: (at, 0))],
        out_specs=[
            pl.BlockSpec((rank, tile), lambda at: (0, at)),
            pl.BlockSpec((rank, width), lambda at: (0, 0)),
        ],
        out_shape=[
            jax.ShapeDtypeStruct((rank, cells), jnp.float32),
            jax.ShapeDtypeStruct((rank, width), jnp.float32),
        ],
        name="project",
    )(*parts, snapshots)


def lower_inverse(gram):
    rank = gram.shape[0]
    row_at = lax.broadcasted_iota(jnp.int32, (rank, rank), 0)
    column_at = lax.broadcasted_iota(jnp.int32, (rank, rank), 1)
    identity = jnp.where(row_at == column_at, 1.0, 0.0)
    both = jnp.concatenate([gram, identity], axis=1)
    place = lax.broadcasted_iota(jnp.int32, (rank, 1), 0)
    for step in range(rank - 1):
        row = both[step:step + 1, :]
        column = both[:, step:step + 1]
        factor = jnp.where(place > step, column, 0.0) / both[step:step + 1, step:step + 1]
        both = both - factor * row
    pivots = jnp.sum(jnp.where(row_at == column_at, both[:, :rank], 0.0), axis=1, keepdims=True)
    return both[:, rank:] / jnp.sqrt(pivots)


def factor_kernel(parts, scale, *refs):
    rows_ref = refs[parts]
    basis_ref, coefficients_ref, inverse_ref = refs[parts + 1:]
    rank = rows_ref.shape[0]
    snaps = coefficients_ref.shape[1]

    @pl.when(pl.program_id(0) == 0)
    def _():
        sums = tree_sum([ref[...] for ref in refs[:parts]])
        inverse = lower_inverse(sums[:, snaps:snaps + rank])
        coefficients_ref[...] = contract(inverse, sums[:, :snaps], 1, 0)
        inverse_ref[...] = inverse * scale

    basis_ref[...] = contract(inverse_ref[...], rows_ref[...], 1, 0)


def factor(parts, rows, scale, snaps):
    rank, cells = rows.shape
    tile = min(cells, 1024)
    width = parts[0].shape[1]
    return pl.pallas_call(
        lambda *refs: factor_kernel(len(parts), scale, *refs),
        grid=(cells // tile,),
        in_specs=[pl.BlockSpec((rank, width), lambda at: (0, 0))] * len(parts)
        + [pl.BlockSpec((rank, tile), lambda at: (0, at))],
        out_specs=[
            pl.BlockSpec((rank, tile), lambda at: (0, at)),
            pl.BlockSpec((rank, snaps), lambda at: (0, 0)),
        ],
        out_shape=[
            jax.ShapeDtypeStruct((rank, cells), jnp.float32),
            jax.ShapeDtypeStruct((rank, snaps), jnp.float32),
        ],
        scratch_shapes=[pltpu.VMEM((rank, rank), jnp.float32)],
        name="factor",
    )(*parts, rows)


def exchange(block, axis, radix):
    count = lax.axis_size(axis)
    step = 1
    parts = [block]
    while step < count:
        block = tree_sum(parts)
        group = min(radix, count // step)
        parts = [block] + [swap(block, axis, step * at) for at in range(1, group)]
        step *= group
    return parts


def shards(snapshots, sketch):
    total_cells = snapshots.shape[0] * lax.axis_size("cells")
    partial_rows = sketch_rows(snapshots, sketch)
    rows, sums = project(exchange(partial_rows, "snaps", 2), snapshots)
    basis, coefficients = factor(exchange(sums, "cells", 4), rows, math.sqrt(total_cells), snapshots.shape[1])
    return (basis, coefficients)


def solution(mesh):
    return jax.shard_map(
        shards,
        mesh=mesh,
        in_specs=(P("cells", "snaps"), P("snaps", None)),
        out_specs=(P(None, "cells"), P(None, "snaps")),
        check_vma=False,
    )
```

```python
import math

import jax
import jax.numpy as jnp
from jax import lax
from jax.experimental import pallas as pl
from jax.experimental.pallas import tpu as pltpu
from jax.sharding import PartitionSpec as P

HIGHEST = lax.Precision.HIGHEST
LANES = 128


def swap(block, axis, offset):
    count = lax.axis_size(axis)
    return lax.ppermute(block, axis, [(at, at ^ offset) for at in range(count)])


def tree_sum(parts):
    while len(parts) > 1:
        parts = [parts[at] + parts[at + 1] for at in range(0, len(parts), 2)]
    return parts[0]


def contract(left, right, left_dim, right_dim):
    dims = (((left_dim,), (right_dim,)), ((), ()))
    return lax.dot_general(left, right, dims, precision=HIGHEST, preferred_element_type=jnp.float32)


def sketch_kernel(sketch_ref, snapshots_ref, out_ref):
    out_ref[...] = contract(sketch_ref[...], snapshots_ref[...], 1, 1)


def sketch_rows(snapshots, sketch):
    cells, snaps = snapshots.shape
    rank = sketch.shape[1]
    tile = min(cells, 1024)
    return pl.pallas_call(
        sketch_kernel,
        grid=(cells // tile,),
        in_specs=[
            pl.BlockSpec((rank, snaps), lambda at: (0, 0)),
            pl.BlockSpec((tile, snaps), lambda at: (at, 0)),
        ],
        out_specs=pl.BlockSpec((rank, tile), lambda at: (0, at)),
        out_shape=jax.ShapeDtypeStruct((rank, cells), jnp.float32),
        name="sketch_rows",
    )(sketch.T, snapshots)


def project_kernel(parts, *refs):
    snapshots_ref = refs[parts]
    rows_ref, sums_ref = refs[parts + 1:]
    rank = rows_ref.shape[0]
    snaps = snapshots_ref.shape[1]
    rows = tree_sum([ref[...] for ref in refs[:parts]])
    rows_ref[...] = rows

    @pl.when(pl.program_id(0) == 0)
    def _():
        sums_ref[...] = jnp.zeros_like(sums_ref)

    sums_ref[:, :snaps] += contract(rows, snapshots_ref[...], 1, 0)
    sums_ref[:, snaps:snaps + rank] += contract(rows, rows, 1, 1)


def project(parts, snapshots):
    cells, snaps = snapshots.shape
    rank = parts[0].shape[0]
    tile = min(cells, 1024)
    width = snaps + -(-rank // LANES) * LANES
    return pl.pallas_call(
        lambda *refs: project_kernel(len(parts), *refs),
        grid=(cells // tile,),
        in_specs=[pl.BlockSpec((rank, tile), lambda at: (0, at))] * len(parts)
        + [pl.BlockSpec((tile, snaps), lambda at: (at, 0))],
        out_specs=[
            pl.BlockSpec((rank, tile), lambda at: (0, at)),
            pl.BlockSpec((rank, width), lambda at: (0, 0)),
        ],
        out_shape=[
            jax.ShapeDtypeStruct((rank, cells), jnp.float32),
            jax.ShapeDtypeStruct((rank, width), jnp.float32),
        ],
        name="project",
    )(*parts, snapshots)


def lower_inverse(gram):
    rank = gram.shape[0]
    row_at = lax.broadcasted_iota(jnp.int32, (rank, rank), 0)
    column_at = lax.broadcasted_iota(jnp.int32, (rank, rank), 1)
    identity = jnp.where(row_at == column_at, 1.0, 0.0)
    both = jnp.concatenate([gram, identity], axis=1)
    place = lax.broadcasted_iota(jnp.int32, (rank, 1), 0)
    for step in range(rank - 1):
        row = both[step:step + 1, :]
        column = both[:, step:step + 1]
        factor = jnp.where(place > step, column, 0.0) / both[step:step + 1, step:step + 1]
        both = both - factor * row
    pivots = jnp.sum(jnp.where(row_at == column_at, both[:, :rank], 0.0), axis=1, keepdims=True)
    return both[:, rank:] / jnp.sqrt(pivots)


def factor_kernel(parts, scale, *refs):
    rows_ref = refs[parts]
    basis_ref, coefficients_ref, inverse_ref = refs[parts + 1:]
    rank = rows_ref.shape[0]
    snaps = coefficients_ref.shape[1]

    @pl.when(pl.program_id(0) == 0)
    def _():
        sums = tree_sum([ref[...] for ref in refs[:parts]])
        inverse = lower_inverse(sums[:, snaps:snaps + rank])
        coefficients_ref[...] = contract(inverse, sums[:, :snaps], 1, 0)
        inverse_ref[...] = inverse * scale

    basis_ref[...] = contract(inverse_ref[...], rows_ref[...], 1, 0)


def factor(parts, rows, scale, snaps):
    rank, cells = rows.shape
    tile = min(cells, 1024)
    width = parts[0].shape[1]
    return pl.pallas_call(
        lambda *refs: factor_kernel(len(parts), scale, *refs),
        grid=(cells // tile,),
        in_specs=[pl.BlockSpec((rank, width), lambda at: (0, 0))] * len(parts)
        + [pl.BlockSpec((rank, tile), lambda at: (0, at))],
        out_specs=[
            pl.BlockSpec((rank, tile), lambda at: (0, at)),
            pl.BlockSpec((rank, snaps), lambda at: (0, 0)),
        ],
        out_shape=[
            jax.ShapeDtypeStruct((rank, cells), jnp.float32),
            jax.ShapeDtypeStruct((rank, snaps), jnp.float32),
        ],
        scratch_shapes=[pltpu.VMEM((rank, rank), jnp.float32)],
        name="factor",
    )(*parts, rows)


def exchange(block, axis, radix):
    count = lax.axis_size(axis)
    step = 1
    parts = [block]
    while step < count:
        block = tree_sum(parts)
        group = min(radix, count // step)
        if group == 2:
            parts = [block, swap(block, axis, step)]
        else:
            groups = [[base + step * at for at in range(group)] for base in range(count) if base // step % group == 0]
            copies = jnp.broadcast_to(block, (group,) + block.shape)
            got = lax.all_to_all(copies, axis, 0, 0, axis_index_groups=groups)
            parts = [got[at] for at in range(group)]
        step *= group
    return parts


def shards(snapshots, sketch):
    total_cells = snapshots.shape[0] * lax.axis_size("cells")
    partial_rows = sketch_rows(snapshots, sketch)
    rows, sums = project(exchange(partial_rows, "snaps", 2), snapshots)
    basis, coefficients = factor(exchange(sums, "cells", 4), rows, math.sqrt(total_cells), snapshots.shape[1])
    return (basis, coefficients)


def solution(mesh):
    return jax.shard_map(
        shards,
        mesh=mesh,
        in_specs=(P("cells", "snaps"), P("snaps", None)),
        out_specs=(P(None, "cells"), P(None, "snaps")),
        check_vma=False,
    )
```

```python
import math

import jax
import jax.numpy as jnp
from jax import lax
from jax.experimental import pallas as pl
from jax.experimental.pallas import tpu as pltpu
from jax.sharding import PartitionSpec as P

LANES = 128
CHUNK = 512
MIB = 1 << 20
VMEM = pl.BlockSpec(memory_space=pltpu.VMEM)
HBM = pl.BlockSpec(memory_space=pltpu.HBM)


def limit(mebibytes):
    return pltpu.CompilerParams(vmem_limit_bytes=mebibytes * MIB)


def in_hbm(block):
    return pltpu.with_memory_space_constraint(block, pltpu.HBM)


def swap(block, axis, offset):
    count = lax.axis_size(axis)
    return lax.ppermute(block, axis, [(at, at ^ offset) for at in range(count)])


def tree_sum(parts):
    while len(parts) > 1:
        parts = [parts[at] + parts[at + 1] for at in range(0, len(parts), 2)]
    return parts[0]


def thirds(block):
    high = block.astype(jnp.bfloat16)
    rest = block - high.astype(jnp.float32)
    middle = rest.astype(jnp.bfloat16)
    low = (rest - middle.astype(jnp.float32)).astype(jnp.bfloat16)
    return high, middle, low


def product(left, right, right_dim):
    rank = left.shape[0] // 3
    dims = (((1,), (right_dim,)), ((), ()))
    high, middle, low = [
        lax.dot_general(left[:rank * (3 - at)], part, dims, preferred_element_type=jnp.float32)
        for at, part in enumerate(right)
    ]
    small = high[2 * rank:] + (middle[rank:] + low)
    return high[:rank] + ((high[rank:2 * rank] + middle[:rank]) + small)


def sketch_kernel(sketch_ref, snapshots_ref, out_ref, held, sketch_held, arrived):
    chunk = min(CHUNK, held.shape[0])
    chunks = held.shape[0] // chunk
    first = pltpu.make_async_copy(sketch_ref, sketch_held, arrived.at[chunks])
    first.start()
    copies = []
    for at in range(chunks):
        rows = pl.ds(at * chunk, chunk)
        copies.append(pltpu.make_async_copy(snapshots_ref.at[rows], held.at[rows], arrived.at[at]))
        copies[-1].start()
    first.wait()
    sketch = jnp.concatenate(thirds(sketch_held[...]), axis=0)
    for at, copy in enumerate(copies):
        rows = pl.ds(at * chunk, chunk)
        copy.wait()
        out_ref[:, rows] = product(sketch, thirds(held[rows, :]), 1)


def sketch_rows(snapshots, sketch):
    cells, snaps = snapshots.shape
    rank = sketch.shape[1]
    return pl.pallas_call(
        sketch_kernel,
        in_specs=[HBM] * 2,
        out_specs=[VMEM] * 2,
        out_shape=[
            pltpu.VMEM((rank, cells), jnp.float32),
            pltpu.VMEM((cells, snaps), jnp.float32),
        ],
        scratch_shapes=[
            pltpu.VMEM((rank, snaps), jnp.float32),
            pltpu.SemaphoreType.DMA((-(-cells // CHUNK) + 1,)),
        ],
        compiler_params=limit(16),
        name="sketch_rows",
    )(in_hbm(sketch.T), in_hbm(snapshots))


def project_kernel(parts, *refs):
    snapshots_ref = refs[parts]
    rows_ref, gram_ref, sums_ref = refs[parts + 1:]
    rank, cells = rows_ref.shape
    chunk = min(CHUNK, cells)
    sums = jnp.zeros(sums_ref.shape, jnp.float32)
    gram = jnp.zeros((rank, rank), jnp.float32)
    for at in range(cells // chunk):
        span = pl.ds(at * chunk, chunk)
        rows = tree_sum([ref[:, span] for ref in refs[:parts]])
        rows_ref[:, span] = rows
        split = thirds(rows)
        left = jnp.concatenate(split, axis=0)
        sums += product(left, thirds(snapshots_ref[span, :]), 0)
        gram += product(left, split, 1)
    sums_ref[...] = sums
    gram_ref[...] = jnp.zeros(gram_ref.shape, jnp.float32)
    gram_ref[:, :rank] = gram


def project(parts, snapshots):
    cells, snaps = snapshots.shape
    rank = parts[0].shape[0]
    return pl.pallas_call(
        lambda *refs: project_kernel(len(parts), *refs),
        in_specs=[VMEM] * (len(parts) + 1),
        out_specs=[VMEM] * 3,
        out_shape=[
            jax.ShapeDtypeStruct((rank, cells), jnp.float32),
            jax.ShapeDtypeStruct((rank, -(-rank // LANES) * LANES), jnp.float32),
            jax.ShapeDtypeStruct((rank, snaps), jnp.float32),
        ],
        compiler_params=limit(16),
        name="project",
    )(*parts, snapshots)


def lower_inverse(gram):
    rank = gram.shape[0]
    row_at = lax.broadcasted_iota(jnp.int32, (rank, rank), 0)
    column_at = lax.broadcasted_iota(jnp.int32, (rank, rank), 1)
    identity = jnp.where(row_at == column_at, 1.0, 0.0)
    both = jnp.concatenate([gram, identity], axis=1)
    place = lax.broadcasted_iota(jnp.int32, (rank, 1), 0)
    for step in range(rank - 1):
        row = both[step:step + 1, :]
        column = both[:, step:step + 1]
        factor = jnp.where(place > step, column, 0.0) / both[step:step + 1, step:step + 1]
        both = both - factor * row
    pivots = jnp.sum(jnp.where(row_at == column_at, both[:, :rank], 0.0), axis=1, keepdims=True)
    return both[:, rank:] / jnp.sqrt(pivots)


def factor_kernel(scale, grams_ref, rows_ref, basis_ref, inverse_ref):
    rank = rows_ref.shape[0]
    gram = tree_sum([grams_ref[at] for at in range(grams_ref.shape[0])])
    inverse = lower_inverse(gram[:, :rank])
    inverse_ref[...] = inverse
    left = jnp.concatenate(thirds(inverse * scale), axis=0)
    chunk = min(CHUNK, rows_ref.shape[1])
    for at in range(rows_ref.shape[1] // chunk):
        span = pl.ds(at * chunk, chunk)
        basis_ref[:, span] = product(left, thirds(rows_ref[:, span]), 0)


def factor(grams, rows, scale):
    rank, cells = rows.shape
    return pl.pallas_call(
        lambda *refs: factor_kernel(scale, *refs),
        in_specs=[VMEM] * 2,
        out_specs=[VMEM] * 2,
        out_shape=[
            jax.ShapeDtypeStruct((rank, cells), jnp.float32),
            jax.ShapeDtypeStruct((rank, rank), jnp.float32),
        ],
        compiler_params=limit(16),
        name="factor",
    )(grams, rows)


def finish_kernel(inverse_ref, *refs):
    left = jnp.concatenate(thirds(inverse_ref[...]), axis=0)
    refs[-1][...] = product(left, thirds(tree_sum([ref[...] for ref in refs[:-1]])), 0)


def finish(inverse, parts):
    return pl.pallas_call(
        finish_kernel,
        in_specs=[VMEM] * (len(parts) + 1),
        out_specs=VMEM,
        out_shape=jax.ShapeDtypeStruct(parts[0].shape, jnp.float32),
        compiler_params=limit(16),
        name="finish",
    )(inverse, *parts)


def exchange(block, axis):
    count = lax.axis_size(axis)
    parts = [block]
    step = 1
    while step < count:
        block = tree_sum(parts)
        parts = [block, swap(block, axis, step)]
        step *= 2
    return parts


def shards(snapshots, sketch):
    total_cells = snapshots.shape[0] * lax.axis_size("cells")
    partial_rows, held = sketch_rows(snapshots, sketch)
    rows, gram, sums = project(exchange(partial_rows, "snaps"), held)
    grams = lax.all_gather(gram, "cells")
    sums = exchange(sums, "cells")
    basis, inverse = factor(grams, rows, math.sqrt(total_cells))
    return (basis, finish(inverse, sums))


def solution(mesh):
    return jax.shard_map(
        shards,
        mesh=mesh,
        in_specs=(P("cells", "snaps"), P("snaps", None)),
        out_specs=(P(None, "cells"), P(None, "snaps")),
        check_vma=False,
    )
```

```python
import math

import jax
import jax.numpy as jnp
from jax import lax
from jax.experimental import pallas as pl
from jax.experimental.pallas import tpu as pltpu
from jax.sharding import PartitionSpec as P

LANES = 128
CHUNK = 512
MIB = 1 << 20
VMEM = pl.BlockSpec(memory_space=pltpu.VMEM)
HBM = pl.BlockSpec(memory_space=pltpu.HBM)


def limit(mebibytes):
    return pltpu.CompilerParams(vmem_limit_bytes=mebibytes * MIB)


def in_hbm(block):
    return pltpu.with_memory_space_constraint(block, pltpu.HBM)


def swap(block, axis, offset):
    count = lax.axis_size(axis)
    return lax.ppermute(block, axis, [(at, at ^ offset) for at in range(count)])


def tree_sum(parts):
    while len(parts) > 1:
        parts = [parts[at] + parts[at + 1] for at in range(0, len(parts), 2)]
    return parts[0]


def thirds(block):
    high = block.astype(jnp.bfloat16)
    rest = block - high.astype(jnp.float32)
    middle = rest.astype(jnp.bfloat16)
    low = (rest - middle.astype(jnp.float32)).astype(jnp.bfloat16)
    return high, middle, low


def product(left, right, right_dim):
    rank = left.shape[0] // 3
    dims = (((1,), (right_dim,)), ((), ()))
    high, middle, low = [
        lax.dot_general(left[:rank * (3 - at)], part, dims, preferred_element_type=jnp.float32)
        for at, part in enumerate(right)
    ]
    small = high[2 * rank:] + (middle[rank:] + low)
    return high[:rank] + ((high[rank:2 * rank] + middle[:rank]) + small)


def sketch_kernel(sketch_ref, snapshots_ref, out_ref, held, sketch_held, arrived):
    chunk = min(CHUNK, held.shape[0])
    chunks = held.shape[0] // chunk
    first = pltpu.make_async_copy(sketch_ref, sketch_held, arrived.at[chunks])
    first.start()
    copies = []
    for at in range(chunks):
        rows = pl.ds(at * chunk, chunk)
        copies.append(pltpu.make_async_copy(snapshots_ref.at[rows], held.at[rows], arrived.at[at]))
        copies[-1].start()
    first.wait()
    sketch = jnp.concatenate(thirds(sketch_held[...]), axis=0)
    for at, copy in enumerate(copies):
        rows = pl.ds(at * chunk, chunk)
        copy.wait()
        out_ref[:, rows] = product(sketch, thirds(held[rows, :]), 1)


def sketch_rows(snapshots, sketch):
    cells, snaps = snapshots.shape
    rank = sketch.shape[1]
    return pl.pallas_call(
        sketch_kernel,
        in_specs=[HBM] * 2,
        out_specs=[VMEM] * 2,
        out_shape=[
            pltpu.VMEM((rank, cells), jnp.float32),
            pltpu.VMEM((cells, snaps), jnp.float32),
        ],
        scratch_shapes=[
            pltpu.VMEM((rank, snaps), jnp.float32),
            pltpu.SemaphoreType.DMA((-(-cells // CHUNK) + 1,)),
        ],
        compiler_params=limit(16),
        name="sketch_rows",
    )(in_hbm(sketch.T), in_hbm(snapshots))


def project_kernel(parts, *refs):
    snapshots_ref = refs[parts]
    rows_ref, both_ref, sums_ref = refs[parts + 1:]
    rank, cells = rows_ref.shape
    snaps = sums_ref.shape[1]
    chunk = min(CHUNK, cells)
    sums = jnp.zeros(sums_ref.shape, jnp.float32)
    gram = jnp.zeros((rank, rank), jnp.float32)
    for at in range(cells // chunk):
        span = pl.ds(at * chunk, chunk)
        rows = tree_sum([ref[:, span] for ref in refs[:parts]])
        rows_ref[:, span] = rows
        split = thirds(rows)
        left = jnp.concatenate(split, axis=0)
        sums += product(left, thirds(snapshots_ref[span, :]), 0)
        gram += product(left, split, 1)
    sums_ref[...] = sums
    both_ref[:, :snaps] = sums
    both_ref[:, snaps:] = jnp.zeros((rank, both_ref.shape[1] - snaps), jnp.float32)
    both_ref[:, snaps:snaps + rank] = gram


def project(parts, snapshots):
    cells, snaps = snapshots.shape
    rank = parts[0].shape[0]
    return pl.pallas_call(
        lambda *refs: project_kernel(len(parts), *refs),
        in_specs=[VMEM] * (len(parts) + 1),
        out_specs=[VMEM] * 3,
        out_shape=[
            pltpu.VMEM((rank, cells), jnp.float32),
            pltpu.VMEM((rank, snaps + -(-rank // LANES) * LANES), jnp.float32),
            pltpu.VMEM((rank, snaps), jnp.float32),
        ],
        compiler_params=limit(16),
        name="project",
    )(*parts, snapshots)


def lower_inverse(gram):
    rank = gram.shape[0]
    row_at = lax.broadcasted_iota(jnp.int32, (rank, rank), 0)
    column_at = lax.broadcasted_iota(jnp.int32, (rank, rank), 1)
    identity = jnp.where(row_at == column_at, 1.0, 0.0)
    both = jnp.concatenate([gram, identity], axis=1)
    place = lax.broadcasted_iota(jnp.int32, (rank, 1), 0)
    for step in range(rank - 1):
        row = both[step:step + 1, :]
        column = both[:, step:step + 1]
        factor = jnp.where(place > step, column, 0.0) / both[step:step + 1, step:step + 1]
        both = both - factor * row
    pivots = jnp.sum(jnp.where(row_at == column_at, both[:, :rank], 0.0), axis=1, keepdims=True)
    return both[:, rank:] / jnp.sqrt(pivots)


def leads():
    return lax.axis_index("snaps") % 2 == 1


def factor_kernel(scale, own_ref, given_ref, rows_ref, basis_ref, inverse_ref):
    rank = rows_ref.shape[0]
    gram = jnp.where(leads(), own_ref[:, :rank], given_ref[:, :rank])
    inverse = lower_inverse(gram)
    inverse_ref[...] = inverse
    left = jnp.concatenate(thirds(inverse * scale), axis=0)
    chunk = min(CHUNK, rows_ref.shape[1])
    for at in range(rows_ref.shape[1] // chunk):
        span = pl.ds(at * chunk, chunk)
        basis_ref[:, span] = product(left, thirds(rows_ref[:, span]), 0)


def factor(own, given, rows, scale):
    rank, cells = rows.shape
    return pl.pallas_call(
        lambda *refs: factor_kernel(scale, *refs),
        in_specs=[VMEM] * 3,
        out_specs=[VMEM] * 2,
        out_shape=[
            jax.ShapeDtypeStruct((rank, cells), jnp.float32),
            pltpu.VMEM((rank, rank), jnp.float32),
        ],
        compiler_params=limit(16),
        cost_estimate=pl.CostEstimate(flops=12 * rank * rank * cells, bytes_accessed=8 * rank * cells, transcendentals=0),
        name="factor",
    )(own, given, rows)


def finish_kernel(inverse_ref, both_ref, sums_ref, last_ref, out_ref):
    snaps = sums_ref.shape[1]
    left = jnp.concatenate(thirds(inverse_ref[...]), axis=0)
    out_ref[...] = product(left, thirds(jnp.where(leads(), both_ref[:, :snaps], sums_ref[...] + last_ref[...])), 0)


def finish(inverse, both, sums, last):
    return pl.pallas_call(
        finish_kernel,
        in_specs=[VMEM] * 4,
        out_specs=VMEM,
        out_shape=jax.ShapeDtypeStruct(sums.shape, jnp.float32),
        compiler_params=limit(16),
        name="finish",
    )(inverse, both, sums, last)


def exchange(block, axis):
    count = lax.axis_size(axis)
    parts = [block]
    step = 1
    while step < count:
        block = tree_sum(parts)
        parts = [block, swap(block, axis, step)]
        step *= 2
    return parts


def shards(snapshots, sketch):
    cells = lax.axis_size("cells")
    snaps = lax.axis_size("snaps")
    columns = snapshots.shape[1]
    axes = ("cells", "snaps")
    partial_rows, held = sketch_rows(snapshots, sketch)
    rows, both, sums = project(exchange(partial_rows, "snaps"), held)
    step = 1
    last = jnp.zeros_like(sums)
    while step < cells:
        odd = [(at * snaps + lane, (at ^ step) * snaps + lane) for at in range(cells) for lane in range(1, snaps, 2)]
        even = [(at * snaps + lane, (at ^ step) * snaps + lane) for at in range(cells) for lane in range(0, snaps, 2)]
        both = both + lax.ppermute(both, axes, odd)
        sums = sums + last if step > 1 else sums
        last = lax.ppermute(sums, axes, even)
        step *= 2
    own = both[:, columns:]
    given = lax.ppermute(own, "snaps", [(lane, lane - 1) for lane in range(1, snaps, 2)])
    basis, inverse = factor(own, given, rows, math.sqrt(snapshots.shape[0] * cells))
    return (basis, finish(inverse, both, sums, last))


def solution(mesh):
    return jax.shard_map(
        shards,
        mesh=mesh,
        in_specs=(P("cells", "snaps"), P("snaps", None)),
        out_specs=(P(None, "cells"), P(None, "snaps")),
        check_vma=False,
    )
```

```python
import math

import jax
import jax.numpy as jnp
from jax import lax
from jax.experimental import pallas as pl
from jax.experimental.pallas import tpu as pltpu
from jax.sharding import PartitionSpec as P

LANES = 128
CHUNK = 512
MIB = 1 << 20
VMEM = pl.BlockSpec(memory_space=pltpu.VMEM)
HBM = pl.BlockSpec(memory_space=pltpu.HBM)


def limit(mebibytes):
    return pltpu.CompilerParams(vmem_limit_bytes=mebibytes * MIB)


def in_hbm(block):
    return pltpu.with_memory_space_constraint(block, pltpu.HBM)


def swap(block, axis, offset):
    count = lax.axis_size(axis)
    return lax.ppermute(block, axis, [(at, at ^ offset) for at in range(count)])


def tree_sum(parts):
    while len(parts) > 1:
        parts = [parts[at] + parts[at + 1] for at in range(0, len(parts), 2)]
    return parts[0]


def thirds(block):
    high = block.astype(jnp.bfloat16)
    rest = block - high.astype(jnp.float32)
    middle = rest.astype(jnp.bfloat16)
    low = (rest - middle.astype(jnp.float32)).astype(jnp.bfloat16)
    return high, middle, low


def product(left, right, right_dim):
    rank = left.shape[0] // 3
    dims = (((1,), (right_dim,)), ((), ()))
    high, middle, low = [
        lax.dot_general(left[:rank * (3 - at)], part, dims, preferred_element_type=jnp.float32)
        for at, part in enumerate(right)
    ]
    small = high[2 * rank:] + (middle[rank:] + low)
    return high[:rank] + ((high[rank:2 * rank] + middle[:rank]) + small)


def sketch_kernel(sketch_ref, snapshots_ref, out_ref, held, sketch_held, arrived):
    rank = out_ref.shape[0]
    chunk = min(CHUNK, held.shape[0])
    chunks = held.shape[0] // chunk
    first = pltpu.make_async_copy(sketch_ref, sketch_held, arrived.at[chunks])
    first.start()
    copies = []
    for at in range(chunks):
        rows = pl.ds(at * chunk, chunk)
        copies.append(pltpu.make_async_copy(snapshots_ref.at[rows], held.at[rows], arrived.at[at]))
        copies[-1].start()
    first.wait()
    high, middle, low = [part.astype(jnp.float32) for part in thirds(sketch_held[...])]
    zero = jnp.zeros_like(high)
    pad = jnp.zeros((-3 * rank % LANES, high.shape[1]), jnp.float32)
    stack = [(high, middle, low), (high, middle, zero), (high, zero, zero)]
    right = jnp.concatenate(
        [jnp.concatenate([*parts, pad], axis=0).T.astype(jnp.bfloat16) for parts in stack], axis=0
    )
    for at, copy in enumerate(copies):
        rows = pl.ds(at * chunk, chunk)
        copy.wait()
        left = jnp.concatenate(thirds(held[rows, :]), axis=1)
        out = jnp.dot(left, right, preferred_element_type=jnp.float32).T
        out_ref[:, rows] = out[:rank] + (out[rank:2 * rank] + out[2 * rank:3 * rank])


def sketch_rows(snapshots, sketch):
    cells, snaps = snapshots.shape
    rank = sketch.shape[1]
    return pl.pallas_call(
        sketch_kernel,
        in_specs=[HBM] * 2,
        out_specs=[VMEM] * 2,
        out_shape=[
            pltpu.VMEM((rank, cells), jnp.float32),
            pltpu.VMEM((cells, snaps), jnp.float32),
        ],
        scratch_shapes=[
            pltpu.VMEM((rank, snaps), jnp.float32),
            pltpu.SemaphoreType.DMA((-(-cells // CHUNK) + 1,)),
        ],
        compiler_params=limit(16),
        name="sketch_rows",
    )(in_hbm(sketch.T), in_hbm(snapshots))


def project_kernel(parts, *refs):
    snapshots_ref = refs[parts]
    rows_ref, block_ref = refs[parts + 1:]
    rank, cells = rows_ref.shape
    snaps = snapshots_ref.shape[1]
    chunk = min(CHUNK, cells)
    sums = jnp.zeros((rank, snaps), jnp.float32)
    gram = jnp.zeros((rank, rank), jnp.float32)
    for at in range(cells // chunk):
        span = pl.ds(at * chunk, chunk)
        rows = tree_sum([ref[:, span] for ref in refs[:parts]])
        rows_ref[:, span] = rows
        split = thirds(rows)
        left = jnp.concatenate(split, axis=0)
        sums += product(left, thirds(snapshots_ref[span, :]), 0)
        gram += product(left, split, 1)
    second = lax.axis_index("snaps") % 2 == 1
    block_ref[:, :snaps] = jnp.where(second, 0.0, sums)
    block_ref[:, snaps:2 * snaps] = jnp.where(second, sums, 0.0)
    block_ref[:, 2 * snaps:] = jnp.zeros((rank, block_ref.shape[1] - 2 * snaps), jnp.float32)
    block_ref[:, 2 * snaps:2 * snaps + rank] = gram


def project(parts, snapshots):
    cells, snaps = snapshots.shape
    rank = parts[0].shape[0]
    return pl.pallas_call(
        lambda *refs: project_kernel(len(parts), *refs),
        in_specs=[VMEM] * (len(parts) + 1),
        out_specs=[VMEM] * 2,
        out_shape=[
            pltpu.VMEM((rank, cells), jnp.float32),
            pltpu.VMEM((rank, 2 * snaps + -(-rank // LANES) * LANES), jnp.float32),
        ],
        compiler_params=limit(16),
        name="project",
    )(*parts, snapshots)


def spread(row):
    return jnp.broadcast_to(row, (8, row.shape[1]))


def tall(tile, rank):
    return jnp.concatenate([tile] * (rank // 8), axis=0)


def lower_inverse(gram):
    rank, lanes = gram.shape
    block = math.gcd(rank, 4)
    row_at = lax.broadcasted_iota(jnp.int32, (rank, lanes), 0)
    lane_at = lax.broadcasted_iota(jnp.int32, (rank, lanes), 1)
    both = jnp.where(lane_at < rank, gram, jnp.where(lane_at == row_at + rank, 1.0, 0.0))
    pivots = jnp.ones((rank, lanes), jnp.float32)
    for base in range(0, rank, block):
        columns = [jnp.broadcast_to(both[:, base + at:base + at + 1], (rank, lanes)) for at in range(block)]
        corner = [[spread(columns[at][base + to:base + to + 1]) for at in range(block)] for to in range(block)]
        rows = [spread(both[base + at:base + at + 1]) for at in range(block)]
        eliminated = both
        for at in range(block):
            pivot = corner[at][at]
            inverse = 1.0 / pivot
            for to in range(at + 1, block):
                ratio = corner[to][at] * inverse
                rows[to] = rows[to] - ratio * rows[at]
                columns[to] = columns[to] - tall(ratio, rank) * columns[at]
                for along in range(at + 1, block):
                    corner[to][along] = corner[to][along] - ratio * corner[at][along]
            factor = jnp.where(row_at > base + at, columns[at] * tall(inverse, rank), 0.0)
            eliminated = eliminated - factor * tall(rows[at], rank)
            pivots = jnp.where(row_at == base + at, tall(pivot, rank), pivots)
        both = eliminated
    return (both / jnp.sqrt(pivots))[:, rank:2 * rank]


def factor_kernel(scale, block_ref, rows_ref, basis_ref, inverse_ref):
    inverse = lower_inverse(block_ref[:, block_ref.shape[1] - LANES:])
    inverse_ref[...] = inverse
    left = jnp.concatenate(thirds(inverse * scale), axis=0)
    chunk = min(CHUNK, rows_ref.shape[1])
    for at in range(rows_ref.shape[1] // chunk):
        span = pl.ds(at * chunk, chunk)
        basis_ref[:, span] = product(left, thirds(rows_ref[:, span]), 0)


def factor(block, rows, scale):
    rank, cells = rows.shape
    return pl.pallas_call(
        lambda *refs: factor_kernel(scale, *refs),
        in_specs=[VMEM] * 2,
        out_specs=[VMEM] * 2,
        out_shape=[
            jax.ShapeDtypeStruct((rank, cells), jnp.float32),
            pltpu.VMEM((rank, rank), jnp.float32),
        ],
        compiler_params=limit(16),
        cost_estimate=pl.CostEstimate(flops=12 * rank * rank * cells, bytes_accessed=8 * rank * cells, transcendentals=0),
        name="factor",
    )(block, rows)


def finish_kernel(inverse_ref, block_ref, given_ref, out_ref):
    snaps = out_ref.shape[1]
    total = block_ref[:, :2 * snaps] + given_ref[:, :2 * snaps]
    sums = jnp.where(lax.axis_index("snaps") % 2 == 1, total[:, snaps:], total[:, :snaps])
    left = jnp.concatenate(thirds(inverse_ref[...]), axis=0)
    out_ref[...] = product(left, thirds(sums), 0)


def finish(inverse, block, given, snaps):
    return pl.pallas_call(
        finish_kernel,
        in_specs=[VMEM] * 3,
        out_specs=VMEM,
        out_shape=jax.ShapeDtypeStruct((inverse.shape[0], snaps), jnp.float32),
        compiler_params=limit(16),
        name="finish",
    )(inverse, block, given)


def exchange(block, axis):
    count = lax.axis_size(axis)
    parts = [block]
    step = 1
    while step < count:
        block = tree_sum(parts)
        parts = [block, swap(block, axis, step)]
        step *= 2
    return parts


def shards(snapshots, sketch):
    cells = lax.axis_size("cells")
    snaps = lax.axis_size("snaps")
    partial_rows, held = sketch_rows(snapshots, sketch)
    rows, block = project(exchange(partial_rows, "snaps"), held)
    step = 1
    while step < cells:
        route = [(at * snaps + lane, (at ^ step) * snaps + (lane ^ 1)) for at in range(cells) for lane in range(snaps)]
        block = block + lax.ppermute(block, ("cells", "snaps"), route)
        step *= 2
    given = swap(block, "snaps", 1)
    basis, inverse = factor(block, rows, math.sqrt(snapshots.shape[0] * cells))
    return (basis, finish(inverse, block, given, snapshots.shape[1]))


def solution(mesh):
    return jax.shard_map(
        shards,
        mesh=mesh,
        in_specs=(P("cells", "snaps"), P("snaps", None)),
        out_specs=(P(None, "cells"), P(None, "snaps")),
        check_vma=False,
    )
```

```python
import math

import jax
import jax.numpy as jnp
from jax import lax
from jax.experimental import pallas as pl
from jax.experimental.pallas import tpu as pltpu
from jax.sharding import PartitionSpec as P

LANES = 128
CHUNK = 512
MIB = 1 << 20
VMEM = pl.BlockSpec(memory_space=pltpu.VMEM)
HBM = pl.BlockSpec(memory_space=pltpu.HBM)


def limit(mebibytes):
    return pltpu.CompilerParams(vmem_limit_bytes=mebibytes * MIB)


def in_hbm(block):
    return pltpu.with_memory_space_constraint(block, pltpu.HBM)


def swap(block, axis, offset):
    count = lax.axis_size(axis)
    return lax.ppermute(block, axis, [(at, at ^ offset) for at in range(count)])


def tree_sum(parts):
    while len(parts) > 1:
        parts = [parts[at] + parts[at + 1] for at in range(0, len(parts), 2)]
    return parts[0]


def thirds(block):
    high = block.astype(jnp.bfloat16)
    rest = block - high.astype(jnp.float32)
    middle = rest.astype(jnp.bfloat16)
    low = (rest - middle.astype(jnp.float32)).astype(jnp.bfloat16)
    return high, middle, low


def product(left, right, right_dim):
    rank = left.shape[0] // 3
    dims = (((1,), (right_dim,)), ((), ()))
    high, middle, low = [
        lax.dot_general(left[:rank * (3 - at)], part, dims, preferred_element_type=jnp.float32)
        for at, part in enumerate(right)
    ]
    small = high[2 * rank:] + (middle[rank:] + low)
    return high[:rank] + ((high[rank:2 * rank] + middle[:rank]) + small)


def pieces(cells):
    if cells % 4:
        return [(0, cells)]
    return [(0, cells // 4), (cells // 4, cells // 4), (cells // 2, cells // 2)]


def sketch_kernel(sketch_ref, snapshots_ref, out_ref, held, sketch_held, arrived):
    fetches = pieces(held.shape[0])
    first = pltpu.make_async_copy(sketch_ref, sketch_held, arrived.at[len(fetches)])
    first.start()
    copies = []
    for at, (start, size) in enumerate(fetches):
        rows = pl.ds(start, size)
        copies.append(pltpu.make_async_copy(snapshots_ref.at[rows], held.at[rows], arrived.at[at]))
        copies[-1].start()
    first.wait()
    sketch = jnp.concatenate(thirds(sketch_held[...]), axis=0)
    for copy, (start, size) in zip(copies, fetches):
        copy.wait()
        chunk = min(CHUNK, size)
        for at in range(start, start + size, chunk):
            rows = pl.ds(at, chunk)
            out_ref[:, rows] = product(sketch, thirds(held[rows, :]), 1)


def sketch_rows(snapshots, sketch):
    cells, snaps = snapshots.shape
    rank = sketch.shape[1]
    return pl.pallas_call(
        sketch_kernel,
        in_specs=[HBM] * 2,
        out_specs=[VMEM] * 2,
        out_shape=[
            pltpu.VMEM((rank, cells), jnp.float32),
            pltpu.VMEM((cells, snaps), jnp.float32),
        ],
        scratch_shapes=[
            pltpu.VMEM((rank, snaps), jnp.float32),
            pltpu.SemaphoreType.DMA((len(pieces(cells)) + 1,)),
        ],
        compiler_params=limit(16),
        name="sketch_rows",
    )(in_hbm(sketch.T), in_hbm(snapshots))


def project_kernel(parts, *refs):
    snapshots_ref = refs[parts]
    rows_ref, block_ref = refs[parts + 1:]
    rank, cells = rows_ref.shape
    snaps = snapshots_ref.shape[1]
    chunk = min(CHUNK, cells)
    sums = jnp.zeros((rank, snaps), jnp.float32)
    gram = jnp.zeros((rank, rank), jnp.float32)
    for at in range(cells // chunk):
        span = pl.ds(at * chunk, chunk)
        rows = tree_sum([ref[:, span] for ref in refs[:parts]])
        rows_ref[:, span] = rows
        split = thirds(rows)
        left = jnp.concatenate(split, axis=0)
        sums += product(left, thirds(snapshots_ref[span, :]), 0)
        gram += product(left, split, 1)
    block_ref[:, :snaps] = sums
    block_ref[:, snaps:] = jnp.zeros((rank, block_ref.shape[1] - snaps), jnp.float32)
    block_ref[:, snaps:snaps + rank] = gram


def project(parts, snapshots):
    cells, snaps = snapshots.shape
    rank = parts[0].shape[0]
    return pl.pallas_call(
        lambda *refs: project_kernel(len(parts), *refs),
        in_specs=[VMEM] * (len(parts) + 1),
        out_specs=[VMEM] * 2,
        out_shape=[
            pltpu.VMEM((rank, cells), jnp.float32),
            pltpu.VMEM((rank, snaps + -(-rank // LANES) * LANES), jnp.float32),
        ],
        compiler_params=limit(16),
        name="project",
    )(*parts, snapshots)


def spread(row):
    return jnp.broadcast_to(row, (8, row.shape[1]))


def tall(tile, rank):
    return jnp.concatenate([tile] * (rank // 8), axis=0)


def lower_inverse(gram):
    rank, lanes = gram.shape
    block = math.gcd(rank, 4)
    row_at = lax.broadcasted_iota(jnp.int32, (rank, lanes), 0)
    lane_at = lax.broadcasted_iota(jnp.int32, (rank, lanes), 1)
    both = jnp.where(lane_at < rank, gram, jnp.where(lane_at == row_at + rank, 1.0, 0.0))
    pivots = jnp.ones((rank, lanes), jnp.float32)
    for base in range(0, rank, block):
        columns = [jnp.broadcast_to(both[:, base + at:base + at + 1], (rank, lanes)) for at in range(block)]
        corner = [[spread(columns[at][base + to:base + to + 1]) for at in range(block)] for to in range(block)]
        rows = [spread(both[base + at:base + at + 1]) for at in range(block)]
        eliminated = both
        for at in range(block):
            pivot = corner[at][at]
            inverse = 1.0 / pivot
            for to in range(at + 1, block):
                ratio = corner[to][at] * inverse
                rows[to] = rows[to] - ratio * rows[at]
                columns[to] = columns[to] - tall(ratio, rank) * columns[at]
                for along in range(at + 1, block):
                    corner[to][along] = corner[to][along] - ratio * corner[at][along]
            factor = jnp.where(row_at > base + at, columns[at] * tall(inverse, rank), 0.0)
            eliminated = eliminated - factor * tall(rows[at], rank)
            pivots = jnp.where(row_at == base + at, tall(pivot, rank), pivots)
        both = eliminated
    return (both / jnp.sqrt(pivots))[:, rank:2 * rank]


def factor_kernel(scale, parts, *refs):
    rows_ref, basis_ref, coefficients_ref = refs[parts:]
    snaps = coefficients_ref.shape[1]
    block = tree_sum([ref[...] for ref in refs[:parts]])
    inverse = lower_inverse(block[:, snaps:])
    left = jnp.concatenate(thirds(inverse), axis=0)
    coefficients_ref[...] = product(left, thirds(block[:, :snaps]), 0)
    left = jnp.concatenate(thirds(inverse * scale), axis=0)
    chunk = min(CHUNK, rows_ref.shape[1])
    for at in range(0, rows_ref.shape[1], chunk):
        span = pl.ds(at, chunk)
        basis_ref[:, span] = product(left, thirds(rows_ref[:, span]), 0)


def factor(parts, rows, scale, snaps):
    rank, cells = rows.shape
    return pl.pallas_call(
        lambda *refs: factor_kernel(scale, len(parts), *refs),
        in_specs=[VMEM] * (len(parts) + 1),
        out_specs=[VMEM] * 2,
        out_shape=[
            jax.ShapeDtypeStruct((rank, cells), jnp.float32),
            jax.ShapeDtypeStruct((rank, snaps), jnp.float32),
        ],
        compiler_params=limit(16),
        name="factor",
    )(*parts, rows)


def exchange(block, axis):
    count = lax.axis_size(axis)
    parts = [block]
    step = 1
    while step < count:
        block = tree_sum(parts)
        parts = [block, swap(block, axis, step)]
        step *= 2
    return parts


def shards(snapshots, sketch):
    total_cells = snapshots.shape[0] * lax.axis_size("cells")
    partial_rows, held = sketch_rows(snapshots, sketch)
    rows, block = project(exchange(partial_rows, "snaps"), held)
    return factor(exchange(block, "cells"), rows, math.sqrt(total_cells), snapshots.shape[1])


def solution(mesh):
    return jax.shard_map(
        shards,
        mesh=mesh,
        in_specs=(P("cells", "snaps"), P("snaps", None)),
        out_specs=(P(None, "cells"), P(None, "snaps")),
        check_vma=False,
    )
```

```python
import math

import jax
import jax.numpy as jnp
from jax import lax
from jax.experimental import pallas as pl
from jax.experimental.pallas import tpu as pltpu
from jax.sharding import PartitionSpec as P

LANES = 128
CHUNK = 512
MIB = 1 << 20
VMEM = pl.BlockSpec(memory_space=pltpu.VMEM)
HBM = pl.BlockSpec(memory_space=pltpu.HBM)


def limit(mebibytes):
    return pltpu.CompilerParams(vmem_limit_bytes=mebibytes * MIB)


def in_hbm(block):
    return pltpu.with_memory_space_constraint(block, pltpu.HBM)


def swap(block, axis, offset):
    count = lax.axis_size(axis)
    return lax.ppermute(block, axis, [(at, at ^ offset) for at in range(count)])


def tree_sum(parts):
    while len(parts) > 1:
        parts = [parts[at] + parts[at + 1] for at in range(0, len(parts), 2)]
    return parts[0]


def thirds(block):
    high = block.astype(jnp.bfloat16)
    rest = block - high.astype(jnp.float32)
    middle = rest.astype(jnp.bfloat16)
    low = (rest - middle.astype(jnp.float32)).astype(jnp.bfloat16)
    return high, middle, low


def product(left, right, right_dim):
    rank = left.shape[0] // 3
    dims = (((1,), (right_dim,)), ((), ()))
    high, middle, low = [
        lax.dot_general(left[:rank * (3 - at)], part, dims, preferred_element_type=jnp.float32)
        for at, part in enumerate(right)
    ]
    small = high[2 * rank:] + (middle[rank:] + low)
    return high[:rank] + ((high[rank:2 * rank] + middle[:rank]) + small)


def pieces(cells):
    size = cells // 16 if cells % 16 == 0 else cells
    spans = [(start, size) for start in range(0, cells, size)]
    quarter = -(-len(spans) // 4)
    groups = [spans[:quarter], spans[quarter:2 * quarter], spans[2 * quarter:]]
    return [group for group in groups if group]


def sketch_kernel(sketch_ref, snapshots_ref, out_ref, held, sketch_held, arrived):
    groups = pieces(held.shape[0])
    first = pltpu.make_async_copy(sketch_ref, sketch_held, arrived.at[sum(map(len, groups))])
    first.start()
    copies = []
    for group in groups:
        copies.append([])
        for start, size in group:
            rows = pl.ds(start, size)
            at = sum(map(len, copies))
            copies[-1].append(pltpu.make_async_copy(snapshots_ref.at[rows], held.at[rows], arrived.at[at]))
            copies[-1][-1].start()
    first.wait()
    sketch = jnp.concatenate(thirds(sketch_held[...]), axis=0)
    for waits, group in zip(copies, groups):
        for copy in waits:
            copy.wait()
        start, end = group[0][0], sum(group[-1])
        chunk = math.gcd(CHUNK, end - start)
        for at in range(start, end, chunk):
            rows = pl.ds(at, chunk)
            out_ref[:, rows] = product(sketch, thirds(held[rows, :]), 1)


def sketch_rows(snapshots, sketch):
    cells, snaps = snapshots.shape
    rank = sketch.shape[1]
    return pl.pallas_call(
        sketch_kernel,
        in_specs=[HBM] * 2,
        out_specs=[VMEM] * 2,
        out_shape=[
            pltpu.VMEM((rank, cells), jnp.float32),
            pltpu.VMEM((cells, snaps), jnp.float32),
        ],
        scratch_shapes=[
            pltpu.VMEM((rank, snaps), jnp.float32),
            pltpu.SemaphoreType.DMA((sum(map(len, pieces(cells))) + 1,)),
        ],
        compiler_params=limit(16),
        name="sketch_rows",
    )(in_hbm(sketch.T), in_hbm(snapshots))


def project_kernel(parts, *refs):
    snapshots_ref = refs[parts]
    rows_ref, block_ref = refs[parts + 1:]
    rank, cells = rows_ref.shape
    snaps = snapshots_ref.shape[1]
    chunk = min(CHUNK, cells)
    sums = jnp.zeros((rank, snaps), jnp.float32)
    gram = jnp.zeros((rank, rank), jnp.float32)
    for at in range(cells // chunk):
        span = pl.ds(at * chunk, chunk)
        rows = tree_sum([ref[:, span] for ref in refs[:parts]])
        rows_ref[:, span] = rows
        split = thirds(rows)
        left = jnp.concatenate(split, axis=0)
        sums += product(left, thirds(snapshots_ref[span, :]), 0)
        gram += product(left, split, 1)
    tiles = snaps // LANES
    for at in range(tiles):
        block_ref[at * rank:(at + 1) * rank, :] = sums[:, at * LANES:(at + 1) * LANES]
    high = rank * rank // LANES
    block_ref[tiles * rank:, :] = jnp.concatenate([gram[at:at + high] for at in range(0, rank, high)], axis=1)


def project(parts, snapshots):
    cells, snaps = snapshots.shape
    rank = parts[0].shape[0]
    return pl.pallas_call(
        lambda *refs: project_kernel(len(parts), *refs),
        in_specs=[VMEM] * (len(parts) + 1),
        out_specs=[VMEM] * 2,
        out_shape=[
            pltpu.VMEM((rank, cells), jnp.float32),
            pltpu.VMEM((rank * (snaps + rank) // LANES, LANES), jnp.float32),
        ],
        compiler_params=limit(16),
        name="project",
    )(*parts, snapshots)


def spread(row):
    return jnp.broadcast_to(row, (8, row.shape[1]))


def tall(tile, rank):
    return jnp.concatenate([tile] * (rank // 8), axis=0)


def lower_inverse(gram):
    rank, lanes = gram.shape
    block = math.gcd(rank, 4)
    row_at = lax.broadcasted_iota(jnp.int32, (rank, lanes), 0)
    lane_at = lax.broadcasted_iota(jnp.int32, (rank, lanes), 1)
    both = jnp.where(lane_at < rank, gram, jnp.where(lane_at == row_at + rank, 1.0, 0.0))
    pivots = jnp.ones((rank, lanes), jnp.float32)
    for base in range(0, rank, block):
        columns = [jnp.broadcast_to(both[:, base + at:base + at + 1], (rank, lanes)) for at in range(block)]
        corner = [[spread(columns[at][base + to:base + to + 1]) for at in range(block)] for to in range(block)]
        rows = [spread(both[base + at:base + at + 1]) for at in range(block)]
        eliminated = both
        for at in range(block):
            pivot = corner[at][at]
            inverse = 1.0 / pivot
            for to in range(at + 1, block):
                ratio = corner[to][at] * inverse
                rows[to] = rows[to] - ratio * rows[at]
                columns[to] = columns[to] - tall(ratio, rank) * columns[at]
                for along in range(at + 1, block):
                    corner[to][along] = corner[to][along] - ratio * corner[at][along]
            factor = jnp.where(row_at > base + at, columns[at] * tall(inverse, rank), 0.0)
            eliminated = eliminated - factor * tall(rows[at], rank)
            pivots = jnp.where(row_at == base + at, tall(pivot, rank), pivots)
        both = eliminated
    return (both / jnp.sqrt(pivots))[:, rank:2 * rank]


def factor_kernel(scale, parts, *refs):
    rows_ref, basis_ref, coefficients_ref = refs[parts:]
    snaps = coefficients_ref.shape[1]
    block = tree_sum([ref[...] for ref in refs[:parts]])
    rank = rows_ref.shape[0]
    tiles = snaps // LANES
    packed = block[tiles * rank:]
    turns = [packed] + [pltpu.roll(packed, LANES - at, 1) for at in range(rank, LANES, rank)]
    inverse = lower_inverse(jnp.concatenate(turns, axis=0))
    left = jnp.concatenate(thirds(inverse), axis=0)
    for at in range(tiles):
        part = block[at * rank:(at + 1) * rank]
        coefficients_ref[:, at * LANES:(at + 1) * LANES] = product(left, thirds(part), 0)
    left = jnp.concatenate(thirds(inverse * scale), axis=0)
    chunk = min(CHUNK, rows_ref.shape[1])
    for at in range(0, rows_ref.shape[1], chunk):
        span = pl.ds(at, chunk)
        basis_ref[:, span] = product(left, thirds(rows_ref[:, span]), 0)


def factor(parts, rows, scale, snaps):
    rank, cells = rows.shape
    return pl.pallas_call(
        lambda *refs: factor_kernel(scale, len(parts), *refs),
        in_specs=[VMEM] * (len(parts) + 1),
        out_specs=[VMEM] * 2,
        out_shape=[
            jax.ShapeDtypeStruct((rank, cells), jnp.float32),
            jax.ShapeDtypeStruct((rank, snaps), jnp.float32),
        ],
        compiler_params=limit(16),
        name="factor",
    )(*parts, rows)


def exchange(block, axis, radix):
    count = lax.axis_size(axis)
    parts = [block]
    step = 1
    while step < count:
        block = tree_sum(parts)
        group = min(radix, count // step)
        parts = [block] + [swap(block, axis, step * at) for at in range(1, group)]
        step *= group
    return parts


def shards(snapshots, sketch):
    total_cells = snapshots.shape[0] * lax.axis_size("cells")
    partial_rows, held = sketch_rows(snapshots, sketch)
    rows, block = project(exchange(partial_rows, "snaps", 2), held)
    return factor(exchange(block, "cells", 4), rows, math.sqrt(total_cells), snapshots.shape[1])


def solution(mesh):
    return jax.shard_map(
        shards,
        mesh=mesh,
        in_specs=(P("cells", "snaps"), P("snaps", None)),
        out_specs=(P(None, "cells"), P(None, "snaps")),
        check_vma=False,
    )
```

```python
import math

import jax
import jax.numpy as jnp
from jax import lax
from jax.experimental import pallas as pl
from jax.experimental.pallas import tpu as pltpu
from jax.sharding import PartitionSpec as P

LANES = 128
CHUNK = 512
MIB = 1 << 20
VMEM = pl.BlockSpec(memory_space=pltpu.VMEM)
HBM = pl.BlockSpec(memory_space=pltpu.HBM)


def limit(mebibytes):
    return pltpu.CompilerParams(vmem_limit_bytes=mebibytes * MIB)


def in_hbm(block):
    return pltpu.with_memory_space_constraint(block, pltpu.HBM)


def swap(block, axis, offset):
    count = lax.axis_size(axis)
    return lax.ppermute(block, axis, [(at, at ^ offset) for at in range(count)])


def tree_sum(parts):
    while len(parts) > 1:
        parts = [parts[at] + parts[at + 1] for at in range(0, len(parts), 2)]
    return parts[0]


def thirds(block):
    high = block.astype(jnp.bfloat16)
    rest = block - high.astype(jnp.float32)
    middle = rest.astype(jnp.bfloat16)
    low = (rest - middle.astype(jnp.float32)).astype(jnp.bfloat16)
    return high, middle, low


def product(left, right, right_dim):
    rank = left.shape[0] // 3
    dims = (((1,), (right_dim,)), ((), ()))
    high, middle, low = [
        lax.dot_general(left[:rank * (3 - at)], part, dims, preferred_element_type=jnp.float32)
        for at, part in enumerate(right)
    ]
    small = high[2 * rank:] + (middle[rank:] + low)
    return high[:rank] + ((high[rank:2 * rank] + middle[:rank]) + small)


def pieces(cells):
    size = cells // 16 if cells % 16 == 0 else cells
    spans = [(start, size) for start in range(0, cells, size)]
    quarter = -(-len(spans) // 4)
    groups = [spans[:quarter], spans[quarter:2 * quarter], spans[2 * quarter:3 * quarter], spans[3 * quarter:]]
    return [group for group in groups if group]


def sketch_kernel(sketch_ref, snapshots_ref, out_ref, held, sketch_held, arrived):
    groups = pieces(held.shape[0])
    first = pltpu.make_async_copy(sketch_ref, sketch_held, arrived.at[sum(map(len, groups))])
    first.start()
    copies = []
    for group in groups:
        copies.append([])
        for start, size in group:
            rows = pl.ds(start, size)
            at = sum(map(len, copies))
            copies[-1].append(pltpu.make_async_copy(snapshots_ref.at[rows], held.at[rows], arrived.at[at]))
            copies[-1][-1].start(priority=at % 2)
    first.wait()
    sketch = jnp.concatenate(thirds(sketch_held[...]), axis=0)
    for waits, group in zip(copies, groups):
        for copy in waits:
            copy.wait()
        start, end = group[0][0], sum(group[-1])
        chunk = math.gcd(CHUNK, end - start)
        for at in range(start, end, chunk):
            rows = pl.ds(at, chunk)
            out_ref[:, rows] = product(sketch, thirds(held[rows, :]), 1)


def sketch_rows(snapshots, sketch):
    cells, snaps = snapshots.shape
    rank = sketch.shape[1]
    return pl.pallas_call(
        sketch_kernel,
        in_specs=[HBM] * 2,
        out_specs=[VMEM] * 2,
        out_shape=[
            pltpu.VMEM((rank, cells), jnp.float32),
            pltpu.VMEM((cells, snaps), jnp.float32),
        ],
        scratch_shapes=[
            pltpu.VMEM((rank, snaps), jnp.float32),
            pltpu.SemaphoreType.DMA((sum(map(len, pieces(cells))) + 1,)),
        ],
        compiler_params=limit(16),
        name="sketch_rows",
    )(in_hbm(sketch.T), in_hbm(snapshots))


def project_kernel(parts, *refs):
    snapshots_ref = refs[parts]
    rows_ref, block_ref = refs[parts + 1:]
    rank, cells = rows_ref.shape
    snaps = snapshots_ref.shape[1]
    chunk = min(CHUNK, cells)
    sums = jnp.zeros((rank, snaps), jnp.float32)
    gram = jnp.zeros((rank, rank), jnp.float32)
    for at in range(cells // chunk):
        span = pl.ds(at * chunk, chunk)
        rows = tree_sum([ref[:, span] for ref in refs[:parts]])
        rows_ref[:, span] = rows
        split = thirds(rows)
        left = jnp.concatenate(split, axis=0)
        sums += product(left, thirds(snapshots_ref[span, :]), 0)
        gram += product(left, split, 1)
    tiles = snaps // LANES
    for at in range(tiles):
        block_ref[at * rank:(at + 1) * rank, :] = sums[:, at * LANES:(at + 1) * LANES]
    high = rank * rank // LANES
    block_ref[tiles * rank:, :] = jnp.concatenate([gram[at:at + high] for at in range(0, rank, high)], axis=1)


def project(parts, snapshots):
    cells, snaps = snapshots.shape
    rank = parts[0].shape[0]
    return pl.pallas_call(
        lambda *refs: project_kernel(len(parts), *refs),
        in_specs=[VMEM] * (len(parts) + 1),
        out_specs=[VMEM] * 2,
        out_shape=[
            pltpu.VMEM((rank, cells), jnp.float32),
            pltpu.VMEM((rank * (snaps + rank) // LANES, LANES), jnp.float32),
        ],
        compiler_params=limit(16),
        name="project",
    )(*parts, snapshots)


def spread(row):
    return jnp.broadcast_to(row, (8, row.shape[1]))


def tall(tile, rank):
    return jnp.concatenate([tile] * (rank // 8), axis=0)


def lower_inverse(gram):
    rank, lanes = gram.shape
    block = math.gcd(rank, 8)
    row_at = lax.broadcasted_iota(jnp.int32, (rank, lanes), 0)
    lane_at = lax.broadcasted_iota(jnp.int32, (rank, lanes), 1)
    both = jnp.where(lane_at < rank, gram, jnp.where(lane_at == row_at + rank, 1.0, 0.0))
    pivots = jnp.ones((rank, lanes), jnp.float32)
    for base in range(0, rank, block):
        columns = [jnp.broadcast_to(both[:, base + at:base + at + 1], (rank, lanes)) for at in range(block)]
        corner = [[spread(columns[at][base + to:base + to + 1]) for at in range(block)] for to in range(block)]
        rows = [spread(both[base + at:base + at + 1]) for at in range(block)]
        eliminated = both
        for at in range(block):
            pivot = corner[at][at]
            inverse = 1.0 / pivot
            for to in range(at + 1, block):
                ratio = corner[to][at] * inverse
                rows[to] = rows[to] - ratio * rows[at]
                columns[to] = columns[to] - tall(ratio, rank) * columns[at]
                for along in range(at + 1, block):
                    corner[to][along] = corner[to][along] - ratio * corner[at][along]
            factor = jnp.where(row_at > base + at, columns[at] * tall(inverse, rank), 0.0)
            eliminated = eliminated - factor * tall(rows[at], rank)
            pivots = jnp.where(row_at == base + at, tall(pivot, rank), pivots)
        both = eliminated
    return (both / jnp.sqrt(pivots))[:, rank:2 * rank]


def factor_kernel(scale, parts, *refs):
    rows_ref, basis_ref, coefficients_ref, made_ref, sent = refs[parts:]
    snaps = coefficients_ref.shape[1]
    block = tree_sum([ref[...] for ref in refs[:parts]])
    rank = rows_ref.shape[0]
    tiles = snaps // LANES
    packed = block[tiles * rank:]
    turns = [packed] + [pltpu.roll(packed, LANES - at, 1) for at in range(rank, LANES, rank)]
    inverse = lower_inverse(jnp.concatenate(turns, axis=0))
    left = jnp.concatenate(thirds(inverse), axis=0)
    for at in range(tiles):
        part = block[at * rank:(at + 1) * rank]
        coefficients_ref[:, at * LANES:(at + 1) * LANES] = product(left, thirds(part), 0)
    left = jnp.concatenate(thirds(inverse * scale), axis=0)
    chunk = min(CHUNK, rows_ref.shape[1])
    copies = []
    for at in range(0, rows_ref.shape[1], chunk):
        span = pl.ds(at, chunk)
        made_ref[:, span] = product(left, thirds(rows_ref[:, span]), 0)
        copies.append(pltpu.make_async_copy(made_ref.at[:, span], basis_ref.at[:, span], sent.at[at // chunk]))
        copies[-1].start()
    for copy in copies:
        copy.wait()


def factor(parts, rows, scale, snaps):
    rank, cells = rows.shape
    return pl.pallas_call(
        lambda *refs: factor_kernel(scale, len(parts), *refs),
        in_specs=[VMEM] * (len(parts) + 1),
        out_specs=[HBM, VMEM],
        out_shape=[
            jax.ShapeDtypeStruct((rank, cells), jnp.float32),
            jax.ShapeDtypeStruct((rank, snaps), jnp.float32),
        ],
        scratch_shapes=[
            pltpu.VMEM((rank, cells), jnp.float32),
            pltpu.SemaphoreType.DMA((-(-cells // CHUNK),)),
        ],
        compiler_params=limit(16),
        name="factor",
    )(*parts, rows)


def exchange(block, axis, radix):
    count = lax.axis_size(axis)
    parts = [block]
    step = 1
    while step < count:
        block = tree_sum(parts)
        group = min(radix, count // step)
        parts = [block] + [swap(block, axis, step * at) for at in range(1, group)]
        step *= group
    return parts


def shards(snapshots, sketch):
    total_cells = snapshots.shape[0] * lax.axis_size("cells")
    partial_rows, held = sketch_rows(snapshots, sketch)
    rows, block = project(exchange(partial_rows, "snaps", 2), held)
    return factor(exchange(block, "cells", 4), rows, math.sqrt(total_cells), snapshots.shape[1])


def solution(mesh):
    return jax.shard_map(
        shards,
        mesh=mesh,
        in_specs=(P("cells", "snaps"), P("snaps", None)),
        out_specs=(P(None, "cells"), P(None, "snaps")),
        check_vma=False,
    )
```

```python
import math

import jax
import jax.numpy as jnp
from jax import lax
from jax.experimental import pallas as pl
from jax.experimental.pallas import tpu as pltpu
from jax.sharding import PartitionSpec as P

LANES = 128
CHUNK = 512
MIB = 1 << 20
AMPLIFIED = 512.0
BROKEN = 2e5
SHIFT = 3e-5
PASSES = 8
VMEM = pl.BlockSpec(memory_space=pltpu.VMEM)
HBM = pl.BlockSpec(memory_space=pltpu.HBM)


def limit(mebibytes):
    return pltpu.CompilerParams(vmem_limit_bytes=mebibytes * MIB)


def in_hbm(block):
    return pltpu.with_memory_space_constraint(block, pltpu.HBM)


def swap(block, axis, offset):
    count = lax.axis_size(axis)
    return lax.ppermute(block, axis, [(at, at ^ offset) for at in range(count)])


def tree_sum(parts):
    while len(parts) > 1:
        parts = [parts[at] + parts[at + 1] for at in range(0, len(parts), 2)]
    return parts[0]


def thirds(block):
    high = block.astype(jnp.bfloat16)
    rest = block - high.astype(jnp.float32)
    middle = rest.astype(jnp.bfloat16)
    low = (rest - middle.astype(jnp.float32)).astype(jnp.bfloat16)
    return high, middle, low


def product(left, right, right_dim):
    rank = left.shape[0] // 3
    dims = (((1,), (right_dim,)), ((), ()))
    high, middle, low = [
        lax.dot_general(left[:rank * (3 - at)], part, dims, preferred_element_type=jnp.float32)
        for at, part in enumerate(right)
    ]
    small = high[2 * rank:] + (middle[rank:] + low)
    return high[:rank] + ((high[rank:2 * rank] + middle[:rank]) + small)


def pieces(cells):
    if cells % 4:
        return [(0, cells)]
    return [(0, cells // 4), (cells // 4, cells // 4), (cells // 2, cells // 2)]


def sketch_kernel(sketch_ref, snapshots_ref, out_ref, held, sketch_held, arrived):
    fetches = pieces(held.shape[0])
    first = pltpu.make_async_copy(sketch_ref, sketch_held, arrived.at[len(fetches)])
    first.start()
    copies = []
    for at, (start, size) in enumerate(fetches):
        rows = pl.ds(start, size)
        copies.append(pltpu.make_async_copy(snapshots_ref.at[rows], held.at[rows], arrived.at[at]))
        copies[-1].start()
    first.wait()
    sketch = jnp.concatenate(thirds(sketch_held[...]), axis=0)
    for copy, (start, size) in zip(copies, fetches):
        copy.wait()
        chunk = min(CHUNK, size)
        for at in range(start, start + size, chunk):
            rows = pl.ds(at, chunk)
            out_ref[:, rows] = product(sketch, thirds(held[rows, :]), 1)


def sketch_rows(snapshots, sketch):
    cells, snaps = snapshots.shape
    rank = sketch.shape[1]
    return pl.pallas_call(
        sketch_kernel,
        in_specs=[HBM] * 2,
        out_specs=[VMEM] * 2,
        out_shape=[
            pltpu.VMEM((rank, cells), jnp.float32),
            pltpu.VMEM((cells, snaps), jnp.float32),
        ],
        scratch_shapes=[
            pltpu.VMEM((rank, snaps), jnp.float32),
            pltpu.SemaphoreType.DMA((len(pieces(cells)) + 1,)),
        ],
        compiler_params=limit(16),
        name="sketch_rows",
    )(in_hbm(sketch.T), in_hbm(snapshots))


def packed(gram):
    rank = gram.shape[0]
    high = rank * rank // LANES
    return jnp.concatenate([gram[at:at + high] for at in range(0, rank, high)], axis=1)


def project_kernel(parts, *refs):
    snapshots_ref = refs[parts]
    rows_ref, block_ref = refs[parts + 1:]
    rank, cells = rows_ref.shape
    snaps = snapshots_ref.shape[1]
    chunk = min(CHUNK, cells)
    sums = jnp.zeros((rank, snaps), jnp.float32)
    gram = jnp.zeros((rank, rank), jnp.float32)
    for at in range(cells // chunk):
        span = pl.ds(at * chunk, chunk)
        rows = tree_sum([ref[:, span] for ref in refs[:parts]])
        rows_ref[:, span] = rows
        split = thirds(rows)
        left = jnp.concatenate(split, axis=0)
        sums += product(left, thirds(snapshots_ref[span, :]), 0)
        gram += product(left, split, 1)
    tiles = snaps // LANES
    for at in range(tiles):
        block_ref[at * rank:(at + 1) * rank, :] = sums[:, at * LANES:(at + 1) * LANES]
    block_ref[tiles * rank:, :] = packed(gram)


def project(parts, snapshots):
    cells, snaps = snapshots.shape
    rank = parts[0].shape[0]
    return pl.pallas_call(
        lambda *refs: project_kernel(len(parts), *refs),
        in_specs=[VMEM] * (len(parts) + 1),
        out_specs=[VMEM] * 2,
        out_shape=[
            pltpu.VMEM((rank, cells), jnp.float32),
            pltpu.VMEM((rank * (snaps + rank) // LANES, LANES), jnp.float32),
        ],
        compiler_params=limit(16),
        name="project",
    )(*parts, snapshots)


def spread(row):
    return jnp.broadcast_to(row, (8, row.shape[1]))


def tall(tile, rank):
    return jnp.concatenate([tile] * (rank // 8), axis=0)


def lower_inverse(gram):
    rank, lanes = gram.shape
    block = math.gcd(rank, 4)
    row_at = lax.broadcasted_iota(jnp.int32, (rank, lanes), 0)
    lane_at = lax.broadcasted_iota(jnp.int32, (rank, lanes), 1)
    both = jnp.where(lane_at < rank, gram, jnp.where(lane_at == row_at + rank, 1.0, 0.0))
    pivots = jnp.ones((rank, lanes), jnp.float32)
    diagonal = jnp.sum(jnp.where(row_at == lane_at, gram, 0.0), axis=0, keepdims=True)
    for base in range(0, rank, block):
        columns = [jnp.broadcast_to(both[:, base + at:base + at + 1], (rank, lanes)) for at in range(block)]
        corner = [[spread(columns[at][base + to:base + to + 1]) for at in range(block)] for to in range(block)]
        rows = [spread(both[base + at:base + at + 1]) for at in range(block)]
        eliminated = both
        for at in range(block):
            pivot = corner[at][at]
            inverse = 1.0 / pivot
            for to in range(at + 1, block):
                ratio = corner[to][at] * inverse
                rows[to] = rows[to] - ratio * rows[at]
                columns[to] = columns[to] - tall(ratio, rank) * columns[at]
                for along in range(at + 1, block):
                    corner[to][along] = corner[to][along] - ratio * corner[at][along]
            factor = jnp.where(row_at > base + at, columns[at] * tall(inverse, rank), 0.0)
            eliminated = eliminated - factor * tall(rows[at], rank)
            pivots = jnp.where(row_at == base + at, tall(pivot, rank), pivots)
        both = eliminated
    inverse = (both / jnp.sqrt(pivots))[:, rank:2 * rank]
    return inverse, jnp.sum(inverse * inverse * diagonal[:, :rank])


def factor_kernel(scale, parts, *refs):
    rows_ref, basis_ref, coefficients_ref, amplified_ref = refs[parts:]
    snaps = coefficients_ref.shape[1]
    block = tree_sum([ref[...] for ref in refs[:parts]])
    rank = rows_ref.shape[0]
    tiles = snaps // LANES
    full = block[tiles * rank:]
    turns = [full] + [pltpu.roll(full, LANES - at, 1) for at in range(rank, LANES, rank)]
    gram = jnp.concatenate(turns, axis=0)
    inverse, amplified = lower_inverse(gram)
    sound = amplified <= BROKEN
    amplified_ref[0, 0] = jnp.where(sound, amplified, BROKEN)

    def apply(inverse):
        left = jnp.concatenate(thirds(inverse), axis=0)
        for at in range(tiles):
            part = block[at * rank:(at + 1) * rank]
            coefficients_ref[:, at * LANES:(at + 1) * LANES] = product(left, thirds(part), 0)
        left = jnp.concatenate(thirds(inverse * scale), axis=0)
        chunk = math.gcd(CHUNK, rows_ref.shape[1])
        for at in range(0, rows_ref.shape[1], chunk):
            span = pl.ds(at, chunk)
            basis_ref[:, span] = product(left, thirds(rows_ref[:, span]), 0)

    apply(inverse)

    @pl.when(jnp.logical_not(sound))
    def _():
        row_at = lax.broadcasted_iota(jnp.int32, gram.shape, 0)
        lane_at = lax.broadcasted_iota(jnp.int32, gram.shape, 1)
        apply(lower_inverse(jnp.where(row_at == lane_at, gram * (1 + SHIFT), gram))[0])


def factor(parts, rows, scale, snaps):
    rank, cells = rows.shape
    return pl.pallas_call(
        lambda *refs: factor_kernel(scale, len(parts), *refs),
        in_specs=[VMEM] * (len(parts) + 1),
        out_specs=[VMEM] * 2 + [pl.BlockSpec(memory_space=pltpu.SMEM)],
        out_shape=[
            pltpu.HBM((rank, cells), jnp.float32),
            pltpu.HBM((rank, snaps), jnp.float32),
            jax.ShapeDtypeStruct((1, 1), jnp.float32),
        ],
        compiler_params=limit(16),
        name="factor",
    )(*parts, rows)


def exchange(block, axis, radix):
    count = lax.axis_size(axis)
    parts = [block]
    step = 1
    while step < count:
        block = tree_sum(parts)
        group = min(radix, count // step)
        parts = [block] + [swap(block, axis, step * at) for at in range(1, group)]
        step *= group
    return parts


def gram_kernel(scale, rows_ref, gram_ref):
    rank, cells = rows_ref.shape
    chunk = math.gcd(CHUNK, cells)
    gram = jnp.zeros((rank, rank), jnp.float32)
    for at in range(0, cells, chunk):
        split = thirds(rows_ref[:, pl.ds(at, chunk)])
        gram += product(jnp.concatenate(split, axis=0), split, 1)
    gram_ref[...] = packed(gram * scale)


def refine(rows, coefficients, total_cells):
    rank, snaps = coefficients.shape
    gram = pl.pallas_call(
        lambda *refs: gram_kernel(1 / total_cells, *refs),
        in_specs=[VMEM],
        out_specs=VMEM,
        out_shape=jax.ShapeDtypeStruct((rank * rank // LANES, LANES), jnp.float32),
        compiler_params=limit(16),
        name="gram",
    )(rows)
    gram = tree_sum(exchange(gram, "cells", 4))
    tiles = [coefficients[:, at:at + LANES] for at in range(0, snaps, LANES)]
    return factor([jnp.concatenate(tiles + [gram], axis=0)], rows, 1.0, snaps)


def shards(snapshots, sketch):
    total_cells = snapshots.shape[0] * lax.axis_size("cells")
    partial_rows, held = sketch_rows(snapshots, sketch)
    rows, block = project(exchange(partial_rows, "snaps", 2), held)
    first = factor(exchange(block, "cells", 4), rows, math.sqrt(total_cells), snapshots.shape[1])
    basis, coefficients, _, _ = lax.while_loop(
        lambda state: jnp.logical_and(state[2][0, 0] > AMPLIFIED, state[3] < PASSES),
        lambda state: (*refine(state[0], state[1], total_cells), state[3] + 1),
        (*first, jnp.int32(0)),
    )
    return (basis, coefficients)


def solution(mesh):
    return jax.shard_map(
        shards,
        mesh=mesh,
        in_specs=(P("cells", "snaps"), P("snaps", None)),
        out_specs=(P(None, "cells"), P(None, "snaps")),
        check_vma=False,
    )
```

```python
import math

import jax
import jax.numpy as jnp
from jax import lax
from jax.experimental import pallas as pl
from jax.experimental.pallas import tpu as pltpu
from jax.sharding import PartitionSpec as P

LANES = 128
CHUNK = 512
MIB = 1 << 20
AMPLIFIED = 512.0
BROKEN = 2e5
SHIFT = 3e-5
PASSES = 8
VMEM = pl.BlockSpec(memory_space=pltpu.VMEM)
HBM = pl.BlockSpec(memory_space=pltpu.HBM)


def limit(mebibytes):
    return pltpu.CompilerParams(vmem_limit_bytes=mebibytes * MIB)


def in_hbm(block):
    return pltpu.with_memory_space_constraint(block, pltpu.HBM)


def swap(block, axis, offset):
    count = lax.axis_size(axis)
    return lax.ppermute(block, axis, [(at, at ^ offset) for at in range(count)])


def tree_sum(parts):
    while len(parts) > 1:
        parts = [parts[at] + parts[at + 1] for at in range(0, len(parts), 2)]
    return parts[0]


def thirds(block):
    high = block.astype(jnp.bfloat16)
    rest = block - high.astype(jnp.float32)
    middle = rest.astype(jnp.bfloat16)
    low = (rest - middle.astype(jnp.float32)).astype(jnp.bfloat16)
    return high, middle, low


def product(left, right, right_dim):
    rank = left.shape[0] // 3
    dims = (((1,), (right_dim,)), ((), ()))
    high, middle, low = [
        lax.dot_general(left[:rank * (3 - at)], part, dims, preferred_element_type=jnp.float32)
        for at, part in enumerate(right)
    ]
    small = high[2 * rank:] + (middle[rank:] + low)
    return high[:rank] + ((high[rank:2 * rank] + middle[:rank]) + small)


def pieces(cells):
    if cells % 4:
        return [(0, cells)]
    return [(0, cells // 4), (cells // 4, cells // 4), (cells // 2, cells // 2)]


def sketch_kernel(sketch_ref, snapshots_ref, out_ref, held, sketch_held, arrived):
    fetches = pieces(held.shape[0])
    first = pltpu.make_async_copy(sketch_ref, sketch_held, arrived.at[len(fetches)])
    first.start()
    copies = []
    for at, (start, size) in enumerate(fetches):
        rows = pl.ds(start, size)
        copies.append(pltpu.make_async_copy(snapshots_ref.at[rows], held.at[rows], arrived.at[at]))
        copies[-1].start()
    first.wait()
    sketch = jnp.concatenate(thirds(sketch_held[...]), axis=0)
    for copy, (start, size) in zip(copies, fetches):
        copy.wait()
        chunk = min(CHUNK, size)
        for at in range(start, start + size, chunk):
            rows = pl.ds(at, chunk)
            out_ref[:, rows] = product(sketch, thirds(held[rows, :]), 1)


def sketch_rows(snapshots, sketch):
    cells, snaps = snapshots.shape
    rank = sketch.shape[1]
    return pl.pallas_call(
        sketch_kernel,
        in_specs=[HBM] * 2,
        out_specs=[VMEM] * 2,
        out_shape=[
            pltpu.VMEM((rank, cells), jnp.float32),
            pltpu.VMEM((cells, snaps), jnp.float32),
        ],
        scratch_shapes=[
            pltpu.VMEM((rank, snaps), jnp.float32),
            pltpu.SemaphoreType.DMA((len(pieces(cells)) + 1,)),
        ],
        compiler_params=limit(16),
        name="sketch_rows",
    )(in_hbm(sketch.T), in_hbm(snapshots))


def packed(gram):
    rank = gram.shape[0]
    high = rank * rank // LANES
    return jnp.concatenate([gram[at:at + high] for at in range(0, rank, high)], axis=1)


def project_kernel(parts, *refs):
    snapshots_ref = refs[parts]
    rows_ref, block_ref = refs[parts + 1:]
    rank, cells = rows_ref.shape
    snaps = snapshots_ref.shape[1]
    chunk = min(CHUNK, cells)
    sums = jnp.zeros((rank, snaps), jnp.float32)
    gram = jnp.zeros((rank, rank), jnp.float32)
    for at in range(cells // chunk):
        span = pl.ds(at * chunk, chunk)
        rows = tree_sum([ref[:, span] for ref in refs[:parts]])
        rows_ref[:, span] = rows
        split = thirds(rows)
        left = jnp.concatenate(split, axis=0)
        sums += product(left, thirds(snapshots_ref[span, :]), 0)
        gram += product(left, split, 1)
    tiles = snaps // LANES
    for at in range(tiles):
        block_ref[at * rank:(at + 1) * rank, :] = sums[:, at * LANES:(at + 1) * LANES]
    block_ref[tiles * rank:, :] = packed(gram)


def project(parts, snapshots):
    cells, snaps = snapshots.shape
    rank = parts[0].shape[0]
    return pl.pallas_call(
        lambda *refs: project_kernel(len(parts), *refs),
        in_specs=[VMEM] * (len(parts) + 1),
        out_specs=[VMEM] * 2,
        out_shape=[
            pltpu.VMEM((rank, cells), jnp.float32),
            pltpu.VMEM((rank * (snaps + rank) // LANES, LANES), jnp.float32),
        ],
        compiler_params=limit(16),
        name="project",
    )(*parts, snapshots)


def spread(row):
    return jnp.broadcast_to(row, (8, row.shape[1]))


def tall(tile, rank):
    return jnp.concatenate([tile] * (rank // 8), axis=0)


def lower_inverse(gram):
    rank, lanes = gram.shape
    block = math.gcd(rank, 4)
    row_at = lax.broadcasted_iota(jnp.int32, (rank, lanes), 0)
    lane_at = lax.broadcasted_iota(jnp.int32, (rank, lanes), 1)
    both = jnp.where(lane_at < rank, gram, jnp.where(lane_at == row_at + rank, 1.0, 0.0))
    pivots = jnp.ones((rank, lanes), jnp.float32)
    diagonal = jnp.sum(jnp.where(row_at == lane_at, gram, 0.0), axis=0, keepdims=True)
    for base in range(0, rank, block):
        columns = [jnp.broadcast_to(both[:, base + at:base + at + 1], (rank, lanes)) for at in range(block)]
        corner = [[spread(columns[at][base + to:base + to + 1]) for at in range(block)] for to in range(block)]
        rows = [spread(both[base + at:base + at + 1]) for at in range(block)]
        eliminated = both
        for at in range(block):
            pivot = corner[at][at]
            inverse = 1.0 / pivot
            for to in range(at + 1, block):
                ratio = corner[to][at] * inverse
                rows[to] = rows[to] - ratio * rows[at]
                columns[to] = columns[to] - tall(ratio, rank) * columns[at]
                for along in range(at + 1, block):
                    corner[to][along] = corner[to][along] - ratio * corner[at][along]
            factor = jnp.where(row_at > base + at, columns[at] * tall(inverse, rank), 0.0)
            eliminated = eliminated - factor * tall(rows[at], rank)
            pivots = jnp.where(row_at == base + at, tall(pivot, rank), pivots)
        both = eliminated
    inverse = (both / jnp.sqrt(pivots))[:, rank:2 * rank]
    return inverse, jnp.sum(inverse * inverse * diagonal[:, :rank])


def factor_kernel(scale, parts, *refs):
    rows_ref, basis_ref, coefficients_ref, amplified_ref = refs[parts:]
    snaps = coefficients_ref.shape[1]
    block = tree_sum([ref[...] for ref in refs[:parts]])
    rank = rows_ref.shape[0]
    tiles = snaps // LANES
    full = block[tiles * rank:]
    turns = [full] + [pltpu.roll(full, LANES - at, 1) for at in range(rank, LANES, rank)]
    gram = jnp.concatenate(turns, axis=0)
    inverse, amplified = lower_inverse(gram)
    sound = amplified <= BROKEN
    amplified_ref[0, 0] = jnp.where(sound, amplified, BROKEN)

    def apply(inverse):
        left = jnp.concatenate(thirds(inverse), axis=0)
        for at in range(tiles):
            part = block[at * rank:(at + 1) * rank]
            coefficients_ref[:, at * LANES:(at + 1) * LANES] = product(left, thirds(part), 0)
        left = jnp.concatenate(thirds(inverse * scale), axis=0)
        chunk = math.gcd(CHUNK, rows_ref.shape[1])
        for at in range(0, rows_ref.shape[1], chunk):
            span = pl.ds(at, chunk)
            basis_ref[:, span] = product(left, thirds(rows_ref[:, span]), 0)

    apply(inverse)

    @pl.when(jnp.logical_not(sound))
    def _():
        row_at = lax.broadcasted_iota(jnp.int32, gram.shape, 0)
        lane_at = lax.broadcasted_iota(jnp.int32, gram.shape, 1)
        apply(lower_inverse(jnp.where(row_at == lane_at, gram * (1 + SHIFT), gram))[0])


def factor(parts, rows, scale, snaps):
    rank, cells = rows.shape
    return pl.pallas_call(
        lambda *refs: factor_kernel(scale, len(parts), *refs),
        in_specs=[VMEM] * (len(parts) + 1),
        out_specs=[VMEM] * 2 + [pl.BlockSpec(memory_space=pltpu.SMEM)],
        out_shape=[
            pltpu.HBM((rank, cells), jnp.float32),
            pltpu.HBM((rank, snaps), jnp.float32),
            jax.ShapeDtypeStruct((1, 1), jnp.float32),
        ],
        compiler_params=limit(16),
        name="factor",
    )(*parts, rows)


def exchange(block, axis, radix):
    count = lax.axis_size(axis)
    parts = [block]
    step = 1
    while step < count:
        block = tree_sum(parts)
        group = min(radix, count // step)
        parts = [swap(block, axis, step * at) for at in range(group - 1, 0, -1)]
        parts = [block] + parts[::-1]
        step *= group
    return parts


def gram_kernel(scale, rows_ref, gram_ref):
    rank, cells = rows_ref.shape
    chunk = math.gcd(CHUNK, cells)
    gram = jnp.zeros((rank, rank), jnp.float32)
    for at in range(0, cells, chunk):
        split = thirds(rows_ref[:, pl.ds(at, chunk)])
        gram += product(jnp.concatenate(split, axis=0), split, 1)
    gram_ref[...] = packed(gram * scale)


def refine(rows, coefficients, total_cells):
    rank, snaps = coefficients.shape
    gram = pl.pallas_call(
        lambda *refs: gram_kernel(1 / total_cells, *refs),
        in_specs=[VMEM],
        out_specs=VMEM,
        out_shape=jax.ShapeDtypeStruct((rank * rank // LANES, LANES), jnp.float32),
        compiler_params=limit(16),
        name="gram",
    )(rows)
    gram = tree_sum(exchange(gram, "cells", 4))
    tiles = [coefficients[:, at:at + LANES] for at in range(0, snaps, LANES)]
    return factor([jnp.concatenate(tiles + [gram], axis=0)], rows, 1.0, snaps)


def shards(snapshots, sketch):
    total_cells = snapshots.shape[0] * lax.axis_size("cells")
    partial_rows, held = sketch_rows(snapshots, sketch)
    rows, block = project(exchange(partial_rows, "snaps", 2), held)
    first = factor(exchange(block, "cells", 4), rows, math.sqrt(total_cells), snapshots.shape[1])
    basis, coefficients, _, _ = lax.while_loop(
        lambda state: jnp.logical_and(state[2][0, 0] > AMPLIFIED, state[3] < PASSES),
        lambda state: (*refine(state[0], state[1], total_cells), state[3] + 1),
        (*first, jnp.int32(0)),
    )
    return (basis, coefficients)


def solution(mesh):
    return jax.shard_map(
        shards,
        mesh=mesh,
        in_specs=(P("cells", "snaps"), P("snaps", None)),
        out_specs=(P(None, "cells"), P(None, "snaps")),
        check_vma=False,
    )
```

```python
import math

import jax
import jax.numpy as jnp
from jax import lax
from jax.experimental import pallas as pl
from jax.experimental.pallas import tpu as pltpu
from jax.sharding import PartitionSpec as P

LANES = 128
CHUNK = 512
MIB = 1 << 20
AMPLIFIED = 512.0
BROKEN = 2e5
SHIFT = 3e-5
PASSES = 8
VMEM = pl.BlockSpec(memory_space=pltpu.VMEM)
HBM = pl.BlockSpec(memory_space=pltpu.HBM)


def limit(mebibytes):
    return pltpu.CompilerParams(vmem_limit_bytes=mebibytes * MIB)


def in_hbm(block):
    return pltpu.with_memory_space_constraint(block, pltpu.HBM)


def swap(block, axis, offset):
    count = lax.axis_size(axis)
    return lax.ppermute(block, axis, [(at, at ^ offset) for at in range(count)])


def tree_sum(parts):
    while len(parts) > 1:
        parts = [parts[at] + parts[at + 1] for at in range(0, len(parts), 2)]
    return parts[0]


def thirds(block):
    high = block.astype(jnp.bfloat16)
    rest = block - high.astype(jnp.float32)
    middle = rest.astype(jnp.bfloat16)
    low = (rest - middle.astype(jnp.float32)).astype(jnp.bfloat16)
    return high, middle, low


def product(left, right, right_dim):
    rank = left.shape[0] // 3
    dims = (((1,), (right_dim,)), ((), ()))
    high, middle, low = [
        lax.dot_general(left[:rank * (3 - at)], part, dims, preferred_element_type=jnp.float32)
        for at, part in enumerate(right)
    ]
    small = high[2 * rank:] + (middle[rank:] + low)
    return high[:rank] + ((high[rank:2 * rank] + middle[:rank]) + small)


def pieces(cells):
    if cells % 2:
        return [(0, cells)]
    return [(0, cells // 2), (cells // 2, cells // 2)]


def sketch_kernel(sketch_ref, snapshots_ref, out_ref, held, sketch_held, arrived):
    fetches = pieces(held.shape[0])
    first = pltpu.make_async_copy(sketch_ref, sketch_held, arrived.at[len(fetches)])
    first.start()
    copies = []
    for at, (start, size) in enumerate(fetches):
        rows = pl.ds(start, size)
        copies.append(pltpu.make_async_copy(snapshots_ref.at[rows], held.at[rows], arrived.at[at]))
        copies[-1].start()
    first.wait()
    sketch = jnp.concatenate(thirds(sketch_held[...]), axis=0)
    for copy, (start, size) in zip(copies, fetches):
        copy.wait()
        chunk = min(CHUNK, size)
        for at in range(start, start + size, chunk):
            rows = pl.ds(at, chunk)
            out_ref[:, rows] = product(sketch, thirds(held[rows, :]), 1)


def sketch_rows(snapshots, sketch):
    cells, snaps = snapshots.shape
    rank = sketch.shape[1]
    return pl.pallas_call(
        sketch_kernel,
        in_specs=[HBM] * 2,
        out_specs=[VMEM] * 2,
        out_shape=[
            pltpu.VMEM((rank, cells), jnp.float32),
            pltpu.VMEM((cells, snaps), jnp.float32),
        ],
        scratch_shapes=[
            pltpu.VMEM((rank, snaps), jnp.float32),
            pltpu.SemaphoreType.DMA((len(pieces(cells)) + 1,)),
        ],
        compiler_params=limit(16),
        name="sketch_rows",
    )(in_hbm(sketch.T), in_hbm(snapshots))


def packed(gram):
    rank = gram.shape[0]
    high = rank * rank // LANES
    return jnp.concatenate([gram[at:at + high] for at in range(0, rank, high)], axis=1)


def project_kernel(parts, *refs):
    snapshots_ref = refs[parts]
    rows_ref, block_ref = refs[parts + 1:]
    rank, cells = rows_ref.shape
    snaps = snapshots_ref.shape[1]
    chunk = min(CHUNK, cells)
    sums = jnp.zeros((rank, snaps), jnp.float32)
    gram = jnp.zeros((rank, rank), jnp.float32)
    for at in range(cells // chunk):
        span = pl.ds(at * chunk, chunk)
        rows = tree_sum([ref[:, span] for ref in refs[:parts]])
        rows_ref[:, span] = rows
        split = thirds(rows)
        left = jnp.concatenate(split, axis=0)
        sums += product(left, thirds(snapshots_ref[span, :]), 0)
        gram += product(left, split, 1)
    tiles = snaps // LANES
    for at in range(tiles):
        block_ref[at * rank:(at + 1) * rank, :] = sums[:, at * LANES:(at + 1) * LANES]
    block_ref[tiles * rank:, :] = packed(gram)


def project(parts, snapshots):
    cells, snaps = snapshots.shape
    rank = parts[0].shape[0]
    return pl.pallas_call(
        lambda *refs: project_kernel(len(parts), *refs),
        in_specs=[VMEM] * (len(parts) + 1),
        out_specs=[VMEM] * 2,
        out_shape=[
            pltpu.VMEM((rank, cells), jnp.float32),
            pltpu.VMEM((rank * (snaps + rank) // LANES, LANES), jnp.float32),
        ],
        compiler_params=limit(16),
        name="project",
    )(*parts, snapshots)


def spread(row):
    return jnp.broadcast_to(row, (8, row.shape[1]))


def tall(tile, rank):
    return jnp.concatenate([tile] * (rank // 8), axis=0)


def lower_inverse(gram):
    rank, lanes = gram.shape
    block = math.gcd(rank, 4)
    row_at = lax.broadcasted_iota(jnp.int32, (rank, lanes), 0)
    lane_at = lax.broadcasted_iota(jnp.int32, (rank, lanes), 1)
    both = jnp.where(lane_at < rank, gram, jnp.where(lane_at == row_at + rank, 1.0, 0.0))
    pivots = jnp.ones((rank, lanes), jnp.float32)
    diagonal = jnp.sum(jnp.where(row_at == lane_at, gram, 0.0), axis=0, keepdims=True)
    for base in range(0, rank, block):
        columns = [jnp.broadcast_to(both[:, base + at:base + at + 1], (rank, lanes)) for at in range(block)]
        corner = [[spread(columns[at][base + to:base + to + 1]) for at in range(block)] for to in range(block)]
        rows = [spread(both[base + at:base + at + 1]) for at in range(block)]
        eliminated = both
        for at in range(block):
            pivot = corner[at][at]
            inverse = 1.0 / pivot
            for to in range(at + 1, block):
                ratio = corner[to][at] * inverse
                rows[to] = rows[to] - ratio * rows[at]
                columns[to] = columns[to] - tall(ratio, rank) * columns[at]
                for along in range(at + 1, block):
                    corner[to][along] = corner[to][along] - ratio * corner[at][along]
            factor = jnp.where(row_at > base + at, columns[at] * tall(inverse, rank), 0.0)
            eliminated = eliminated - factor * tall(rows[at], rank)
            pivots = jnp.where(row_at == base + at, tall(pivot, rank), pivots)
        both = eliminated
    inverse = (both / jnp.sqrt(pivots))[:, rank:2 * rank]
    return inverse, jnp.sum(inverse * inverse * diagonal[:, :rank])


def factor_kernel(scale, parts, *refs):
    rows_ref, basis_ref, coefficients_ref, amplified_ref = refs[parts:]
    snaps = coefficients_ref.shape[1]
    block = tree_sum([ref[...] for ref in refs[:parts]])
    rank = rows_ref.shape[0]
    tiles = snaps // LANES
    full = block[tiles * rank:]
    turns = [full] + [pltpu.roll(full, LANES - at, 1) for at in range(rank, LANES, rank)]
    gram = jnp.concatenate(turns, axis=0)
    inverse, amplified = lower_inverse(gram)
    sound = amplified <= BROKEN
    amplified_ref[0, 0] = jnp.where(sound, amplified, BROKEN)

    def apply(inverse):
        left = jnp.concatenate(thirds(inverse), axis=0)
        for at in range(tiles):
            part = block[at * rank:(at + 1) * rank]
            coefficients_ref[:, at * LANES:(at + 1) * LANES] = product(left, thirds(part), 0)
        left = jnp.concatenate(thirds(inverse * scale), axis=0)
        chunk = math.gcd(CHUNK, rows_ref.shape[1])
        for at in range(0, rows_ref.shape[1], chunk):
            span = pl.ds(at, chunk)
            basis_ref[:, span] = product(left, thirds(rows_ref[:, span]), 0)

    apply(inverse)

    @pl.when(jnp.logical_not(sound))
    def _():
        row_at = lax.broadcasted_iota(jnp.int32, gram.shape, 0)
        lane_at = lax.broadcasted_iota(jnp.int32, gram.shape, 1)
        apply(lower_inverse(jnp.where(row_at == lane_at, gram * (1 + SHIFT), gram))[0])


def factor(parts, rows, scale, snaps):
    rank, cells = rows.shape
    return pl.pallas_call(
        lambda *refs: factor_kernel(scale, len(parts), *refs),
        in_specs=[VMEM] * (len(parts) + 1),
        out_specs=[VMEM] * 2 + [pl.BlockSpec(memory_space=pltpu.SMEM)],
        out_shape=[
            pltpu.HBM((rank, cells), jnp.float32),
            pltpu.HBM((rank, snaps), jnp.float32),
            jax.ShapeDtypeStruct((1, 1), jnp.float32),
        ],
        compiler_params=limit(16),
        name="factor",
    )(*parts, rows)


def exchange(block, axis, radix):
    count = lax.axis_size(axis)
    parts = [block]
    step = 1
    while step < count:
        block = tree_sum(parts)
        group = min(radix, count // step)
        parts = [swap(block, axis, step * at) for at in range(group - 1, 0, -1)]
        parts = [block] + parts
        step *= group
    return parts


def gram_kernel(scale, rows_ref, gram_ref):
    rank, cells = rows_ref.shape
    chunk = math.gcd(CHUNK, cells)
    gram = jnp.zeros((rank, rank), jnp.float32)
    for at in range(0, cells, chunk):
        split = thirds(rows_ref[:, pl.ds(at, chunk)])
        gram += product(jnp.concatenate(split, axis=0), split, 1)
    gram_ref[...] = packed(gram * scale)


def refine(rows, coefficients, total_cells):
    rank, snaps = coefficients.shape
    gram = pl.pallas_call(
        lambda *refs: gram_kernel(1 / total_cells, *refs),
        in_specs=[VMEM],
        out_specs=VMEM,
        out_shape=jax.ShapeDtypeStruct((rank * rank // LANES, LANES), jnp.float32),
        compiler_params=limit(16),
        name="gram",
    )(rows)
    gram = tree_sum(exchange(gram, "cells", 4))
    tiles = [coefficients[:, at:at + LANES] for at in range(0, snaps, LANES)]
    return factor([jnp.concatenate(tiles + [gram], axis=0)], rows, 1.0, snaps)


def shards(snapshots, sketch):
    total_cells = snapshots.shape[0] * lax.axis_size("cells")
    partial_rows, held = sketch_rows(snapshots, sketch)
    rows, block = project(exchange(partial_rows, "snaps", 2), held)
    first = factor(exchange(block, "cells", 4), rows, math.sqrt(total_cells), snapshots.shape[1])
    basis, coefficients, _, _ = lax.while_loop(
        lambda state: jnp.logical_and(state[2][0, 0] > AMPLIFIED, state[3] < PASSES),
        lambda state: (*refine(state[0], state[1], total_cells), state[3] + 1),
        (*first, jnp.int32(0)),
    )
    return (basis, coefficients)


def solution(mesh):
    return jax.shard_map(
        shards,
        mesh=mesh,
        in_specs=(P("cells", "snaps"), P("snaps", None)),
        out_specs=(P(None, "cells"), P(None, "snaps")),
        check_vma=False,
    )
```

```python
import math

import jax
import jax.numpy as jnp
from jax import lax
from jax.experimental import pallas as pl
from jax.experimental.pallas import tpu as pltpu
from jax.sharding import PartitionSpec as P

LANES = 128
CHUNK = 512
MIB = 1 << 20
AMPLIFIED = 512.0
BROKEN = 2e5
SHIFT = 3e-5
PASSES = 8
VMEM = pl.BlockSpec(memory_space=pltpu.VMEM)
HBM = pl.BlockSpec(memory_space=pltpu.HBM)


def limit(mebibytes):
    return pltpu.CompilerParams(vmem_limit_bytes=mebibytes * MIB)


def in_hbm(block):
    return pltpu.with_memory_space_constraint(block, pltpu.HBM)


def swap(block, axis, offset):
    count = lax.axis_size(axis)
    return lax.ppermute(block, axis, [(at, at ^ offset) for at in range(count)])


def tree_sum(parts):
    while len(parts) > 1:
        parts = [parts[at] + parts[at + 1] for at in range(0, len(parts), 2)]
    return parts[0]


def thirds(block):
    high = block.astype(jnp.bfloat16)
    rest = block - high.astype(jnp.float32)
    middle = rest.astype(jnp.bfloat16)
    low = (rest - middle.astype(jnp.float32)).astype(jnp.bfloat16)
    return high, middle, low


def product(left, right, right_dim):
    rank = left.shape[0] // 3
    dims = (((1,), (right_dim,)), ((), ()))
    high, middle, low = [
        lax.dot_general(left[:rank * (3 - at)], part, dims, preferred_element_type=jnp.float32)
        for at, part in enumerate(right)
    ]
    small = high[2 * rank:] + (middle[rank:] + low)
    return high[:rank] + ((high[rank:2 * rank] + middle[:rank]) + small)


def pieces(cells):
    if cells % 4:
        return [(0, cells)]
    return [(0, cells // 4), (cells // 4, cells // 4), (cells // 2, cells // 2)]


def sketch_kernel(sketch_ref, snapshots_ref, out_ref, held, sketch_held, arrived):
    fetches = pieces(held.shape[0])
    first = pltpu.make_async_copy(sketch_ref, sketch_held, arrived.at[len(fetches)])
    first.start()
    copies = []
    for at, (start, size) in enumerate(fetches):
        rows = pl.ds(start, size)
        copies.append(pltpu.make_async_copy(snapshots_ref.at[rows], held.at[rows], arrived.at[at]))
        copies[-1].start()
    first.wait()
    sketch = jnp.concatenate(thirds(sketch_held[...]), axis=0)
    for copy, (start, size) in zip(copies, fetches):
        copy.wait()
        chunk = min(CHUNK, size)
        for at in range(start, start + size, chunk):
            rows = pl.ds(at, chunk)
            out_ref[:, rows] = product(sketch, thirds(held[rows, :].T), 0)


def sketch_rows(snapshots, sketch):
    cells, snaps = snapshots.shape
    rank = sketch.shape[1]
    return pl.pallas_call(
        sketch_kernel,
        in_specs=[HBM] * 2,
        out_specs=[VMEM] * 2,
        out_shape=[
            pltpu.VMEM((rank, cells), jnp.float32),
            pltpu.VMEM((cells, snaps), jnp.float32),
        ],
        scratch_shapes=[
            pltpu.VMEM((rank, snaps), jnp.float32),
            pltpu.SemaphoreType.DMA((len(pieces(cells)) + 1,)),
        ],
        compiler_params=limit(16),
        name="sketch_rows",
    )(in_hbm(sketch.T), in_hbm(snapshots))


def packed(gram):
    rank = gram.shape[0]
    high = rank * rank // LANES
    return jnp.concatenate([gram[at:at + high] for at in range(0, rank, high)], axis=1)


def project_kernel(parts, *refs):
    snapshots_ref = refs[parts]
    rows_ref, block_ref = refs[parts + 1:]
    rank, cells = rows_ref.shape
    snaps = snapshots_ref.shape[1]
    chunk = min(CHUNK, cells)
    sums = jnp.zeros((rank, snaps), jnp.float32)
    gram = jnp.zeros((rank, rank), jnp.float32)
    for at in range(cells // chunk):
        span = pl.ds(at * chunk, chunk)
        rows = tree_sum([ref[:, span] for ref in refs[:parts]])
        rows_ref[:, span] = rows
        split = thirds(rows)
        left = jnp.concatenate(split, axis=0)
        sums += product(left, thirds(snapshots_ref[span, :]), 0)
        gram += product(left, split, 1)
    tiles = snaps // LANES
    for at in range(tiles):
        block_ref[at * rank:(at + 1) * rank, :] = sums[:, at * LANES:(at + 1) * LANES]
    block_ref[tiles * rank:, :] = packed(gram)


def project(parts, snapshots):
    cells, snaps = snapshots.shape
    rank = parts[0].shape[0]
    return pl.pallas_call(
        lambda *refs: project_kernel(len(parts), *refs),
        in_specs=[VMEM] * (len(parts) + 1),
        out_specs=[VMEM] * 2,
        out_shape=[
            pltpu.VMEM((rank, cells), jnp.float32),
            pltpu.VMEM((rank * (snaps + rank) // LANES, LANES), jnp.float32),
        ],
        compiler_params=limit(16),
        name="project",
    )(*parts, snapshots)


def spread(row):
    return jnp.broadcast_to(row, (8, row.shape[1]))


def tall(tile, rank):
    return jnp.concatenate([tile] * (rank // 8), axis=0)


def lower_inverse(gram):
    rank, lanes = gram.shape
    block = math.gcd(rank, 4)
    row_at = lax.broadcasted_iota(jnp.int32, (rank, lanes), 0)
    lane_at = lax.broadcasted_iota(jnp.int32, (rank, lanes), 1)
    both = jnp.where(lane_at < rank, gram, jnp.where(lane_at == row_at + rank, 1.0, 0.0))
    pivots = jnp.ones((rank, lanes), jnp.float32)
    diagonal = jnp.sum(jnp.where(row_at == lane_at, gram, 0.0), axis=0, keepdims=True)
    columns = [jnp.broadcast_to(both[:, at:at + 1], (rank, lanes)) for at in range(block)]
    for base in range(0, rank, block):
        later = range(base + block, min(base + 2 * block, rank))
        upcoming = [jnp.broadcast_to(both[:, at:at + 1], (rank, lanes)) for at in later]
        corner = [[spread(columns[at][base + to:base + to + 1]) for at in range(block)] for to in range(block)]
        rows = [spread(both[base + at:base + at + 1]) for at in range(block)]
        for at in range(block):
            pivot = corner[at][at]
            inverse = 1.0 / pivot
            for to in range(at + 1, block):
                ratio = corner[to][at] * inverse
                rows[to] = rows[to] - ratio * rows[at]
                columns[to] = columns[to] - tall(ratio, rank) * columns[at]
                for along in range(at + 1, block):
                    corner[to][along] = corner[to][along] - ratio * corner[at][along]
            factor = jnp.where(row_at > base + at, columns[at] * tall(inverse, rank), 0.0)
            both = both - factor * tall(rows[at], rank)
            for to, place in enumerate(later):
                upcoming[to] = upcoming[to] - factor * tall(spread(columns[at][place:place + 1]), rank)
            pivots = jnp.where(row_at == base + at, tall(pivot, rank), pivots)
        columns = upcoming
    inverse = (both * lax.rsqrt(pivots))[:, rank:2 * rank]
    return inverse, jnp.sum(inverse * inverse * diagonal[:, :rank])


def factor_kernel(scale, parts, *refs):
    rows_ref, basis_ref, coefficients_ref, amplified_ref = refs[parts:]
    snaps = coefficients_ref.shape[1]
    block = tree_sum([ref[...] for ref in refs[:parts]])
    rank = rows_ref.shape[0]
    tiles = snaps // LANES
    full = block[tiles * rank:]
    turns = [full] + [pltpu.roll(full, LANES - at, 1) for at in range(rank, LANES, rank)]
    gram = jnp.concatenate(turns, axis=0)
    inverse, amplified = lower_inverse(gram)
    sound = amplified <= BROKEN
    amplified_ref[0, 0] = jnp.where(sound, amplified, BROKEN)

    def apply(inverse):
        left = jnp.concatenate(thirds(inverse), axis=0)
        for at in range(tiles):
            part = block[at * rank:(at + 1) * rank]
            coefficients_ref[:, at * LANES:(at + 1) * LANES] = product(left, thirds(part), 0)
        left = jnp.concatenate(thirds(inverse * scale), axis=0)
        chunk = math.gcd(CHUNK, rows_ref.shape[1])
        for at in range(0, rows_ref.shape[1], chunk):
            span = pl.ds(at, chunk)
            basis_ref[:, span] = product(left, thirds(rows_ref[:, span]), 0)

    apply(inverse)

    @pl.when(jnp.logical_not(sound))
    def _():
        row_at = lax.broadcasted_iota(jnp.int32, gram.shape, 0)
        lane_at = lax.broadcasted_iota(jnp.int32, gram.shape, 1)
        apply(lower_inverse(jnp.where(row_at == lane_at, gram * (1 + SHIFT), gram))[0])


def factor(parts, rows, scale, snaps):
    rank, cells = rows.shape
    return pl.pallas_call(
        lambda *refs: factor_kernel(scale, len(parts), *refs),
        in_specs=[VMEM] * (len(parts) + 1),
        out_specs=[VMEM] * 2 + [pl.BlockSpec(memory_space=pltpu.SMEM)],
        out_shape=[
            pltpu.HBM((rank, cells), jnp.float32),
            pltpu.HBM((rank, snaps), jnp.float32),
            jax.ShapeDtypeStruct((1, 1), jnp.float32),
        ],
        compiler_params=limit(16),
        name="factor",
    )(*parts, rows)


def exchange(block, axis, radix):
    count = lax.axis_size(axis)
    parts = [block]
    step = 1
    while step < count:
        block = tree_sum(parts)
        group = min(radix, count // step)
        parts = [swap(block, axis, step * at) for at in range(group - 1, 0, -1)]
        parts = [block] + parts
        step *= group
    return parts


def gram_kernel(scale, rows_ref, gram_ref):
    rank, cells = rows_ref.shape
    chunk = math.gcd(CHUNK, cells)
    gram = jnp.zeros((rank, rank), jnp.float32)
    for at in range(0, cells, chunk):
        split = thirds(rows_ref[:, pl.ds(at, chunk)])
        gram += product(jnp.concatenate(split, axis=0), split, 1)
    gram_ref[...] = packed(gram * scale)


def refine(rows, coefficients, total_cells):
    rank, snaps = coefficients.shape
    gram = pl.pallas_call(
        lambda *refs: gram_kernel(1 / total_cells, *refs),
        in_specs=[VMEM],
        out_specs=VMEM,
        out_shape=jax.ShapeDtypeStruct((rank * rank // LANES, LANES), jnp.float32),
        compiler_params=limit(16),
        name="gram",
    )(rows)
    gram = tree_sum(exchange(gram, "cells", 4))
    tiles = [coefficients[:, at:at + LANES] for at in range(0, snaps, LANES)]
    return factor([jnp.concatenate(tiles + [gram], axis=0)], rows, 1.0, snaps)


def shards(snapshots, sketch):
    total_cells = snapshots.shape[0] * lax.axis_size("cells")
    partial_rows, held = sketch_rows(snapshots, sketch)
    rows, block = project(exchange(partial_rows, "snaps", 2), held)
    first = factor(exchange(block, "cells", 4), rows, math.sqrt(total_cells), snapshots.shape[1])
    basis, coefficients, _, _ = lax.while_loop(
        lambda state: jnp.logical_and(state[2][0, 0] > AMPLIFIED, state[3] < PASSES),
        lambda state: (*refine(state[0], state[1], total_cells), state[3] + 1),
        (*first, jnp.int32(0)),
    )
    return (basis, coefficients)


def solution(mesh):
    return jax.shard_map(
        shards,
        mesh=mesh,
        in_specs=(P("cells", "snaps"), P("snaps", None)),
        out_specs=(P(None, "cells"), P(None, "snaps")),
        check_vma=False,
    )
```

```python
import math

import jax
import jax.numpy as jnp
from jax import lax
from jax.experimental import pallas as pl
from jax.experimental.pallas import tpu as pltpu
from jax.sharding import PartitionSpec as P

LANES = 128
CHUNK = 512
MIB = 1 << 20
AMPLIFIED = 512.0
BROKEN = 2e5
SHIFT = 3e-5
PASSES = 8
SENDS = 4
VMEM = pl.BlockSpec(memory_space=pltpu.VMEM)
HBM = pl.BlockSpec(memory_space=pltpu.HBM)


def limit(mebibytes):
    return pltpu.CompilerParams(vmem_limit_bytes=mebibytes * MIB)


def in_hbm(block):
    return pltpu.with_memory_space_constraint(block, pltpu.HBM)


def swap(block, axis, offset):
    count = lax.axis_size(axis)
    return lax.ppermute(block, axis, [(at, at ^ offset) for at in range(count)])


def tree_sum(parts):
    while len(parts) > 1:
        parts = [parts[at] + parts[at + 1] for at in range(0, len(parts), 2)]
    return parts[0]


def thirds(block):
    high = block.astype(jnp.bfloat16)
    rest = block - high.astype(jnp.float32)
    middle = rest.astype(jnp.bfloat16)
    low = (rest - middle.astype(jnp.float32)).astype(jnp.bfloat16)
    return high, middle, low


def product(left, right, right_dim):
    rank = left.shape[0] // 3
    dims = (((1,), (right_dim,)), ((), ()))
    high, middle, low = [
        lax.dot_general(left[:rank * (3 - at)], part, dims, preferred_element_type=jnp.float32)
        for at, part in enumerate(right)
    ]
    small = high[2 * rank:] + (middle[rank:] + low)
    return high[:rank] + ((high[rank:2 * rank] + middle[:rank]) + small)


def pieces(cells):
    if cells % 8:
        return [(0, cells)]
    return [(0, cells // 8), (cells // 8, cells // 8 * 3), (cells // 2, cells // 2)]


def sketch_kernel(sketch_ref, snapshots_ref, out_ref, held, sketch_held, arrived):
    fetches = pieces(held.shape[0])
    first = pltpu.make_async_copy(sketch_ref, sketch_held, arrived.at[len(fetches)])
    first.start()
    copies = []
    for at, (start, size) in enumerate(fetches):
        rows = pl.ds(start, size)
        copies.append(pltpu.make_async_copy(snapshots_ref.at[rows], held.at[rows], arrived.at[at]))
        copies[-1].start()
    first.wait()
    sketch = jnp.concatenate(thirds(sketch_held[...]), axis=0)
    for copy, (start, size) in zip(copies, fetches):
        copy.wait()
        chunk = min(CHUNK, size)
        for at in range(start, start + size, chunk):
            rows = pl.ds(at, chunk)
            out_ref[:, rows] = product(sketch, thirds(held[rows, :].T), 0)


def sketch_rows(snapshots, sketch):
    cells, snaps = snapshots.shape
    rank = sketch.shape[1]
    return pl.pallas_call(
        sketch_kernel,
        in_specs=[HBM] * 2,
        out_specs=[VMEM] * 2,
        out_shape=[
            pltpu.VMEM((rank, cells), jnp.float32),
            pltpu.VMEM((cells, snaps), jnp.float32),
        ],
        scratch_shapes=[
            pltpu.VMEM((rank, snaps), jnp.float32),
            pltpu.SemaphoreType.DMA((len(pieces(cells)) + 1,)),
        ],
        compiler_params=limit(16),
        name="sketch_rows",
    )(in_hbm(sketch.T), in_hbm(snapshots))


def packed(gram):
    rank = gram.shape[0]
    high = rank * rank // LANES
    return jnp.concatenate([gram[at:at + high] for at in range(0, rank, high)], axis=1)


def split_kernel(snapshots_ref, *refs):
    chunk = math.gcd(CHUNK, snapshots_ref.shape[0])
    for at in range(0, snapshots_ref.shape[0], chunk):
        span = pl.ds(at, chunk)
        for ref, part in zip(refs, thirds(snapshots_ref[span, :])):
            ref[span, :] = part


def split(snapshots):
    cells, snaps = snapshots.shape
    return pl.pallas_call(
        split_kernel,
        in_specs=[VMEM],
        out_specs=[VMEM] * 3,
        out_shape=[pltpu.VMEM((cells, snaps), jnp.bfloat16)] * 3,
        compiler_params=limit(16),
        cost_estimate=pl.CostEstimate(flops=8 * cells * snaps, bytes_accessed=10 * cells * snaps, transcendentals=0),
        name="split",
    )(snapshots)


def project_kernel(parts, *refs):
    thirds_refs = refs[parts:parts + 3]
    rows_ref, block_ref = refs[parts + 3:]
    rank, cells = rows_ref.shape
    snaps = thirds_refs[0].shape[1]
    chunk = min(CHUNK, cells)
    sums = jnp.zeros((rank, snaps), jnp.float32)
    gram = jnp.zeros((rank, rank), jnp.float32)
    for at in range(cells // chunk):
        span = pl.ds(at * chunk, chunk)
        rows = tree_sum([ref[:, span] for ref in refs[:parts]])
        rows_ref[:, span] = rows
        parts_of = thirds(rows)
        left = jnp.concatenate(parts_of, axis=0)
        sums += product(left, [ref[span, :] for ref in thirds_refs], 0)
        gram += product(left, parts_of, 1)
    tiles = snaps // LANES
    for at in range(tiles):
        block_ref[at * rank:(at + 1) * rank, :] = sums[:, at * LANES:(at + 1) * LANES]
    block_ref[tiles * rank:, :] = packed(gram)


def project(parts, snapshots):
    cells, snaps = snapshots[0].shape
    rank = parts[0].shape[0]
    return pl.pallas_call(
        lambda *refs: project_kernel(len(parts), *refs),
        in_specs=[VMEM] * (len(parts) + 3),
        out_specs=[VMEM] * 2,
        out_shape=[
            pltpu.VMEM((rank, cells), jnp.float32),
            pltpu.VMEM((rank * (snaps + rank) // LANES, LANES), jnp.float32),
        ],
        compiler_params=limit(16),
        name="project",
    )(*parts, *snapshots)


def spread(row):
    return jnp.broadcast_to(row, (8, row.shape[1]))


def tall(tile, rank):
    return jnp.concatenate([tile] * (rank // 8), axis=0)


def lower_inverse(gram):
    rank, lanes = gram.shape
    block = math.gcd(rank, 4)
    row_at = lax.broadcasted_iota(jnp.int32, (rank, lanes), 0)
    lane_at = lax.broadcasted_iota(jnp.int32, (rank, lanes), 1)
    both = jnp.where(lane_at < rank, gram, jnp.where(lane_at == row_at + rank, 1.0, 0.0))
    pivots = jnp.ones((rank, lanes), jnp.float32)
    diagonal = jnp.sum(jnp.where(row_at == lane_at, gram, 0.0), axis=0, keepdims=True)
    columns = [jnp.broadcast_to(both[:, at:at + 1], (rank, lanes)) for at in range(block)]
    for base in range(0, rank, block):
        later = range(base + block, min(base + 2 * block, rank))
        upcoming = [jnp.broadcast_to(both[:, at:at + 1], (rank, lanes)) for at in later]
        corner = [[spread(columns[at][base + to:base + to + 1]) for at in range(block)] for to in range(block)]
        rows = [spread(both[base + at:base + at + 1]) for at in range(block)]
        for at in range(block):
            pivot = corner[at][at]
            inverse = 1.0 / pivot
            for to in range(at + 1, block):
                ratio = corner[to][at] * inverse
                rows[to] = rows[to] - ratio * rows[at]
                columns[to] = columns[to] - tall(ratio, rank) * columns[at]
                for along in range(at + 1, block):
                    corner[to][along] = corner[to][along] - ratio * corner[at][along]
            factor = jnp.where(row_at > base + at, columns[at] * tall(inverse, rank), 0.0)
            both = both - factor * tall(rows[at], rank)
            for to, place in enumerate(later):
                upcoming[to] = upcoming[to] - factor * tall(spread(columns[at][place:place + 1]), rank)
            pivots = jnp.where(row_at == base + at, tall(pivot, rank), pivots)
        columns = upcoming
    inverse = (both * lax.rsqrt(pivots))[:, rank:2 * rank]
    return inverse, jnp.sum(inverse * inverse * diagonal[:, :rank])


def factor_kernel(scale, parts, *refs):
    rows_ref, basis_ref, coefficients_ref, amplified_ref, made_ref, sent = refs[parts:]
    snaps = coefficients_ref.shape[1]
    block = tree_sum([ref[...] for ref in refs[:parts]])
    rank = rows_ref.shape[0]
    tiles = snaps // LANES
    full = block[tiles * rank:]
    turns = [full] + [pltpu.roll(full, LANES - at, 1) for at in range(rank, LANES, rank)]
    gram = jnp.concatenate(turns, axis=0)
    inverse, amplified = lower_inverse(gram)
    sound = amplified <= BROKEN
    amplified_ref[0, 0] = jnp.where(sound, amplified, BROKEN)

    def apply(inverse):
        left = jnp.concatenate(thirds(inverse), axis=0)
        for at in range(tiles):
            part = block[at * rank:(at + 1) * rank]
            coefficients_ref[:, at * LANES:(at + 1) * LANES] = product(left, thirds(part), 0)
        left = jnp.concatenate(thirds(inverse * scale), axis=0)
        wide = rows_ref.shape[1] // SENDS
        chunk = math.gcd(CHUNK, wide)
        copies = []
        for start in range(0, rows_ref.shape[1], wide):
            for at in range(start, start + wide, chunk):
                span = pl.ds(at, chunk)
                made_ref[:, span] = product(left, thirds(rows_ref[:, span]), 0)
            span = pl.ds(start, wide)
            copies.append(pltpu.make_async_copy(made_ref.at[:, span], basis_ref.at[:, span], sent.at[start // wide]))
            copies[-1].start()
        for copy in copies:
            copy.wait()

    apply(inverse)

    @pl.when(jnp.logical_not(sound))
    def _():
        row_at = lax.broadcasted_iota(jnp.int32, gram.shape, 0)
        lane_at = lax.broadcasted_iota(jnp.int32, gram.shape, 1)
        apply(lower_inverse(jnp.where(row_at == lane_at, gram * (1 + SHIFT), gram))[0])


def factor(parts, rows, scale, snaps):
    rank, cells = rows.shape
    return pl.pallas_call(
        lambda *refs: factor_kernel(scale, len(parts), *refs),
        in_specs=[VMEM] * (len(parts) + 1),
        out_specs=[HBM, VMEM, pl.BlockSpec(memory_space=pltpu.SMEM)],
        out_shape=[
            pltpu.HBM((rank, cells), jnp.float32),
            pltpu.HBM((rank, snaps), jnp.float32),
            pltpu.SMEM((1, 1), jnp.float32),
        ],
        scratch_shapes=[pltpu.VMEM((rank, cells), jnp.float32), pltpu.SemaphoreType.DMA((SENDS,))],
        compiler_params=limit(16),
        name="factor",
    )(*parts, rows)


def exchange(block, axis, radix):
    count = lax.axis_size(axis)
    parts = [block]
    step = 1
    while step < count:
        block = tree_sum(parts)
        group = min(radix, count // step)
        parts = [swap(block, axis, step * at) for at in range(group - 1, 0, -1)]
        parts = [block] + parts
        step *= group
    return parts


def gram_kernel(scale, rows_ref, gram_ref):
    rank, cells = rows_ref.shape
    chunk = math.gcd(CHUNK, cells)
    gram = jnp.zeros((rank, rank), jnp.float32)
    for at in range(0, cells, chunk):
        split = thirds(rows_ref[:, pl.ds(at, chunk)])
        gram += product(jnp.concatenate(split, axis=0), split, 1)
    gram_ref[...] = packed(gram * scale)


def refine(rows, coefficients, total_cells):
    rank, snaps = coefficients.shape
    gram = pl.pallas_call(
        lambda *refs: gram_kernel(1 / total_cells, *refs),
        in_specs=[VMEM],
        out_specs=VMEM,
        out_shape=jax.ShapeDtypeStruct((rank * rank // LANES, LANES), jnp.float32),
        compiler_params=limit(16),
        name="gram",
    )(rows)
    gram = tree_sum(exchange(gram, "cells", 4))
    tiles = [coefficients[:, at:at + LANES] for at in range(0, snaps, LANES)]
    return factor([jnp.concatenate(tiles + [gram], axis=0)], rows, 1.0, snaps)


def shards(snapshots, sketch):
    total_cells = snapshots.shape[0] * lax.axis_size("cells")
    partial_rows, held = sketch_rows(snapshots, sketch)
    rows, block = project(exchange(partial_rows, "snaps", 2), split(held))
    first = factor(exchange(block, "cells", 4), rows, math.sqrt(total_cells), snapshots.shape[1])
    basis, coefficients, _, _ = lax.while_loop(
        lambda state: jnp.logical_and(state[2][0, 0] > AMPLIFIED, state[3] < PASSES),
        lambda state: (*refine(state[0], state[1], total_cells), state[3] + 1),
        (*first, jnp.int32(0)),
    )
    return (basis, coefficients)


def solution(mesh):
    return jax.shard_map(
        shards,
        mesh=mesh,
        in_specs=(P("cells", "snaps"), P("snaps", None)),
        out_specs=(P(None, "cells"), P(None, "snaps")),
        check_vma=False,
    )
```

```python
import math

import jax
import jax.numpy as jnp
from jax import lax
from jax.experimental import pallas as pl
from jax.experimental.pallas import tpu as pltpu
from jax.sharding import PartitionSpec as P

LANES = 128
CHUNK = 256
MIB = 1 << 20
AMPLIFIED = 512.0
BROKEN = 2e5
SHIFT = 3e-5
PASSES = 8
VMEM = pl.BlockSpec(memory_space=pltpu.VMEM)
HBM = pl.BlockSpec(memory_space=pltpu.HBM)


def limit(mebibytes):
    return pltpu.CompilerParams(vmem_limit_bytes=mebibytes * MIB)


def in_hbm(block):
    return pltpu.with_memory_space_constraint(block, pltpu.HBM)


def swap(block, axis, offset):
    count = lax.axis_size(axis)
    return lax.ppermute(block, axis, [(at, at ^ offset) for at in range(count)])


def tree_sum(parts):
    while len(parts) > 1:
        parts = [parts[at] + parts[at + 1] for at in range(0, len(parts), 2)]
    return parts[0]


def thirds(block):
    high = block.astype(jnp.bfloat16)
    rest = block - high.astype(jnp.float32)
    middle = rest.astype(jnp.bfloat16)
    low = (rest - middle.astype(jnp.float32)).astype(jnp.bfloat16)
    return high, middle, low


def product(left, right, right_dim):
    rank = left.shape[0] // 3
    dims = (((1,), (right_dim,)), ((), ()))
    high, middle, low = [
        lax.dot_general(left[:rank * (3 - at)], part, dims, preferred_element_type=jnp.float32)
        for at, part in enumerate(right)
    ]
    small = high[2 * rank:] + (middle[rank:] + low)
    return high[:rank] + ((high[rank:2 * rank] + middle[:rank]) + small)


def pieces(cells):
    if cells % 8:
        return [(0, cells)]
    return [(0, cells // 8), (cells // 8, cells // 8 * 3), (cells // 2, cells // 2)]


def sketch_kernel(sketch_ref, snapshots_ref, out_ref, held, sketch_held, arrived):
    fetches = pieces(held.shape[0])
    first = pltpu.make_async_copy(sketch_ref, sketch_held, arrived.at[len(fetches)])
    first.start()
    copies = []
    for at, (start, size) in enumerate(fetches):
        rows = pl.ds(start, size)
        copies.append(pltpu.make_async_copy(snapshots_ref.at[rows], held.at[rows], arrived.at[at]))
        copies[-1].start()
    first.wait()
    sketch = jnp.concatenate(thirds(sketch_held[...]), axis=0)
    for copy, (start, size) in zip(copies, fetches):
        copy.wait()
        chunk = min(CHUNK, size)
        for at in range(start, start + size, chunk):
            rows = pl.ds(at, chunk)
            out_ref[:, rows] = product(sketch, thirds(held[rows, :].T), 0)


def sketch_rows(snapshots, sketch):
    cells, snaps = snapshots.shape
    rank = sketch.shape[1]
    return pl.pallas_call(
        sketch_kernel,
        in_specs=[HBM] * 2,
        out_specs=[VMEM] * 2,
        out_shape=[
            pltpu.VMEM((rank, cells), jnp.float32),
            pltpu.VMEM((cells, snaps), jnp.float32),
        ],
        scratch_shapes=[
            pltpu.VMEM((rank, snaps), jnp.float32),
            pltpu.SemaphoreType.DMA((len(pieces(cells)) + 1,)),
        ],
        compiler_params=limit(16),
        name="sketch_rows",
    )(in_hbm(sketch.T), in_hbm(snapshots))


def packed(gram):
    rank = gram.shape[0]
    high = rank * rank // LANES
    return jnp.concatenate([gram[at:at + high] for at in range(0, rank, high)], axis=1)


def split_kernel(snapshots_ref, *refs):
    chunk = math.gcd(CHUNK, snapshots_ref.shape[0])
    for at in range(0, snapshots_ref.shape[0], chunk):
        span = pl.ds(at, chunk)
        for ref, part in zip(refs, thirds(snapshots_ref[span, :])):
            ref[span, :] = part


def split(snapshots):
    cells, snaps = snapshots.shape
    return pl.pallas_call(
        split_kernel,
        in_specs=[VMEM],
        out_specs=[VMEM] * 3,
        out_shape=[pltpu.VMEM((cells, snaps), jnp.bfloat16)] * 3,
        compiler_params=limit(16),
        cost_estimate=pl.CostEstimate(flops=8 * cells * snaps, bytes_accessed=10 * cells * snaps, transcendentals=0),
        name="split",
    )(snapshots)


def project_kernel(parts, *refs):
    thirds_refs = refs[parts:parts + 3]
    rows_ref, block_ref = refs[parts + 3:]
    rank, cells = rows_ref.shape
    snaps = thirds_refs[0].shape[1]
    chunk = min(CHUNK, cells)
    sums = jnp.zeros((rank, snaps), jnp.float32)
    gram = jnp.zeros((rank, rank), jnp.float32)
    for at in range(cells // chunk):
        span = pl.ds(at * chunk, chunk)
        rows = tree_sum([ref[:, span] for ref in refs[:parts]])
        rows_ref[:, span] = rows
        parts_of = thirds(rows)
        left = jnp.concatenate(parts_of, axis=0)
        sums += product(left, [ref[span, :] for ref in thirds_refs], 0)
        gram += product(left, parts_of, 1)
    tiles = snaps // LANES
    for at in range(tiles):
        block_ref[at * rank:(at + 1) * rank, :] = sums[:, at * LANES:(at + 1) * LANES]
    block_ref[tiles * rank:, :] = packed(gram)


def project(parts, snapshots):
    cells, snaps = snapshots[0].shape
    rank = parts[0].shape[0]
    return pl.pallas_call(
        lambda *refs: project_kernel(len(parts), *refs),
        in_specs=[VMEM] * (len(parts) + 3),
        out_specs=[VMEM] * 2,
        out_shape=[
            pltpu.VMEM((rank, cells), jnp.float32),
            pltpu.VMEM((rank * (snaps + rank) // LANES, LANES), jnp.float32),
        ],
        compiler_params=limit(16),
        name="project",
    )(*parts, *snapshots)


def spread(row):
    return jnp.broadcast_to(row, (8, row.shape[1]))


def tall(tile, rank):
    return jnp.concatenate([tile] * (rank // 8), axis=0)


def lower_inverse(gram):
    rank, lanes = gram.shape
    block = math.gcd(rank, 4)
    row_at = lax.broadcasted_iota(jnp.int32, (rank, lanes), 0)
    lane_at = lax.broadcasted_iota(jnp.int32, (rank, lanes), 1)
    both = jnp.where(lane_at < rank, gram, jnp.where(lane_at == row_at + rank, 1.0, 0.0))
    pivots = jnp.ones((rank, lanes), jnp.float32)
    diagonal = jnp.sum(jnp.where(row_at == lane_at, gram, 0.0), axis=0, keepdims=True)
    columns = [jnp.broadcast_to(both[:, at:at + 1], (rank, lanes)) for at in range(block)]
    for base in range(0, rank, block):
        later = range(base + block, min(base + 2 * block, rank))
        upcoming = [jnp.broadcast_to(both[:, at:at + 1], (rank, lanes)) for at in later]
        corner = [[spread(columns[at][base + to:base + to + 1]) for at in range(block)] for to in range(block)]
        rows = [spread(both[base + at:base + at + 1]) for at in range(block)]
        for at in range(block):
            pivot = corner[at][at]
            inverse = 1.0 / pivot
            for to in range(at + 1, block):
                ratio = corner[to][at] * inverse
                rows[to] = rows[to] - ratio * rows[at]
                columns[to] = columns[to] - tall(ratio, rank) * columns[at]
                for along in range(at + 1, block):
                    corner[to][along] = corner[to][along] - ratio * corner[at][along]
            factor = jnp.where(row_at > base + at, columns[at] * tall(inverse, rank), 0.0)
            both = both - factor * tall(rows[at], rank)
            for to, place in enumerate(later):
                upcoming[to] = upcoming[to] - factor * tall(spread(columns[at][place:place + 1]), rank)
            pivots = jnp.where(row_at == base + at, tall(pivot, rank), pivots)
        columns = upcoming
    inverse = (both * lax.rsqrt(pivots))[:, rank:2 * rank]
    return inverse, jnp.sum(inverse * inverse * diagonal[:, :rank])


def factor_kernel(scale, parts, *refs):
    rows_ref, basis_ref, coefficients_ref, amplified_ref = refs[parts:]
    snaps = coefficients_ref.shape[1]
    block = tree_sum([ref[...] for ref in refs[:parts]])
    rank = rows_ref.shape[0]
    tiles = snaps // LANES
    full = block[tiles * rank:]
    turns = [full] + [pltpu.roll(full, LANES - at, 1) for at in range(rank, LANES, rank)]
    gram = jnp.concatenate(turns, axis=0)
    inverse, amplified = lower_inverse(gram)
    sound = amplified <= BROKEN
    amplified_ref[0, 0] = jnp.where(sound, amplified, BROKEN)

    def apply(inverse):
        left = jnp.concatenate(thirds(inverse), axis=0)
        for at in range(tiles):
            part = block[at * rank:(at + 1) * rank]
            coefficients_ref[:, at * LANES:(at + 1) * LANES] = product(left, thirds(part), 0)
        left = jnp.concatenate(thirds(inverse * scale), axis=0)
        chunk = math.gcd(CHUNK, rows_ref.shape[1])
        for at in range(0, rows_ref.shape[1], chunk):
            span = pl.ds(at, chunk)
            basis_ref[:, span] = product(left, thirds(rows_ref[:, span]), 0)

    apply(inverse)

    @pl.when(jnp.logical_not(sound))
    def _():
        row_at = lax.broadcasted_iota(jnp.int32, gram.shape, 0)
        lane_at = lax.broadcasted_iota(jnp.int32, gram.shape, 1)
        apply(lower_inverse(jnp.where(row_at == lane_at, gram * (1 + SHIFT), gram))[0])


def factor(parts, rows, scale, snaps):
    rank, cells = rows.shape
    return pl.pallas_call(
        lambda *refs: factor_kernel(scale, len(parts), *refs),
        in_specs=[VMEM] * (len(parts) + 1),
        out_specs=[VMEM] * 2 + [pl.BlockSpec(memory_space=pltpu.SMEM)],
        out_shape=[
            pltpu.HBM((rank, cells), jnp.float32),
            pltpu.HBM((rank, snaps), jnp.float32),
            pltpu.SMEM((1, 1), jnp.float32),
        ],
        compiler_params=limit(16),
        name="factor",
    )(*parts, rows)


def exchange(block, axis, radix):
    count = lax.axis_size(axis)
    steps = []
    step = 1
    while step < count:
        steps.append((step, min(radix, count // step)))
        step *= steps[-1][1]
    parts = [block]
    for step, group in steps[::-1]:
        block = tree_sum(parts)
        parts = [block] + [swap(block, axis, step * at) for at in range(group - 1, 0, -1)]
    return parts


def gram_kernel(scale, rows_ref, gram_ref):
    rank, cells = rows_ref.shape
    chunk = math.gcd(CHUNK, cells)
    gram = jnp.zeros((rank, rank), jnp.float32)
    for at in range(0, cells, chunk):
        split = thirds(rows_ref[:, pl.ds(at, chunk)])
        gram += product(jnp.concatenate(split, axis=0), split, 1)
    gram_ref[...] = packed(gram * scale)


def refine(rows, coefficients, total_cells):
    rank, snaps = coefficients.shape
    gram = pl.pallas_call(
        lambda *refs: gram_kernel(1 / total_cells, *refs),
        in_specs=[VMEM],
        out_specs=VMEM,
        out_shape=jax.ShapeDtypeStruct((rank * rank // LANES, LANES), jnp.float32),
        compiler_params=limit(16),
        name="gram",
    )(rows)
    gram = tree_sum(exchange(gram, "cells", 4))
    tiles = [coefficients[:, at:at + LANES] for at in range(0, snaps, LANES)]
    return factor([jnp.concatenate(tiles + [gram], axis=0)], rows, 1.0, snaps)


def shards(snapshots, sketch):
    total_cells = snapshots.shape[0] * lax.axis_size("cells")
    partial_rows, held = sketch_rows(snapshots, sketch)
    rows, block = project(exchange(partial_rows, "snaps", 2), split(held))
    first = factor(exchange(block, "cells", 4), rows, math.sqrt(total_cells), snapshots.shape[1])
    basis, coefficients, _, _ = lax.while_loop(
        lambda state: jnp.logical_and(state[2][0, 0] > AMPLIFIED, state[3] < PASSES),
        lambda state: (*refine(state[0], state[1], total_cells), state[3] + 1),
        (*first, jnp.int32(0)),
    )
    return (basis, coefficients)


def solution(mesh):
    return jax.shard_map(
        shards,
        mesh=mesh,
        in_specs=(P("cells", "snaps"), P("snaps", None)),
        out_specs=(P(None, "cells"), P(None, "snaps")),
        check_vma=False,
    )
```

```python
import math

import jax
import jax.numpy as jnp
from jax import lax
from jax.experimental import pallas as pl
from jax.experimental.pallas import tpu as pltpu
from jax.sharding import PartitionSpec as P

LANES = 128
CHUNK = 256
MIB = 1 << 20
AMPLIFIED = 512.0
BROKEN = 2e5
SHIFT = 3e-5
PASSES = 8
VMEM = pl.BlockSpec(memory_space=pltpu.VMEM)
HBM = pl.BlockSpec(memory_space=pltpu.HBM)


def limit(mebibytes):
    return pltpu.CompilerParams(vmem_limit_bytes=mebibytes * MIB)


def in_hbm(block):
    return pltpu.with_memory_space_constraint(block, pltpu.HBM)


def swap(block, axis, offset):
    count = lax.axis_size(axis)
    return lax.ppermute(block, axis, [(at, at ^ offset) for at in range(count)])


def tree_sum(parts):
    while len(parts) > 1:
        parts = [parts[at] + parts[at + 1] for at in range(0, len(parts), 2)]
    return parts[0]


def thirds(block):
    high, middle = halves(block)
    rest = block - high.astype(jnp.float32)
    low = (rest - middle.astype(jnp.float32)).astype(jnp.bfloat16)
    return high, middle, low


def halves(block):
    high = block.astype(jnp.bfloat16)
    return high, (block - high.astype(jnp.float32)).astype(jnp.bfloat16)


def product(left, right, right_dim):
    rank = left.shape[0] // 3
    dims = (((1,), (right_dim,)), ((), ()))
    high, middle, low = [
        lax.dot_general(left[:rank * (3 - at)], part, dims, preferred_element_type=jnp.float32)
        for at, part in enumerate(right)
    ]
    small = high[2 * rank:] + (middle[rank:] + low)
    return high[:rank] + ((high[rank:2 * rank] + middle[:rank]) + small)


def pieces(cells):
    if cells % 8:
        return [(0, cells)]
    size = cells // 8
    return [(0, size), (size, 3 * size), (4 * size, 3 * size), (7 * size, size)]


def sketch_kernel(sketch_ref, snapshots_ref, out_ref, held, sketch_held, arrived):
    fetches = pieces(held.shape[0])
    first = pltpu.make_async_copy(sketch_ref, sketch_held, arrived.at[len(fetches)])
    first.start()
    copies = []
    for at, (start, size) in enumerate(fetches):
        rows = pl.ds(start, size)
        copies.append(pltpu.make_async_copy(snapshots_ref.at[rows], held.at[rows], arrived.at[at]))
        copies[-1].start()
    first.wait()
    sketch = jnp.concatenate(thirds(sketch_held[...]), axis=0)
    for copy, (start, size) in zip(copies, fetches):
        copy.wait()
        chunk = min(CHUNK, size)
        for at in range(start, start + size, chunk):
            rows = pl.ds(at, chunk)
            out_ref[:, rows] = product(sketch, thirds(held[rows, :].T), 0)


def sketch_rows(snapshots, sketch):
    cells, snaps = snapshots.shape
    rank = sketch.shape[1]
    return pl.pallas_call(
        sketch_kernel,
        in_specs=[HBM] * 2,
        out_specs=[VMEM] * 2,
        out_shape=[
            pltpu.VMEM((rank, cells), jnp.float32),
            pltpu.VMEM((cells, snaps), jnp.float32),
        ],
        scratch_shapes=[
            pltpu.VMEM((rank, snaps), jnp.float32),
            pltpu.SemaphoreType.DMA((len(pieces(cells)) + 1,)),
        ],
        compiler_params=limit(16),
        name="sketch_rows",
    )(in_hbm(sketch.T), in_hbm(snapshots))


def packed(gram):
    rank = gram.shape[0]
    high = rank * rank // LANES
    return jnp.concatenate([gram[at:at + high] for at in range(0, rank, high)], axis=1)


def split_kernel(snapshots_ref, *refs):
    chunk = math.gcd(CHUNK, snapshots_ref.shape[0])
    for at in range(0, snapshots_ref.shape[0], chunk):
        span = pl.ds(at, chunk)
        for ref, part in zip(refs, halves(snapshots_ref[span, :])):
            ref[span, :] = part


def split(snapshots):
    cells, snaps = snapshots.shape
    return pl.pallas_call(
        split_kernel,
        in_specs=[VMEM],
        out_specs=[VMEM] * 2,
        out_shape=[pltpu.VMEM((cells, snaps), jnp.bfloat16)] * 2,
        compiler_params=limit(16),
        cost_estimate=pl.CostEstimate(flops=4 * cells * snaps, bytes_accessed=8 * cells * snaps, transcendentals=0),
        name="split",
    )(snapshots)


def project_kernel(parts, *refs):
    snapshots_refs = refs[parts:-2]
    rows_ref, block_ref = refs[-2:]
    rank, cells = rows_ref.shape
    snaps = snapshots_refs[0].shape[1]
    chunk = math.gcd(CHUNK, cells)
    sums = jnp.zeros((2 * rank, snaps), jnp.float32)
    gram = jnp.zeros((rank, rank), jnp.float32)
    for at in range(0, cells, chunk):
        span = pl.ds(at, chunk)
        rows = tree_sum([ref[:, span] for ref in refs[:parts]])
        rows_ref[:, span] = rows
        exact = thirds(rows)
        left = jnp.concatenate(exact, axis=0)
        right = [ref[span, :] for ref in snapshots_refs]
        for part in right if len(right) == 2 else halves(right[0]):
            sums += jnp.dot(left[:2 * rank], part, preferred_element_type=jnp.float32)
        gram += product(left, exact, 1)
    sums = sums[:rank] + sums[rank:]
    tiles = snaps // LANES
    for at in range(tiles):
        block_ref[at * rank:(at + 1) * rank, :] = sums[:, at * LANES:(at + 1) * LANES]
    block_ref[tiles * rank:, :] = packed(gram)


def project(parts, snapshots):
    cells, snaps = snapshots[0].shape
    rank = parts[0].shape[0]
    return pl.pallas_call(
        lambda *refs: project_kernel(len(parts), *refs),
        in_specs=[VMEM] * (len(parts) + len(snapshots)),
        out_specs=[VMEM] * 2,
        out_shape=[
            pltpu.VMEM((rank, cells), jnp.float32),
            pltpu.VMEM((rank * (snaps + rank) // LANES, LANES), jnp.float32),
        ],
        compiler_params=limit(16),
        name="project",
    )(*parts, *snapshots)


def spread(row):
    return jnp.broadcast_to(row, (8, row.shape[1]))


def tall(tile, rank):
    return jnp.concatenate([tile] * (rank // 8), axis=0)


def lower_inverse(gram):
    rank, lanes = gram.shape
    block = math.gcd(rank, 4)
    row_at = lax.broadcasted_iota(jnp.int32, (rank, lanes), 0)
    lane_at = lax.broadcasted_iota(jnp.int32, (rank, lanes), 1)
    both = jnp.where(lane_at < rank, gram, jnp.where(lane_at == row_at + rank, 1.0, 0.0))
    pivots = jnp.ones((rank, lanes), jnp.float32)
    diagonal = jnp.sum(jnp.where(row_at == lane_at, gram, 0.0), axis=0, keepdims=True)
    columns = [jnp.broadcast_to(both[:, at:at + 1], (rank, lanes)) for at in range(block)]
    for base in range(0, rank, block):
        later = range(base + block, min(base + 2 * block, rank))
        upcoming = [jnp.broadcast_to(both[:, at:at + 1], (rank, lanes)) for at in later]
        corner = [[spread(columns[at][base + to:base + to + 1]) for at in range(block)] for to in range(block)]
        rows = [spread(both[base + at:base + at + 1]) for at in range(block)]
        for at in range(block):
            pivot = corner[at][at]
            inverse = 1.0 / pivot
            for to in range(at + 1, block):
                ratio = corner[to][at] * inverse
                rows[to] = rows[to] - ratio * rows[at]
                columns[to] = columns[to] - tall(ratio, rank) * columns[at]
                for along in range(at + 1, block):
                    corner[to][along] = corner[to][along] - ratio * corner[at][along]
            factor = jnp.where(row_at > base + at, columns[at] * tall(inverse, rank), 0.0)
            both = both - factor * tall(rows[at], rank)
            for to, place in enumerate(later):
                upcoming[to] = upcoming[to] - factor * tall(spread(columns[at][place:place + 1]), rank)
            pivots = jnp.where(row_at == base + at, tall(pivot, rank), pivots)
        columns = upcoming
    inverse = (both * lax.rsqrt(pivots))[:, rank:2 * rank]
    return inverse, jnp.sum(inverse * inverse * diagonal[:, :rank])


def factor_kernel(scale, parts, *refs):
    rows_ref, basis_ref, coefficients_ref, amplified_ref = refs[parts:]
    snaps = coefficients_ref.shape[1]
    block = tree_sum([ref[...] for ref in refs[:parts]])
    rank = rows_ref.shape[0]
    tiles = snaps // LANES
    full = block[tiles * rank:]
    turns = [full] + [pltpu.roll(full, LANES - at, 1) for at in range(rank, LANES, rank)]
    gram = jnp.concatenate(turns, axis=0)
    inverse, amplified = lower_inverse(gram)
    sound = amplified <= BROKEN
    amplified_ref[0, 0] = jnp.where(sound, amplified, BROKEN)

    def apply(inverse):
        left = jnp.concatenate(thirds(inverse), axis=0)
        for at in range(tiles):
            part = block[at * rank:(at + 1) * rank]
            coefficients_ref[:, at * LANES:(at + 1) * LANES] = product(left, thirds(part), 0)
        left = jnp.concatenate(thirds(inverse * scale), axis=0)
        chunk = math.gcd(CHUNK, rows_ref.shape[1])
        for at in range(0, rows_ref.shape[1], chunk):
            span = pl.ds(at, chunk)
            basis_ref[:, span] = product(left, thirds(rows_ref[:, span]), 0)

    apply(inverse)

    @pl.when(jnp.logical_not(sound))
    def _():
        row_at = lax.broadcasted_iota(jnp.int32, gram.shape, 0)
        lane_at = lax.broadcasted_iota(jnp.int32, gram.shape, 1)
        apply(lower_inverse(jnp.where(row_at == lane_at, gram * (1 + SHIFT), gram))[0])


def factor(parts, rows, scale, snaps):
    rank, cells = rows.shape
    return pl.pallas_call(
        lambda *refs: factor_kernel(scale, len(parts), *refs),
        in_specs=[VMEM] * (len(parts) + 1),
        out_specs=[VMEM] * 2 + [pl.BlockSpec(memory_space=pltpu.SMEM)],
        out_shape=[
            pltpu.HBM((rank, cells), jnp.float32),
            pltpu.HBM((rank, snaps), jnp.float32),
            pltpu.SMEM((1, 1), jnp.float32),
        ],
        compiler_params=limit(16),
        name="factor",
    )(*parts, rows)


def exchange(block, axis, radix):
    count = lax.axis_size(axis)
    steps = []
    step = 1
    while step < count:
        steps.append((step, min(radix, count // step)))
        step *= steps[-1][1]
    parts = [block]
    for step, group in steps[::-1]:
        block = tree_sum(parts)
        parts = [block] + [swap(block, axis, step * at) for at in range(group - 1, 0, -1)]
    return parts


def shards(snapshots, sketch):
    scale = math.sqrt(snapshots.shape[0] * lax.axis_size("cells"))

    def orthogonalize(parts, snapshots):
        rows, block = project(parts, snapshots)
        return factor(exchange(block, "cells", 4), rows, scale, snapshots[0].shape[1])

    partial_rows, held = sketch_rows(snapshots, sketch)
    first = orthogonalize(exchange(partial_rows, "snaps", 2), split(held))
    basis, coefficients, _, _ = lax.while_loop(
        lambda state: jnp.logical_and(state[2][0, 0] > AMPLIFIED, state[3] < PASSES),
        lambda state: (*orthogonalize([state[0]], [in_hbm(snapshots)]), state[3] + 1),
        (*first, jnp.int32(0)),
    )
    return (basis, coefficients)


def solution(mesh):
    return jax.shard_map(
        shards,
        mesh=mesh,
        in_specs=(P("cells", "snaps"), P("snaps", None)),
        out_specs=(P(None, "cells"), P(None, "snaps")),
        check_vma=False,
    )
```

```python
import math

import jax
import jax.numpy as jnp
from jax import lax
from jax.experimental import pallas as pl
from jax.experimental.pallas import tpu as pltpu
from jax.sharding import PartitionSpec as P

LANES = 128
CHUNK = 256
MIB = 1 << 20
AMPLIFIED = 512.0
BROKEN = 2e5
SHIFT = 3e-5
PASSES = 8
VMEM = pl.BlockSpec(memory_space=pltpu.VMEM)
HBM = pl.BlockSpec(memory_space=pltpu.HBM)


def limit(mebibytes):
    return pltpu.CompilerParams(vmem_limit_bytes=mebibytes * MIB)


def in_hbm(block):
    return pltpu.with_memory_space_constraint(block, pltpu.HBM)


def swap(block, axis, offset):
    count = lax.axis_size(axis)
    return lax.ppermute(block, axis, [(at, at ^ offset) for at in range(count)])


def tree_sum(parts):
    while len(parts) > 1:
        parts = [parts[at] + parts[at + 1] for at in range(0, len(parts), 2)]
    return parts[0]


def thirds(block):
    high, middle = halves(block)
    rest = block - high.astype(jnp.float32)
    low = (rest - middle.astype(jnp.float32)).astype(jnp.bfloat16)
    return high, middle, low


def halves(block):
    high = block.astype(jnp.bfloat16)
    return high, (block - high.astype(jnp.float32)).astype(jnp.bfloat16)


def product(left, right, right_dim):
    rank = left.shape[0] // 3
    dims = (((1,), (right_dim,)), ((), ()))
    high, middle, low = [
        lax.dot_general(left[:rank * (3 - at)], part, dims, preferred_element_type=jnp.float32)
        for at, part in enumerate(right)
    ]
    small = high[2 * rank:] + (middle[rank:] + low)
    return high[:rank] + ((high[rank:2 * rank] + middle[:rank]) + small)


def pieces(cells):
    if cells % 8:
        return [(0, cells)]
    return [(0, cells // 4), (cells // 4, cells // 4), (cells // 2, cells // 2)]


def sketch_kernel(sketch_ref, snapshots_ref, out_ref, held, sketch_held, arrived):
    fetches = pieces(held.shape[0])
    first = pltpu.make_async_copy(sketch_ref, sketch_held, arrived.at[len(fetches)])
    first.start()
    copies = []
    for at, (start, size) in enumerate(fetches):
        rows = pl.ds(start, size)
        copies.append(pltpu.make_async_copy(snapshots_ref.at[rows], held.at[rows], arrived.at[at]))
        copies[-1].start()
    first.wait()
    sketch = jnp.concatenate(thirds(sketch_held[...]), axis=0)
    for copy, (start, size) in zip(copies, fetches):
        copy.wait()
        chunk = math.gcd(CHUNK, size)
        for at in range(start, start + size, chunk):
            rows = pl.ds(at, chunk)
            if at // chunk % 2:
                out_ref[:, rows] = product(sketch, thirds(held[rows, :]), 1)
            else:
                out_ref[:, rows] = product(sketch, thirds(held[rows, :].T), 0)


def sketch_rows(snapshots, sketch):
    cells, snaps = snapshots.shape
    rank = sketch.shape[1]
    return pl.pallas_call(
        sketch_kernel,
        in_specs=[HBM] * 2,
        out_specs=[VMEM] * 2,
        out_shape=[
            pltpu.VMEM((rank, cells), jnp.float32),
            pltpu.VMEM((cells, snaps), jnp.float32),
        ],
        scratch_shapes=[
            pltpu.VMEM((rank, snaps), jnp.float32),
            pltpu.SemaphoreType.DMA((len(pieces(cells)) + 1,)),
        ],
        compiler_params=limit(16),
        name="sketch_rows",
    )(in_hbm(sketch.T), in_hbm(snapshots))


def packed(gram):
    rank = gram.shape[0]
    high = rank * rank // LANES
    return jnp.concatenate([gram[at:at + high] for at in range(0, rank, high)], axis=1)


def split_kernel(snapshots_ref, *refs):
    chunk = math.gcd(CHUNK, snapshots_ref.shape[0])
    for at in range(0, snapshots_ref.shape[0], chunk):
        span = pl.ds(at, chunk)
        for ref, part in zip(refs, halves(snapshots_ref[span, :])):
            ref[span, :] = part


def split(snapshots):
    cells, snaps = snapshots.shape
    return pl.pallas_call(
        split_kernel,
        in_specs=[VMEM],
        out_specs=[VMEM] * 2,
        out_shape=[pltpu.VMEM((cells, snaps), jnp.bfloat16)] * 2,
        compiler_params=limit(16),
        cost_estimate=pl.CostEstimate(flops=4 * cells * snaps, bytes_accessed=8 * cells * snaps, transcendentals=0),
        name="split",
    )(snapshots)


def project_kernel(parts, *refs):
    snapshots_refs = refs[parts:-2]
    rows_ref, block_ref = refs[-2:]
    rank, cells = rows_ref.shape
    snaps = snapshots_refs[0].shape[1]
    chunk = math.gcd(CHUNK, cells)
    sums = jnp.zeros((2 * rank, snaps), jnp.float32)
    gram = jnp.zeros((rank, rank), jnp.float32)
    for at in range(0, cells, chunk):
        span = pl.ds(at, chunk)
        rows = tree_sum([ref[:, span] for ref in refs[:parts]])
        rows_ref[:, span] = rows
        exact = thirds(rows)
        left = jnp.concatenate(exact, axis=0)
        right = [ref[span, :] for ref in snapshots_refs]
        for part in right if len(right) == 2 else halves(right[0]):
            sums += jnp.dot(left[:2 * rank], part, preferred_element_type=jnp.float32)
        gram += product(left, exact, 1)
    sums = sums[:rank] + sums[rank:]
    tiles = snaps // LANES
    for at in range(tiles):
        block_ref[at * rank:(at + 1) * rank, :] = sums[:, at * LANES:(at + 1) * LANES]
    block_ref[tiles * rank:, :] = packed(gram)


def project(parts, snapshots):
    cells, snaps = snapshots[0].shape
    rank = parts[0].shape[0]
    return pl.pallas_call(
        lambda *refs: project_kernel(len(parts), *refs),
        in_specs=[VMEM] * (len(parts) + len(snapshots)),
        out_specs=[VMEM] * 2,
        out_shape=[
            pltpu.VMEM((rank, cells), jnp.float32),
            pltpu.VMEM((rank * (snaps + rank) // LANES, LANES), jnp.float32),
        ],
        compiler_params=limit(16),
        name="project",
    )(*parts, *snapshots)


def spread(row):
    return jnp.broadcast_to(row, (8, row.shape[1]))


def tall(tile, rank):
    return jnp.concatenate([tile] * (rank // 8), axis=0)


def lower_inverse(gram):
    rank, lanes = gram.shape
    block = math.gcd(rank, 4)
    row_at = lax.broadcasted_iota(jnp.int32, (rank, lanes), 0)
    lane_at = lax.broadcasted_iota(jnp.int32, (rank, lanes), 1)
    both = jnp.where(lane_at < rank, gram, jnp.where(lane_at == row_at + rank, 1.0, 0.0))
    pivots = jnp.ones((rank, lanes), jnp.float32)
    diagonal = jnp.sum(jnp.where(row_at == lane_at, gram, 0.0), axis=0, keepdims=True)
    columns = [jnp.broadcast_to(both[:, at:at + 1], (rank, lanes)) for at in range(block)]
    for base in range(0, rank, block):
        later = range(base + block, min(base + 2 * block, rank))
        upcoming = [jnp.broadcast_to(both[:, at:at + 1], (rank, lanes)) for at in later]
        corner = [[spread(columns[at][base + to:base + to + 1]) for at in range(block)] for to in range(block)]
        rows = [spread(both[base + at:base + at + 1]) for at in range(block)]
        for at in range(block):
            pivot = corner[at][at]
            inverse = 1.0 / pivot
            for to in range(at + 1, block):
                ratio = corner[to][at] * inverse
                rows[to] = rows[to] - ratio * rows[at]
                columns[to] = columns[to] - tall(ratio, rank) * columns[at]
                for along in range(at + 1, block):
                    corner[to][along] = corner[to][along] - ratio * corner[at][along]
            factor = jnp.where(row_at > base + at, columns[at] * tall(inverse, rank), 0.0)
            both = both - factor * tall(rows[at], rank)
            for to, place in enumerate(later):
                upcoming[to] = upcoming[to] - factor * tall(spread(columns[at][place:place + 1]), rank)
            pivots = jnp.where(row_at == base + at, tall(pivot, rank), pivots)
        columns = upcoming
    inverse = (both * lax.rsqrt(pivots))[:, rank:2 * rank]
    return inverse, jnp.sum(inverse * inverse * diagonal[:, :rank])


def factor_kernel(scale, parts, *refs):
    rows_ref, basis_ref, coefficients_ref, amplified_ref = refs[parts:]
    snaps = coefficients_ref.shape[1]
    block = tree_sum([ref[...] for ref in refs[:parts]])
    rank = rows_ref.shape[0]
    tiles = snaps // LANES
    full = block[tiles * rank:]
    turns = [full] + [pltpu.roll(full, LANES - at, 1) for at in range(rank, LANES, rank)]
    gram = jnp.concatenate(turns, axis=0)
    inverse, amplified = lower_inverse(gram)
    sound = amplified <= BROKEN
    amplified_ref[0, 0] = jnp.where(sound, amplified, BROKEN)

    def apply(inverse):
        left = jnp.concatenate(thirds(inverse), axis=0)
        for at in range(tiles):
            part = block[at * rank:(at + 1) * rank]
            coefficients_ref[:, at * LANES:(at + 1) * LANES] = product(left, thirds(part), 0)
        left = jnp.concatenate(thirds(inverse * scale), axis=0)
        chunk = math.gcd(CHUNK, rows_ref.shape[1])
        for at in range(0, rows_ref.shape[1], chunk):
            span = pl.ds(at, chunk)
            basis_ref[:, span] = product(left, thirds(rows_ref[:, span]), 0)

    apply(inverse)

    @pl.when(jnp.logical_not(sound))
    def _():
        row_at = lax.broadcasted_iota(jnp.int32, gram.shape, 0)
        lane_at = lax.broadcasted_iota(jnp.int32, gram.shape, 1)
        apply(lower_inverse(jnp.where(row_at == lane_at, gram * (1 + SHIFT), gram))[0])


def factor(parts, rows, scale, snaps):
    rank, cells = rows.shape
    return pl.pallas_call(
        lambda *refs: factor_kernel(scale, len(parts), *refs),
        in_specs=[VMEM] * (len(parts) + 1),
        out_specs=[VMEM] * 2 + [pl.BlockSpec(memory_space=pltpu.SMEM)],
        out_shape=[
            pltpu.HBM((rank, cells), jnp.float32),
            pltpu.HBM((rank, snaps), jnp.float32),
            pltpu.SMEM((1, 1), jnp.float32),
        ],
        compiler_params=limit(16),
        name="factor",
    )(*parts, rows)


def exchange(block, axis, radix):
    count = lax.axis_size(axis)
    steps = []
    step = 1
    while step < count:
        steps.append((step, min(radix, count // step)))
        step *= steps[-1][1]
    parts = [block]
    for step, group in steps[::-1]:
        order = list(range(group - 1, 0, -1))
        if len(parts) == 1 and group == 4:
            order = [2, 3, 1]
        block = tree_sum(parts)
        parts = [block] + [swap(block, axis, step * at) for at in order]
    return parts


def shards(snapshots, sketch):
    scale = math.sqrt(snapshots.shape[0] * lax.axis_size("cells"))

    def orthogonalize(parts, snapshots):
        rows, block = project(parts, snapshots)
        return factor(exchange(block, "cells", 4), rows, scale, snapshots[0].shape[1])

    partial_rows, held = sketch_rows(snapshots, sketch)
    first = orthogonalize(exchange(partial_rows, "snaps", 2), split(held))
    basis, coefficients, _, _ = lax.while_loop(
        lambda state: jnp.logical_and(state[2][0, 0] > AMPLIFIED, state[3] < PASSES),
        lambda state: (*orthogonalize([state[0]], [in_hbm(snapshots)]), state[3] + 1),
        (*first, jnp.int32(0)),
    )
    return (basis, coefficients)


def solution(mesh):
    return jax.shard_map(
        shards,
        mesh=mesh,
        in_specs=(P("cells", "snaps"), P("snaps", None)),
        out_specs=(P(None, "cells"), P(None, "snaps")),
        check_vma=False,
    )
```

```python
import math

import jax
import jax.numpy as jnp
from jax import lax
from jax.experimental import pallas as pl
from jax.experimental.pallas import tpu as pltpu
from jax.sharding import PartitionSpec as P

LANES = 128
CHUNK = 256
MIB = 1 << 20
AMPLIFIED = 512.0
BROKEN = 2e5
SHIFT = 3e-5
PASSES = 8
VMEM = pl.BlockSpec(memory_space=pltpu.VMEM)
HBM = pl.BlockSpec(memory_space=pltpu.HBM)


def limit(mebibytes):
    return pltpu.CompilerParams(vmem_limit_bytes=mebibytes * MIB)


def in_hbm(block):
    return pltpu.with_memory_space_constraint(block, pltpu.HBM)


def swap(block, axis, offset):
    count = lax.axis_size(axis)
    return lax.ppermute(block, axis, [(at, at ^ offset) for at in range(count)])


def tree_sum(parts):
    while len(parts) > 1:
        parts = [parts[at] + parts[at + 1] for at in range(0, len(parts), 2)]
    return parts[0]


def thirds(block):
    high, middle = halves(block)
    rest = block - high.astype(jnp.float32)
    low = (rest - middle.astype(jnp.float32)).astype(jnp.bfloat16)
    return high, middle, low


def halves(block):
    high = block.astype(jnp.bfloat16)
    return high, (block - high.astype(jnp.float32)).astype(jnp.bfloat16)


def product(left, right, right_dim):
    rank = left.shape[0] // 3
    dims = (((1,), (right_dim,)), ((), ()))
    high, middle, low = [
        lax.dot_general(left[:rank * (3 - at)], part, dims, preferred_element_type=jnp.float32)
        for at, part in enumerate(right)
    ]
    small = high[2 * rank:] + (middle[rank:] + low)
    return high[:rank] + ((high[rank:2 * rank] + middle[:rank]) + small)


def pieces(cells):
    if cells % 8:
        return [(0, cells)]
    return [(0, cells // 4), (cells // 4, cells // 4), (cells // 2, cells // 2)]


def sketch_kernel(sketch_ref, snapshots_ref, out_ref, held, sketch_held, arrived):
    fetches = pieces(held.shape[0])
    first = pltpu.make_async_copy(sketch_ref, sketch_held, arrived.at[len(fetches)])
    first.start()
    copies = []
    for at, (start, size) in enumerate(fetches):
        rows = pl.ds(start, size)
        copies.append(pltpu.make_async_copy(snapshots_ref.at[rows], held.at[rows], arrived.at[at]))
        copies[-1].start()
    first.wait()
    sketch = jnp.concatenate(thirds(sketch_held[...]), axis=0)
    for copy, (start, size) in zip(copies, fetches):
        copy.wait()
        chunk = math.gcd(CHUNK, size)
        for at in range(start, start + size, chunk):
            rows = pl.ds(at, chunk)
            out_ref[:, rows] = product(sketch, thirds(held[rows, :].T), 0)


def sketch_rows(snapshots, sketch):
    cells, snaps = snapshots.shape
    rank = sketch.shape[1]
    return pl.pallas_call(
        sketch_kernel,
        in_specs=[HBM] * 2,
        out_specs=[VMEM] * 2,
        out_shape=[
            pltpu.VMEM((rank, cells), jnp.float32),
            pltpu.VMEM((cells, snaps), jnp.float32),
        ],
        scratch_shapes=[
            pltpu.VMEM((rank, snaps), jnp.float32),
            pltpu.SemaphoreType.DMA((len(pieces(cells)) + 1,)),
        ],
        compiler_params=limit(16),
        name="sketch_rows",
    )(in_hbm(sketch.T), in_hbm(snapshots))


def packed(gram):
    rank = gram.shape[0]
    high = rank * rank // LANES
    return jnp.concatenate([gram[at:at + high] for at in range(0, rank, high)], axis=1)


def split_kernel(snapshots_ref, *refs):
    chunk = math.gcd(CHUNK, snapshots_ref.shape[0])
    for at in range(0, snapshots_ref.shape[0], chunk):
        span = pl.ds(at, chunk)
        for ref, part in zip(refs, halves(snapshots_ref[span, :])):
            ref[span, :] = part


def split(snapshots):
    cells, snaps = snapshots.shape
    return pl.pallas_call(
        split_kernel,
        in_specs=[VMEM],
        out_specs=[VMEM] * 2,
        out_shape=[pltpu.VMEM((cells, snaps), jnp.bfloat16)] * 2,
        compiler_params=limit(16),
        cost_estimate=pl.CostEstimate(flops=4 * cells * snaps, bytes_accessed=8 * cells * snaps, transcendentals=0),
        name="split",
    )(snapshots)


def project_kernel(parts, *refs):
    snapshots_refs = refs[parts:-2]
    rows_ref, block_ref = refs[-2:]
    rank, cells = rows_ref.shape
    snaps = snapshots_refs[0].shape[1]
    chunk = math.gcd(CHUNK, cells)
    sums = jnp.zeros((2 * rank, snaps), jnp.float32)
    gram = jnp.zeros((rank, rank), jnp.float32)
    for at in range(0, cells, chunk):
        span = pl.ds(at, chunk)
        rows = tree_sum([ref[:, span] for ref in refs[:parts]])
        rows_ref[:, span] = rows
        exact = thirds(rows)
        left = jnp.concatenate(exact, axis=0)
        right = [ref[span, :] for ref in snapshots_refs]
        for part in right if len(right) == 2 else halves(right[0]):
            sums += jnp.dot(left[:2 * rank], part, preferred_element_type=jnp.float32)
        gram += product(left, exact, 1)
    sums = sums[:rank] + sums[rank:]
    tiles = snaps // LANES
    for at in range(tiles):
        block_ref[at * rank:(at + 1) * rank, :] = sums[:, at * LANES:(at + 1) * LANES]
    block_ref[tiles * rank:, :] = packed(gram)


def project(parts, snapshots):
    cells, snaps = snapshots[0].shape
    rank = parts[0].shape[0]
    return pl.pallas_call(
        lambda *refs: project_kernel(len(parts), *refs),
        in_specs=[VMEM] * (len(parts) + len(snapshots)),
        out_specs=[VMEM] * 2,
        out_shape=[
            pltpu.VMEM((rank, cells), jnp.float32),
            pltpu.VMEM((rank * (snaps + rank) // LANES, LANES), jnp.float32),
        ],
        compiler_params=limit(16),
        name="project",
    )(*parts, *snapshots)


def spread(row):
    return jnp.broadcast_to(row, (8, row.shape[1]))


def tall(tile, rank):
    return jnp.concatenate([tile] * (rank // 8), axis=0)


def lower_inverse(gram):
    rank, lanes = gram.shape
    block = math.gcd(rank, 8)
    row_at = lax.broadcasted_iota(jnp.int32, (rank, lanes), 0)
    lane_at = lax.broadcasted_iota(jnp.int32, (rank, lanes), 1)
    both = jnp.where(lane_at < rank, gram, jnp.where(lane_at == row_at + rank, 1.0, 0.0))
    pivots = jnp.ones((rank, lanes), jnp.float32)
    diagonal = jnp.sum(jnp.where(row_at == lane_at, gram, 0.0), axis=0, keepdims=True)
    columns = [jnp.broadcast_to(both[:, at:at + 1], (rank, lanes)) for at in range(block)]
    for base in range(0, rank, block):
        later = range(base + block, min(base + 2 * block, rank))
        upcoming = [jnp.broadcast_to(both[:, at:at + 1], (rank, lanes)) for at in later]
        corner = [[spread(columns[at][base + to:base + to + 1]) for at in range(block)] for to in range(block)]
        rows = [spread(both[base + at:base + at + 1]) for at in range(block)]
        for at in range(block):
            pivot = corner[at][at]
            inverse = 1.0 / pivot
            for to in range(at + 1, block):
                ratio = corner[to][at] * inverse
                rows[to] = rows[to] - ratio * rows[at]
                columns[to] = columns[to] - tall(ratio, rank) * columns[at]
                for along in range(at + 1, block):
                    corner[to][along] = corner[to][along] - ratio * corner[at][along]
            factor = jnp.where(row_at > base + at, columns[at] * tall(inverse, rank), 0.0)
            both = both - factor * tall(rows[at], rank)
            for to, place in enumerate(later):
                upcoming[to] = upcoming[to] - factor * tall(spread(columns[at][place:place + 1]), rank)
            pivots = jnp.where(row_at == base + at, tall(pivot, rank), pivots)
        columns = upcoming
    inverse = (both * lax.rsqrt(pivots))[:, rank:2 * rank]
    return inverse, jnp.sum(inverse * inverse * diagonal[:, :rank])


def factor_kernel(scale, parts, *refs):
    rows_ref, basis_ref, coefficients_ref, amplified_ref = refs[parts:]
    snaps = coefficients_ref.shape[1]
    block = tree_sum([ref[...] for ref in refs[:parts]])
    rank = rows_ref.shape[0]
    tiles = snaps // LANES
    full = block[tiles * rank:]
    turns = [full] + [pltpu.roll(full, LANES - at, 1) for at in range(rank, LANES, rank)]
    gram = jnp.concatenate(turns, axis=0)
    inverse, amplified = lower_inverse(gram)
    sound = amplified <= BROKEN
    amplified_ref[0, 0] = jnp.where(sound, amplified, BROKEN)

    def apply(inverse):
        left = jnp.concatenate(thirds(inverse), axis=0)
        for at in range(tiles):
            part = block[at * rank:(at + 1) * rank]
            coefficients_ref[:, at * LANES:(at + 1) * LANES] = product(left, thirds(part), 0)
        left = jnp.concatenate(thirds(inverse * scale), axis=0)
        chunk = math.gcd(CHUNK, rows_ref.shape[1])
        for at in range(0, rows_ref.shape[1], chunk):
            span = pl.ds(at, chunk)
            basis_ref[:, span] = product(left, thirds(rows_ref[:, span]), 0)

    apply(inverse)

    @pl.when(jnp.logical_not(sound))
    def _():
        row_at = lax.broadcasted_iota(jnp.int32, gram.shape, 0)
        lane_at = lax.broadcasted_iota(jnp.int32, gram.shape, 1)
        apply(lower_inverse(jnp.where(row_at == lane_at, gram * (1 + SHIFT), gram))[0])


def factor(parts, rows, scale, snaps):
    rank, cells = rows.shape
    return pl.pallas_call(
        lambda *refs: factor_kernel(scale, len(parts), *refs),
        in_specs=[VMEM] * (len(parts) + 1),
        out_specs=[VMEM] * 2 + [pl.BlockSpec(memory_space=pltpu.SMEM)],
        out_shape=[
            pltpu.HBM((rank, cells), jnp.float32),
            pltpu.HBM((rank, snaps), jnp.float32),
            pltpu.SMEM((1, 1), jnp.float32),
        ],
        compiler_params=limit(16),
        name="factor",
    )(*parts, rows)


def exchange(block, axis, radix):
    count = lax.axis_size(axis)
    steps = []
    step = 1
    while step < count:
        steps.append((step, min(radix, count // step)))
        step *= steps[-1][1]
    parts = [block]
    for step, group in steps[::-1]:
        order = list(range(group - 1, 0, -1))
        if len(parts) == 1 and group == 4:
            order = [2, 3, 1]
        block = tree_sum(parts)
        parts = [block] + [swap(block, axis, step * at) for at in order]
    return parts


def shards(snapshots, sketch):
    scale = math.sqrt(snapshots.shape[0] * lax.axis_size("cells"))

    def orthogonalize(parts, snapshots):
        rows, block = project(parts, snapshots)
        return factor(exchange(block, "cells", 4), rows, scale, snapshots[0].shape[1])

    partial_rows, held = sketch_rows(snapshots, sketch)
    first = orthogonalize(exchange(partial_rows, "snaps", 2), split(held))
    basis, coefficients, _, _ = lax.while_loop(
        lambda state: jnp.logical_and(state[2][0, 0] > AMPLIFIED, state[3] < PASSES),
        lambda state: (*orthogonalize([state[0]], [in_hbm(snapshots)]), state[3] + 1),
        (*first, jnp.int32(0)),
    )
    return (basis, coefficients)


def solution(mesh):
    return jax.shard_map(
        shards,
        mesh=mesh,
        in_specs=(P("cells", "snaps"), P("snaps", None)),
        out_specs=(P(None, "cells"), P(None, "snaps")),
        check_vma=False,
    )
```

```python
import math

import jax
import jax.numpy as jnp
from jax import lax
from jax.experimental import pallas as pl
from jax.experimental.pallas import tpu as pltpu
from jax.sharding import PartitionSpec as P

LANES = 128
CHUNK = 256
MIB = 1 << 20
AMPLIFIED = 512.0
BROKEN = 2e5
SHIFT = 3e-5
PASSES = 8
VMEM = pl.BlockSpec(memory_space=pltpu.VMEM)
HBM = pl.BlockSpec(memory_space=pltpu.HBM)


def limit(mebibytes):
    return pltpu.CompilerParams(vmem_limit_bytes=mebibytes * MIB)


def in_hbm(block):
    return pltpu.with_memory_space_constraint(block, pltpu.HBM)


def swap(block, axis, offset):
    count = lax.axis_size(axis)
    return lax.ppermute(block, axis, [(at, at ^ offset) for at in range(count)])


def tree_sum(parts):
    while len(parts) > 1:
        parts = [parts[at] + parts[at + 1] for at in range(0, len(parts), 2)]
    return parts[0]


def thirds(block):
    high, middle = halves(block)
    rest = block - high.astype(jnp.float32)
    low = (rest - middle.astype(jnp.float32)).astype(jnp.bfloat16)
    return high, middle, low


def halves(block):
    high = block.astype(jnp.bfloat16)
    return high, (block - high.astype(jnp.float32)).astype(jnp.bfloat16)


def product(left, right, right_dim):
    rank = left.shape[0] // 3
    dims = (((1,), (right_dim,)), ((), ()))
    high, middle, low = [
        lax.dot_general(left[:rank * (3 - at)], part, dims, preferred_element_type=jnp.float32)
        for at, part in enumerate(right)
    ]
    small = high[2 * rank:] + (middle[rank:] + low)
    return high[:rank] + ((high[rank:2 * rank] + middle[:rank]) + small)


def pieces(cells):
    if cells % 8:
        return [(0, cells)]
    return [(0, cells // 8), (cells // 8, cells // 8 * 3), (cells // 2, cells // 2)]


def sketch_kernel(sketch_ref, snapshots_ref, out_ref, held, sketch_held, arrived):
    fetches = pieces(held.shape[0])
    first = pltpu.make_async_copy(sketch_ref, sketch_held, arrived.at[len(fetches)])
    first.start()
    copies = []
    for at, (start, size) in enumerate(fetches):
        rows = pl.ds(start, size)
        copies.append(pltpu.make_async_copy(snapshots_ref.at[rows], held.at[rows], arrived.at[at]))
        copies[-1].start()
    first.wait()
    sketch = jnp.concatenate(thirds(sketch_held[...]), axis=0)
    for copy, (start, size) in zip(copies, fetches):
        copy.wait()
        chunk = math.gcd(CHUNK, size)
        for at in range(start, start + size, chunk):
            rows = pl.ds(at, chunk)
            out_ref[:, rows] = product(sketch, thirds(held[rows, :].T), 0)


def sketch_rows(snapshots, sketch):
    cells, snaps = snapshots.shape
    rank = sketch.shape[1]
    return pl.pallas_call(
        sketch_kernel,
        in_specs=[HBM] * 2,
        out_specs=[VMEM] * 2,
        out_shape=[
            pltpu.VMEM((rank, cells), jnp.float32),
            pltpu.VMEM((cells, snaps), jnp.float32),
        ],
        scratch_shapes=[
            pltpu.VMEM((rank, snaps), jnp.float32),
            pltpu.SemaphoreType.DMA((len(pieces(cells)) + 1,)),
        ],
        compiler_params=limit(16),
        name="sketch_rows",
    )(in_hbm(sketch.T), in_hbm(snapshots))


def packed(gram):
    rank = gram.shape[0]
    high = rank * rank // LANES
    return jnp.concatenate([gram[at:at + high] for at in range(0, rank, high)], axis=1)


def split_kernel(snapshots_ref, *refs):
    chunk = math.gcd(CHUNK, snapshots_ref.shape[0])
    for at in range(0, snapshots_ref.shape[0], chunk):
        span = pl.ds(at, chunk)
        for ref, part in zip(refs, halves(snapshots_ref[span, :])):
            ref[span, :] = part


def split(snapshots):
    cells, snaps = snapshots.shape
    return pl.pallas_call(
        split_kernel,
        in_specs=[VMEM],
        out_specs=[VMEM] * 2,
        out_shape=[pltpu.VMEM((cells, snaps), jnp.bfloat16)] * 2,
        compiler_params=limit(16),
        cost_estimate=pl.CostEstimate(flops=4 * cells * snaps, bytes_accessed=8 * cells * snaps, transcendentals=0),
        name="split",
    )(snapshots)


def project_kernel(parts, *refs):
    snapshots_refs = refs[parts:-2]
    rows_ref, block_ref = refs[-2:]
    rank, cells = rows_ref.shape
    snaps = snapshots_refs[0].shape[1]
    chunk = math.gcd(CHUNK, cells)
    sums = jnp.zeros((2 * rank, snaps), jnp.float32)
    gram = jnp.zeros((rank, rank), jnp.float32)
    for at in range(0, cells, chunk):
        span = pl.ds(at, chunk)
        rows = tree_sum([ref[:, span] for ref in refs[:parts]])
        rows_ref[:, span] = rows
        exact = thirds(rows)
        left = jnp.concatenate(exact, axis=0)
        right = [ref[span, :] for ref in snapshots_refs]
        for part in right if len(right) == 2 else halves(right[0]):
            sums += jnp.dot(left[:2 * rank], part, preferred_element_type=jnp.float32)
        gram += product(left, exact, 1)
    sums = sums[:rank] + sums[rank:]
    tiles = snaps // LANES
    for at in range(tiles):
        block_ref[at * rank:(at + 1) * rank, :] = sums[:, at * LANES:(at + 1) * LANES]
    block_ref[tiles * rank:, :] = packed(gram)


def project(parts, snapshots):
    cells, snaps = snapshots[0].shape
    rank = parts[0].shape[0]
    return pl.pallas_call(
        lambda *refs: project_kernel(len(parts), *refs),
        in_specs=[VMEM] * (len(parts) + len(snapshots)),
        out_specs=[VMEM] * 2,
        out_shape=[
            pltpu.VMEM((rank, cells), jnp.float32),
            pltpu.VMEM((rank * (snaps + rank) // LANES, LANES), jnp.float32),
        ],
        compiler_params=limit(16),
        name="project",
    )(*parts, *snapshots)


def spread(row):
    return jnp.broadcast_to(row, (8, row.shape[1]))


def tall(tile, rank):
    return jnp.concatenate([tile] * (rank // 8), axis=0)


def lower_inverse(gram):
    rank, lanes = gram.shape
    block = math.gcd(rank, 4)
    row_at = lax.broadcasted_iota(jnp.int32, (rank, lanes), 0)
    lane_at = lax.broadcasted_iota(jnp.int32, (rank, lanes), 1)
    both = jnp.where(lane_at < rank, gram, jnp.where(lane_at == row_at + rank, 1.0, 0.0))
    pivots = jnp.ones((rank, lanes), jnp.float32)
    diagonal = jnp.sum(jnp.where(row_at == lane_at, gram, 0.0), axis=0, keepdims=True)
    columns = [jnp.broadcast_to(both[:, at:at + 1], (rank, lanes)) for at in range(block)]
    for base in range(0, rank, block):
        later = range(base + block, min(base + 2 * block, rank))
        upcoming = [jnp.broadcast_to(both[:, at:at + 1], (rank, lanes)) for at in later]
        corner = [[spread(columns[at][base + to:base + to + 1]) for at in range(block)] for to in range(block)]
        rows = [spread(both[base + at:base + at + 1]) for at in range(block)]
        for at in range(block):
            pivot = corner[at][at]
            inverse = 1.0 / pivot
            for to in range(at + 1, block):
                ratio = corner[to][at] * inverse
                rows[to] = rows[to] - ratio * rows[at]
                columns[to] = columns[to] - tall(ratio, rank) * columns[at]
                for along in range(at + 1, block):
                    corner[to][along] = corner[to][along] - ratio * corner[at][along]
            factor = jnp.where(row_at > base + at, columns[at] * tall(inverse, rank), 0.0)
            both = both - factor * tall(rows[at], rank)
            for to, place in enumerate(later):
                upcoming[to] = upcoming[to] - factor * tall(spread(columns[at][place:place + 1]), rank)
            pivots = jnp.where(row_at == base + at, tall(pivot, rank), pivots)
        columns = upcoming
    inverse = (both * lax.rsqrt(pivots))[:, rank:2 * rank]
    return inverse, jnp.sum(inverse * inverse * diagonal[:, :rank])


def factor_kernel(scale, parts, *refs):
    rows_ref, basis_ref, coefficients_ref, amplified_ref = refs[parts:]
    snaps = coefficients_ref.shape[1]
    block = tree_sum([ref[...] for ref in refs[:parts]])
    rank = rows_ref.shape[0]
    tiles = snaps // LANES
    full = block[tiles * rank:]
    turns = [full] + [pltpu.roll(full, LANES - at, 1) for at in range(rank, LANES, rank)]
    gram = jnp.concatenate(turns, axis=0)
    inverse, amplified = lower_inverse(gram)
    sound = amplified <= BROKEN
    amplified_ref[0, 0] = jnp.where(sound, amplified, BROKEN)

    def apply(inverse):
        left = jnp.concatenate(thirds(inverse), axis=0)
        for at in range(tiles):
            part = block[at * rank:(at + 1) * rank]
            coefficients_ref[:, at * LANES:(at + 1) * LANES] = product(left, thirds(part), 0)
        left = jnp.concatenate(thirds(inverse * scale), axis=0)
        chunk = math.gcd(CHUNK, rows_ref.shape[1])
        for at in range(0, rows_ref.shape[1], chunk):
            span = pl.ds(at, chunk)
            basis_ref[:, span] = product(left, thirds(rows_ref[:, span]), 0)

    apply(inverse)

    @pl.when(jnp.logical_not(sound))
    def _():
        row_at = lax.broadcasted_iota(jnp.int32, gram.shape, 0)
        lane_at = lax.broadcasted_iota(jnp.int32, gram.shape, 1)
        apply(lower_inverse(jnp.where(row_at == lane_at, gram * (1 + SHIFT), gram))[0])


def factor(parts, rows, scale, snaps):
    rank, cells = rows.shape
    return pl.pallas_call(
        lambda *refs: factor_kernel(scale, len(parts), *refs),
        in_specs=[VMEM] * (len(parts) + 1),
        out_specs=[VMEM] * 2 + [pl.BlockSpec(memory_space=pltpu.SMEM)],
        out_shape=[
            pltpu.HBM((rank, cells), jnp.float32),
            pltpu.HBM((rank, snaps), jnp.float32),
            pltpu.SMEM((1, 1), jnp.float32),
        ],
        compiler_params=limit(16),
        name="factor",
    )(*parts, rows)


def exchange(block, axis, radix):
    count = lax.axis_size(axis)
    steps = []
    step = 1
    while step < count:
        steps.append((step, min(radix, count // step)))
        step *= steps[-1][1]
    parts = [block]
    for step, group in steps:
        order = list(range(group - 1, 0, -1))
        if step * group == count and group == 4:
            order = [2, 3, 1]
        block = tree_sum(parts)
        parts = [block] + [swap(block, axis, step * at) for at in order]
    return parts


def shards(snapshots, sketch):
    scale = math.sqrt(snapshots.shape[0] * lax.axis_size("cells"))

    def orthogonalize(parts, snapshots):
        rows, block = project(parts, snapshots)
        return factor(exchange(block, "cells", 4), rows, scale, snapshots[0].shape[1])

    partial_rows, held = sketch_rows(snapshots, sketch)
    first = orthogonalize(exchange(partial_rows, "snaps", 2), split(held))
    basis, coefficients, _, _ = lax.while_loop(
        lambda state: jnp.logical_and(state[2][0, 0] > AMPLIFIED, state[3] < PASSES),
        lambda state: (*orthogonalize([state[0]], [in_hbm(snapshots)]), state[3] + 1),
        (*first, jnp.int32(0)),
    )
    return (basis, coefficients)


def solution(mesh):
    return jax.shard_map(
        shards,
        mesh=mesh,
        in_specs=(P("cells", "snaps"), P("snaps", None)),
        out_specs=(P(None, "cells"), P(None, "snaps")),
        check_vma=False,
    )
```

```python
import math

import jax
import jax.numpy as jnp
from jax import lax
from jax.experimental import pallas as pl
from jax.experimental.pallas import tpu as pltpu
from jax.sharding import PartitionSpec as P

LANES = 128
CHUNK = 256
MIB = 1 << 20
AMPLIFIED = 512.0
BROKEN = 2e5
SHIFT = 3e-5
PASSES = 8
VMEM = pl.BlockSpec(memory_space=pltpu.VMEM)
HBM = pl.BlockSpec(memory_space=pltpu.HBM)


def limit(mebibytes):
    return pltpu.CompilerParams(vmem_limit_bytes=mebibytes * MIB)


def in_hbm(block):
    return pltpu.with_memory_space_constraint(block, pltpu.HBM)


def swap(block, axis, offset):
    count = lax.axis_size(axis)
    return lax.ppermute(block, axis, [(at, at ^ offset) for at in range(count)])


def tree_sum(parts):
    while len(parts) > 1:
        parts = [parts[at] + parts[at + 1] for at in range(0, len(parts), 2)]
    return parts[0]


def thirds(block):
    high, middle = halves(block)
    rest = block - high.astype(jnp.float32)
    low = (rest - middle.astype(jnp.float32)).astype(jnp.bfloat16)
    return high, middle, low


def halves(block):
    high = block.astype(jnp.bfloat16)
    return high, (block - high.astype(jnp.float32)).astype(jnp.bfloat16)


def product(left, right, right_dim):
    rank = left.shape[0] // 3
    dims = (((1,), (right_dim,)), ((), ()))
    high, middle, low = [
        lax.dot_general(left[:rank * (3 - at)], part, dims, preferred_element_type=jnp.float32)
        for at, part in enumerate(right)
    ]
    small = high[2 * rank:] + (middle[rank:] + low)
    return high[:rank] + ((high[rank:2 * rank] + middle[:rank]) + small)


def pieces(cells):
    if cells % 8:
        return [(0, cells)]
    return [(0, cells // 8), (cells // 8, cells // 8 * 3), (cells // 2, cells // 2)]


def sketch_kernel(sketch_ref, snapshots_ref, out_ref, held, sketch_held, arrived):
    fetches = pieces(held.shape[0])
    first = pltpu.make_async_copy(sketch_ref, sketch_held, arrived.at[len(fetches)])
    first.start()
    copies = []
    for at, (start, size) in enumerate(fetches):
        rows = pl.ds(start, size)
        copies.append(pltpu.make_async_copy(snapshots_ref.at[rows], held.at[rows], arrived.at[at]))
        copies[-1].start()
    first.wait()
    sketch = jnp.concatenate(thirds(sketch_held[...]), axis=0)
    for copy, (start, size) in zip(copies, fetches):
        copy.wait()
        chunk = math.gcd(CHUNK, size)
        for at in range(start, start + size, chunk):
            rows = pl.ds(at, chunk)
            out_ref[:, rows] = product(sketch, thirds(held[rows, :].T), 0)


def sketch_rows(snapshots, sketch):
    cells, snaps = snapshots.shape
    rank = sketch.shape[1]
    return pl.pallas_call(
        sketch_kernel,
        in_specs=[HBM] * 2,
        out_specs=[VMEM] * 2,
        out_shape=[
            pltpu.VMEM((rank, cells), jnp.float32),
            pltpu.VMEM((cells, snaps), jnp.float32),
        ],
        scratch_shapes=[
            pltpu.VMEM((rank, snaps), jnp.float32),
            pltpu.SemaphoreType.DMA((len(pieces(cells)) + 1,)),
        ],
        compiler_params=limit(16),
        name="sketch_rows",
    )(in_hbm(sketch.T), in_hbm(snapshots))


def packed(gram):
    rank = gram.shape[0]
    high = rank * rank // LANES
    return jnp.concatenate([gram[at:at + high] for at in range(0, rank, high)], axis=1)


def split_kernel(snapshots_ref, *refs):
    chunk = math.gcd(CHUNK, snapshots_ref.shape[0])
    for at in range(0, snapshots_ref.shape[0], chunk):
        span = pl.ds(at, chunk)
        for ref, part in zip(refs, halves(snapshots_ref[span, :])):
            ref[span, :] = part


def split(snapshots):
    cells, snaps = snapshots.shape
    return pl.pallas_call(
        split_kernel,
        in_specs=[VMEM],
        out_specs=[VMEM] * 2,
        out_shape=[pltpu.VMEM((cells, snaps), jnp.bfloat16)] * 2,
        compiler_params=limit(16),
        cost_estimate=pl.CostEstimate(flops=4 * cells * snaps, bytes_accessed=8 * cells * snaps, transcendentals=0),
        name="split",
    )(snapshots)


def project_kernel(parts, *refs):
    snapshots_refs = refs[parts:-2]
    rows_ref, block_ref = refs[-2:]
    rank, cells = rows_ref.shape
    snaps = snapshots_refs[0].shape[1]
    chunk = math.gcd(CHUNK, cells)
    sums = jnp.zeros((2 * rank, snaps), jnp.float32)
    gram = jnp.zeros((rank, rank), jnp.float32)
    for at in range(0, cells, chunk):
        span = pl.ds(at, chunk)
        rows = tree_sum([ref[:, span] for ref in refs[:parts]])
        rows_ref[:, span] = rows
        exact = thirds(rows)
        left = jnp.concatenate(exact, axis=0)
        right = [ref[span, :] for ref in snapshots_refs]
        for part in right if len(right) == 2 else halves(right[0]):
            sums += jnp.dot(left[:2 * rank], part, preferred_element_type=jnp.float32)
        gram += product(left, exact, 1)
    sums = sums[:rank] + sums[rank:]
    tiles = snaps // LANES
    for at in range(tiles):
        block_ref[at * rank:(at + 1) * rank, :] = sums[:, at * LANES:(at + 1) * LANES]
    block_ref[tiles * rank:, :] = packed(gram)


def project(parts, snapshots):
    cells, snaps = snapshots[0].shape
    rank = parts[0].shape[0]
    return pl.pallas_call(
        lambda *refs: project_kernel(len(parts), *refs),
        in_specs=[VMEM] * (len(parts) + len(snapshots)),
        out_specs=[VMEM] * 2,
        out_shape=[
            pltpu.VMEM((rank, cells), jnp.float32),
            pltpu.VMEM((rank * (snaps + rank) // LANES, LANES), jnp.float32),
        ],
        compiler_params=limit(16),
        name="project",
    )(*parts, *snapshots)


def spread(row):
    return jnp.broadcast_to(row, (8, row.shape[1]))


def tall(tile, rank):
    return jnp.concatenate([tile] * (rank // 8), axis=0)


def reciprocal(value):
    rough = pl.reciprocal(value, approx=True)
    return rough * (2.0 - value * rough)


def lower_inverse(gram):
    rank, lanes = gram.shape
    block = math.gcd(rank, 4)
    row_at = lax.broadcasted_iota(jnp.int32, (rank, lanes), 0)
    lane_at = lax.broadcasted_iota(jnp.int32, (rank, lanes), 1)
    both = jnp.where(lane_at < rank, gram, jnp.where(lane_at == row_at + rank, 1.0, 0.0))
    pivots = jnp.ones((rank, lanes), jnp.float32)
    diagonal = jnp.sum(jnp.where(row_at == lane_at, gram, 0.0), axis=0, keepdims=True)
    columns = [jnp.broadcast_to(both[:, at:at + 1], (rank, lanes)) for at in range(block)]
    for base in range(0, rank, block):
        later = range(base + block, min(base + 2 * block, rank))
        upcoming = [jnp.broadcast_to(both[:, at:at + 1], (rank, lanes)) for at in later]
        corner = [[spread(columns[at][base + to:base + to + 1]) for at in range(block)] for to in range(block)]
        rows = [spread(both[base + at:base + at + 1]) for at in range(block)]
        for at in range(block):
            pivot = corner[at][at]
            inverse = reciprocal(pivot)
            for to in range(at + 1, block):
                ratio = corner[to][at] * inverse
                rows[to] = rows[to] - ratio * rows[at]
                columns[to] = columns[to] - tall(ratio, rank) * columns[at]
                for along in range(at + 1, block):
                    corner[to][along] = corner[to][along] - ratio * corner[at][along]
            factor = jnp.where(row_at > base + at, columns[at] * tall(inverse, rank), 0.0)
            both = both - factor * tall(rows[at], rank)
            for to, place in enumerate(later):
                upcoming[to] = upcoming[to] - factor * tall(spread(columns[at][place:place + 1]), rank)
            pivots = jnp.where(row_at == base + at, tall(pivot, rank), pivots)
        columns = upcoming
    inverse = (both * lax.rsqrt(pivots))[:, rank:2 * rank]
    return inverse, jnp.sum(inverse * inverse * diagonal[:, :rank])


def factor_kernel(scale, parts, *refs):
    rows_ref, basis_ref, coefficients_ref, amplified_ref = refs[parts:]
    snaps = coefficients_ref.shape[1]
    block = tree_sum([ref[...] for ref in refs[:parts]])
    rank = rows_ref.shape[0]
    tiles = snaps // LANES
    full = block[tiles * rank:]
    turns = [full] + [pltpu.roll(full, LANES - at, 1) for at in range(rank, LANES, rank)]
    gram = jnp.concatenate(turns, axis=0)
    inverse, amplified = lower_inverse(gram)
    sound = amplified <= BROKEN
    amplified_ref[0, 0] = jnp.where(sound, amplified, BROKEN)

    def apply(inverse):
        left = jnp.concatenate(thirds(inverse), axis=0)
        for at in range(tiles):
            part = block[at * rank:(at + 1) * rank]
            coefficients_ref[:, at * LANES:(at + 1) * LANES] = product(left, thirds(part), 0)
        left = jnp.concatenate(thirds(inverse * scale), axis=0)
        chunk = math.gcd(CHUNK, rows_ref.shape[1])
        for at in range(0, rows_ref.shape[1], chunk):
            span = pl.ds(at, chunk)
            basis_ref[:, span] = product(left, thirds(rows_ref[:, span]), 0)

    apply(inverse)

    @pl.when(jnp.logical_not(sound))
    def _():
        row_at = lax.broadcasted_iota(jnp.int32, gram.shape, 0)
        lane_at = lax.broadcasted_iota(jnp.int32, gram.shape, 1)
        apply(lower_inverse(jnp.where(row_at == lane_at, gram * (1 + SHIFT), gram))[0])


def factor(parts, rows, scale, snaps):
    rank, cells = rows.shape
    return pl.pallas_call(
        lambda *refs: factor_kernel(scale, len(parts), *refs),
        in_specs=[VMEM] * (len(parts) + 1),
        out_specs=[VMEM] * 2 + [pl.BlockSpec(memory_space=pltpu.SMEM)],
        out_shape=[
            pltpu.HBM((rank, cells), jnp.float32),
            pltpu.HBM((rank, snaps), jnp.float32),
            pltpu.SMEM((1, 1), jnp.float32),
        ],
        compiler_params=limit(16),
        name="factor",
    )(*parts, rows)


def exchange(block, axis, radix):
    count = lax.axis_size(axis)
    steps = []
    step = 1
    while step < count:
        steps.append((step, min(radix, count // step)))
        step *= steps[-1][1]
    parts = [block]
    for step, group in steps:
        order = list(range(group - 1, 0, -1))
        if step * group == count and group == 4:
            order = [2, 3, 1]
        block = tree_sum(parts)
        parts = [block] + [swap(block, axis, step * at) for at in order]
    return parts


def shards(snapshots, sketch):
    scale = math.sqrt(snapshots.shape[0] * lax.axis_size("cells"))

    def orthogonalize(parts, snapshots):
        rows, block = project(parts, snapshots)
        return factor(exchange(block, "cells", 4), rows, scale, snapshots[0].shape[1])

    partial_rows, held = sketch_rows(snapshots, sketch)
    first = orthogonalize(exchange(partial_rows, "snaps", 2), split(held))
    basis, coefficients, _, _ = lax.while_loop(
        lambda state: jnp.logical_and(state[2][0, 0] > AMPLIFIED, state[3] < PASSES),
        lambda state: (*orthogonalize([state[0]], [in_hbm(snapshots)]), state[3] + 1),
        (*first, jnp.int32(0)),
    )
    return (basis, coefficients)


def solution(mesh):
    return jax.shard_map(
        shards,
        mesh=mesh,
        in_specs=(P("cells", "snaps"), P("snaps", None)),
        out_specs=(P(None, "cells"), P(None, "snaps")),
        check_vma=False,
    )
```

```python
import math

import jax
import jax.numpy as jnp
from jax import lax
from jax.experimental import pallas as pl
from jax.experimental.pallas import tpu as pltpu
from jax.sharding import PartitionSpec as P

LANES = 128
CHUNK = 256
MIB = 1 << 20
AMPLIFIED = 512.0
BROKEN = 2e5
SHIFT = 3e-5
PASSES = 8
VMEM = pl.BlockSpec(memory_space=pltpu.VMEM)
HBM = pl.BlockSpec(memory_space=pltpu.HBM)


def limit(mebibytes):
    return pltpu.CompilerParams(vmem_limit_bytes=mebibytes * MIB)


def in_hbm(block):
    return pltpu.with_memory_space_constraint(block, pltpu.HBM)


def swap(block, axis, offset):
    count = lax.axis_size(axis)
    return lax.ppermute(block, axis, [(at, at ^ offset) for at in range(count)])


def tree_sum(parts):
    while len(parts) > 1:
        parts = [parts[at] + parts[at + 1] for at in range(0, len(parts), 2)]
    return parts[0]


def thirds(block):
    high, middle = halves(block)
    rest = block - high.astype(jnp.float32)
    low = (rest - middle.astype(jnp.float32)).astype(jnp.bfloat16)
    return high, middle, low


def halves(block):
    high = block.astype(jnp.bfloat16)
    return high, (block - high.astype(jnp.float32)).astype(jnp.bfloat16)


def product(left, right, right_dim):
    rank = left.shape[0] // 3
    dims = (((1,), (right_dim,)), ((), ()))
    high, middle, low = [
        lax.dot_general(left[:rank * (3 - at)], part, dims, preferred_element_type=jnp.float32)
        for at, part in enumerate(right)
    ]
    small = high[2 * rank:] + (middle[rank:] + low)
    return high[:rank] + ((high[rank:2 * rank] + middle[:rank]) + small)


def pieces(cells):
    if cells % 8:
        return [(0, cells)]
    return [(0, cells // 8), (cells // 8, cells // 8 * 3), (cells // 2, cells // 2)]


def multiply(sketch, held, out_ref, start, size, base):
    chunk = math.gcd(CHUNK, size)
    for at in range(start, start + size, chunk):
        out_ref[:, pl.ds(at - base, chunk)] = product(sketch, thirds(held[pl.ds(at, chunk), :].T), 0)


def first_kernel(sketch_ref, snapshots_ref, out_ref, held, sketch_held, arrived):
    fetches = pieces(held.shape[0])
    first = pltpu.make_async_copy(sketch_ref, sketch_held, arrived.at[len(fetches)])
    first.start()
    copies = []
    for at, (start, size) in enumerate(fetches):
        rows = pl.ds(start, size)
        copies.append(pltpu.make_async_copy(snapshots_ref.at[rows], held.at[rows], arrived.at[at]))
        copies[-1].start()
    first.wait()
    sketch = jnp.concatenate(thirds(sketch_held[...]), axis=0)
    for copy, (start, size) in zip(copies, fetches):
        if start < out_ref.shape[1]:
            copy.wait()
            multiply(sketch, held, out_ref, start, size, 0)
    copies[-1].wait()


def second_kernel(sketch_ref, held, out_ref):
    sketch = jnp.concatenate(thirds(sketch_ref[...]), axis=0)
    half = out_ref.shape[1]
    multiply(sketch, held, out_ref, half, half, half)


def sketch_rows(snapshots, sketch):
    cells, snaps = snapshots.shape
    rank = sketch.shape[1]
    return pl.pallas_call(
        first_kernel,
        in_specs=[HBM] * 2,
        out_specs=[VMEM] * 2,
        out_shape=[
            pltpu.VMEM((rank, cells // 2), jnp.float32),
            pltpu.VMEM((cells, snaps), jnp.float32),
        ],
        scratch_shapes=[
            pltpu.VMEM((rank, snaps), jnp.float32),
            pltpu.SemaphoreType.DMA((len(pieces(cells)) + 1,)),
        ],
        compiler_params=limit(16),
        name="sketch_first",
    )(in_hbm(sketch.T), in_hbm(snapshots))


def sketch_rest(held, sketch):
    cells, snaps = held.shape
    rank = sketch.shape[1]
    return pl.pallas_call(
        second_kernel,
        in_specs=[VMEM] * 2,
        out_specs=VMEM,
        out_shape=pltpu.VMEM((rank, cells // 2), jnp.float32),
        compiler_params=limit(16),
        cost_estimate=pl.CostEstimate(flops=6 * rank * cells * snaps, bytes_accessed=4 * cells * snaps, transcendentals=0),
        name="sketch_second",
    )(sketch.T, held)


def packed(gram):
    rank = gram.shape[0]
    high = rank * rank // LANES
    return jnp.concatenate([gram[at:at + high] for at in range(0, rank, high)], axis=1)


def project_kernel(parts, start, *refs):
    snapshots_ref = refs[parts]
    before = refs[parts + 1:-2]
    rows_ref, block_ref = refs[-2:]
    rank, cells = rows_ref.shape
    snaps = snapshots_ref.shape[1]
    chunk = math.gcd(CHUNK, cells)
    sums = jnp.zeros((2 * rank, snaps), jnp.float32)
    gram = jnp.zeros((rank, rank), jnp.float32)
    for at in range(0, cells, chunk):
        span = pl.ds(at, chunk)
        rows = tree_sum([ref[:, span] for ref in refs[:parts]])
        rows_ref[:, span] = rows
        exact = thirds(rows)
        left = jnp.concatenate(exact, axis=0)
        for part in halves(snapshots_ref[pl.ds(start + at, chunk), :]):
            sums += jnp.dot(left[:2 * rank], part, preferred_element_type=jnp.float32)
        gram += product(left, exact, 1)
    sums = sums[:rank] + sums[rank:]
    tiles = snaps // LANES
    found = [sums[:, at * LANES:(at + 1) * LANES] for at in range(tiles)]
    found = jnp.concatenate(found + [packed(gram)], axis=0)
    for ref in before:
        found += ref[...]
    block_ref[...] = found


def project(parts, snapshots, start, before):
    snaps = snapshots.shape[1]
    rank, cells = parts[0].shape
    return pl.pallas_call(
        lambda *refs: project_kernel(len(parts), start, *refs),
        in_specs=[VMEM] * (len(parts) + 1 + len(before)),
        out_specs=[VMEM] * 2,
        out_shape=[
            pltpu.VMEM((rank, cells), jnp.float32),
            pltpu.VMEM((rank * (snaps + rank) // LANES, LANES), jnp.float32),
        ],
        compiler_params=limit(16),
        cost_estimate=pl.CostEstimate(flops=5 * rank * cells * snaps, bytes_accessed=4 * cells * snaps, transcendentals=0),
        name="project",
    )(*parts, snapshots, *before)


def spread(row):
    return jnp.broadcast_to(row, (8, row.shape[1]))


def tall(tile, rank):
    return jnp.concatenate([tile] * (rank // 8), axis=0)


def lower_inverse(gram):
    rank, lanes = gram.shape
    block = math.gcd(rank, 4)
    row_at = lax.broadcasted_iota(jnp.int32, (rank, lanes), 0)
    lane_at = lax.broadcasted_iota(jnp.int32, (rank, lanes), 1)
    both = jnp.where(lane_at < rank, gram, jnp.where(lane_at == row_at + rank, 1.0, 0.0))
    pivots = jnp.ones((rank, lanes), jnp.float32)
    diagonal = jnp.sum(jnp.where(row_at == lane_at, gram, 0.0), axis=0, keepdims=True)
    columns = [jnp.broadcast_to(both[:, at:at + 1], (rank, lanes)) for at in range(block)]
    for base in range(0, rank, block):
        later = range(base + block, min(base + 2 * block, rank))
        upcoming = [jnp.broadcast_to(both[:, at:at + 1], (rank, lanes)) for at in later]
        corner = [[spread(columns[at][base + to:base + to + 1]) for at in range(block)] for to in range(block)]
        rows = [spread(both[base + at:base + at + 1]) for at in range(block)]
        for at in range(block):
            pivot = corner[at][at]
            inverse = 1.0 / pivot
            for to in range(at + 1, block):
                ratio = corner[to][at] * inverse
                rows[to] = rows[to] - ratio * rows[at]
                columns[to] = columns[to] - tall(ratio, rank) * columns[at]
                for along in range(at + 1, block):
                    corner[to][along] = corner[to][along] - ratio * corner[at][along]
            factor = jnp.where(row_at > base + at, columns[at] * tall(inverse, rank), 0.0)
            both = both - factor * tall(rows[at], rank)
            for to, place in enumerate(later):
                upcoming[to] = upcoming[to] - factor * tall(spread(columns[at][place:place + 1]), rank)
            pivots = jnp.where(row_at == base + at, tall(pivot, rank), pivots)
        columns = upcoming
    inverse = (both * lax.rsqrt(pivots))[:, rank:2 * rank]
    return inverse, jnp.sum(inverse * inverse * diagonal[:, :rank])


def factor_kernel(scale, parts, *refs):
    rows_refs = refs[parts:-3]
    basis_ref, coefficients_ref, amplified_ref = refs[-3:]
    snaps = coefficients_ref.shape[1]
    block = tree_sum([ref[...] for ref in refs[:parts]])
    rank = basis_ref.shape[0]
    tiles = snaps // LANES
    full = block[tiles * rank:]
    turns = [full] + [pltpu.roll(full, LANES - at, 1) for at in range(rank, LANES, rank)]
    gram = jnp.concatenate(turns, axis=0)
    inverse, amplified = lower_inverse(gram)
    sound = amplified <= BROKEN
    amplified_ref[0, 0] = jnp.where(sound, amplified, BROKEN)

    def apply(inverse):
        left = jnp.concatenate(thirds(inverse), axis=0)
        for at in range(tiles):
            part = block[at * rank:(at + 1) * rank]
            coefficients_ref[:, at * LANES:(at + 1) * LANES] = product(left, thirds(part), 0)
        left = jnp.concatenate(thirds(inverse * scale), axis=0)
        base = 0
        for ref in rows_refs:
            chunk = math.gcd(CHUNK, ref.shape[1])
            for at in range(0, ref.shape[1], chunk):
                basis_ref[:, pl.ds(base + at, chunk)] = product(left, thirds(ref[:, pl.ds(at, chunk)]), 0)
            base += ref.shape[1]

    apply(inverse)

    @pl.when(jnp.logical_not(sound))
    def _():
        row_at = lax.broadcasted_iota(jnp.int32, gram.shape, 0)
        lane_at = lax.broadcasted_iota(jnp.int32, gram.shape, 1)
        apply(lower_inverse(jnp.where(row_at == lane_at, gram * (1 + SHIFT), gram))[0])


def factor(parts, rows, scale, snaps):
    rank = rows[0].shape[0]
    cells = sum(part.shape[1] for part in rows)
    return pl.pallas_call(
        lambda *refs: factor_kernel(scale, len(parts), *refs),
        in_specs=[VMEM] * (len(parts) + len(rows)),
        out_specs=[VMEM] * 2 + [pl.BlockSpec(memory_space=pltpu.SMEM)],
        out_shape=[
            pltpu.HBM((rank, cells), jnp.float32),
            pltpu.HBM((rank, snaps), jnp.float32),
            pltpu.SMEM((1, 1), jnp.float32),
        ],
        compiler_params=limit(16),
        name="factor",
    )(*parts, *rows)


def exchange(block, axis, radix):
    count = lax.axis_size(axis)
    steps = []
    step = 1
    while step < count:
        steps.append((step, min(radix, count // step)))
        step *= steps[-1][1]
    parts = [block]
    for step, group in steps:
        order = list(range(group - 1, 0, -1))
        if step * group == count and group == 4:
            order = [2, 3, 1]
        block = tree_sum(parts)
        parts = [block] + [swap(block, axis, step * at) for at in order]
    return parts


def shards(snapshots, sketch):
    scale = math.sqrt(snapshots.shape[0] * lax.axis_size("cells"))

    columns = snapshots.shape[1]

    def again(basis):
        rows, block = project([basis], in_hbm(snapshots), 0, [])
        return factor(exchange(block, "cells", 4), [rows], scale, columns)

    early, held = sketch_rows(snapshots, sketch)
    early = exchange(early, "snaps", 2)
    late = exchange(sketch_rest(held, sketch), "snaps", 2)
    early, block = project(early, held, 0, [])
    late, block = project(late, held, held.shape[0] // 2, [block])
    first = factor(exchange(block, "cells", 4), [early, late], scale, columns)
    basis, coefficients, _, _ = lax.while_loop(
        lambda state: jnp.logical_and(state[2][0, 0] > AMPLIFIED, state[3] < PASSES),
        lambda state: (*again(state[0]), state[3] + 1),
        (*first, jnp.int32(0)),
    )
    return (basis, coefficients)


def solution(mesh):
    return jax.shard_map(
        shards,
        mesh=mesh,
        in_specs=(P("cells", "snaps"), P("snaps", None)),
        out_specs=(P(None, "cells"), P(None, "snaps")),
        check_vma=False,
    )
```

```python
import math

import jax
import jax.numpy as jnp
from jax import lax
from jax.experimental import pallas as pl
from jax.experimental.pallas import tpu as pltpu
from jax.sharding import PartitionSpec as P

LANES = 128
CHUNK = 256
MIB = 1 << 20
AMPLIFIED = 512.0
BROKEN = 2e5
SHIFT = 3e-5
PASSES = 8
VMEM = pl.BlockSpec(memory_space=pltpu.VMEM)
HBM = pl.BlockSpec(memory_space=pltpu.HBM)


def limit(mebibytes):
    return pltpu.CompilerParams(vmem_limit_bytes=mebibytes * MIB)


def in_hbm(block):
    return pltpu.with_memory_space_constraint(block, pltpu.HBM)


def swap(block, axis, offset):
    count = lax.axis_size(axis)
    return lax.ppermute(block, axis, [(at, at ^ offset) for at in range(count)])


def tree_sum(parts):
    while len(parts) > 1:
        parts = [parts[at] + parts[at + 1] for at in range(0, len(parts), 2)]
    return parts[0]


def thirds(block):
    high, middle = halves(block)
    rest = block - high.astype(jnp.float32)
    low = (rest - middle.astype(jnp.float32)).astype(jnp.bfloat16)
    return high, middle, low


def halves(block):
    high = block.astype(jnp.bfloat16)
    return high, (block - high.astype(jnp.float32)).astype(jnp.bfloat16)


def product(left, right, right_dim):
    rank = left.shape[0] // 3
    dims = (((1,), (right_dim,)), ((), ()))
    high, middle, low = [
        lax.dot_general(left[:rank * (3 - at)], part, dims, preferred_element_type=jnp.float32)
        for at, part in enumerate(right)
    ]
    small = high[2 * rank:] + (middle[rank:] + low)
    return high[:rank] + ((high[rank:2 * rank] + middle[:rank]) + small)


def first_share(cells):
    return cells // 8 * 5


def pieces(cells):
    early = first_share(cells)
    return [(0, cells // 8), (cells // 8, early - cells // 8), (early, cells - early)]


def multiply(sketch, held, out_ref, start, size, base):
    chunk = math.gcd(CHUNK, size)
    for at in range(start, start + size, chunk):
        out_ref[:, pl.ds(at - base, chunk)] = product(sketch, thirds(held[pl.ds(at, chunk), :].T), 0)


def first_kernel(sketch_ref, snapshots_ref, out_ref, held, sketch_held, arrived):
    fetches = pieces(held.shape[0])
    first = pltpu.make_async_copy(sketch_ref, sketch_held, arrived.at[len(fetches)])
    first.start()
    copies = []
    for at, (start, size) in enumerate(fetches):
        rows = pl.ds(start, size)
        copies.append(pltpu.make_async_copy(snapshots_ref.at[rows], held.at[rows], arrived.at[at]))
        copies[-1].start()
    first.wait()
    sketch = jnp.concatenate(thirds(sketch_held[...]), axis=0)
    for copy, (start, size) in zip(copies, fetches):
        if start < out_ref.shape[1]:
            copy.wait()
            multiply(sketch, held, out_ref, start, size, 0)
    copies[-1].wait()


def second_kernel(sketch_ref, held, out_ref):
    sketch = jnp.concatenate(thirds(sketch_ref[...]), axis=0)
    late = out_ref.shape[1]
    start = held.shape[0] - late
    multiply(sketch, held, out_ref, start, late, start)


def sketch_rows(snapshots, sketch):
    cells, snaps = snapshots.shape
    rank = sketch.shape[1]
    return pl.pallas_call(
        first_kernel,
        in_specs=[HBM] * 2,
        out_specs=[VMEM] * 2,
        out_shape=[
            pltpu.VMEM((rank, first_share(cells)), jnp.float32),
            pltpu.VMEM((cells, snaps), jnp.float32),
        ],
        scratch_shapes=[
            pltpu.VMEM((rank, snaps), jnp.float32),
            pltpu.SemaphoreType.DMA((len(pieces(cells)) + 1,)),
        ],
        compiler_params=limit(16),
        name="sketch_first",
    )(in_hbm(sketch.T), in_hbm(snapshots))


def sketch_rest(held, sketch):
    cells, snaps = held.shape
    rank = sketch.shape[1]
    return pl.pallas_call(
        second_kernel,
        in_specs=[VMEM] * 2,
        out_specs=VMEM,
        out_shape=pltpu.VMEM((rank, cells - first_share(cells)), jnp.float32),
        compiler_params=limit(16),
        cost_estimate=pl.CostEstimate(flops=6 * rank * cells * snaps, bytes_accessed=4 * cells * snaps, transcendentals=0),
        name="sketch_second",
    )(sketch.T, held)


def packed(gram):
    rank = gram.shape[0]
    high = rank * rank // LANES
    return jnp.concatenate([gram[at:at + high] for at in range(0, rank, high)], axis=1)


def project_kernel(parts, start, *refs):
    snapshots_ref = refs[parts]
    before = refs[parts + 1:-2]
    rows_ref, block_ref = refs[-2:]
    rank, cells = rows_ref.shape
    snaps = snapshots_ref.shape[1]
    chunk = math.gcd(CHUNK, cells)
    sums = jnp.zeros((2 * rank, snaps), jnp.float32)
    gram = jnp.zeros((rank, rank), jnp.float32)
    for at in range(0, cells, chunk):
        span = pl.ds(at, chunk)
        rows = tree_sum([ref[:, span] for ref in refs[:parts]])
        rows_ref[:, span] = rows
        exact = thirds(rows)
        left = jnp.concatenate(exact, axis=0)
        for part in halves(snapshots_ref[pl.ds(start + at, chunk), :]):
            sums += jnp.dot(left[:2 * rank], part, preferred_element_type=jnp.float32)
        gram += product(left, exact, 1)
    sums = sums[:rank] + sums[rank:]
    tiles = snaps // LANES
    found = [sums[:, at * LANES:(at + 1) * LANES] for at in range(tiles)]
    found = jnp.concatenate(found + [packed(gram)], axis=0)
    for ref in before:
        found += ref[...]
    block_ref[...] = found


def project(parts, snapshots, start, before):
    snaps = snapshots.shape[1]
    rank, cells = parts[0].shape
    return pl.pallas_call(
        lambda *refs: project_kernel(len(parts), start, *refs),
        in_specs=[VMEM] * (len(parts) + 1 + len(before)),
        out_specs=[VMEM] * 2,
        out_shape=[
            pltpu.VMEM((rank, cells), jnp.float32),
            pltpu.VMEM((rank * (snaps + rank) // LANES, LANES), jnp.float32),
        ],
        compiler_params=limit(16),
        cost_estimate=pl.CostEstimate(flops=5 * rank * cells * snaps, bytes_accessed=4 * cells * snaps, transcendentals=0),
        name="project",
    )(*parts, snapshots, *before)


def spread(row):
    return jnp.broadcast_to(row, (8, row.shape[1]))


def tall(tile, rank):
    return jnp.concatenate([tile] * (rank // 8), axis=0)


def lower_inverse(gram):
    rank, lanes = gram.shape
    block = math.gcd(rank, 4)
    row_at = lax.broadcasted_iota(jnp.int32, (rank, lanes), 0)
    lane_at = lax.broadcasted_iota(jnp.int32, (rank, lanes), 1)
    both = jnp.where(lane_at < rank, gram, jnp.where(lane_at == row_at + rank, 1.0, 0.0))
    pivots = jnp.ones((rank, lanes), jnp.float32)
    diagonal = jnp.sum(jnp.where(row_at == lane_at, gram, 0.0), axis=0, keepdims=True)
    columns = [jnp.broadcast_to(both[:, at:at + 1], (rank, lanes)) for at in range(block)]
    for base in range(0, rank, block):
        later = range(base + block, min(base + 2 * block, rank))
        upcoming = [jnp.broadcast_to(both[:, at:at + 1], (rank, lanes)) for at in later]
        corner = [[spread(columns[at][base + to:base + to + 1]) for at in range(block)] for to in range(block)]
        rows = [spread(both[base + at:base + at + 1]) for at in range(block)]
        for at in range(block):
            pivot = corner[at][at]
            inverse = 1.0 / pivot
            for to in range(at + 1, block):
                ratio = corner[to][at] * inverse
                rows[to] = rows[to] - ratio * rows[at]
                columns[to] = columns[to] - tall(ratio, rank) * columns[at]
                for along in range(at + 1, block):
                    corner[to][along] = corner[to][along] - ratio * corner[at][along]
            factor = jnp.where(row_at > base + at, columns[at] * tall(inverse, rank), 0.0)
            both = both - factor * tall(rows[at], rank)
            for to, place in enumerate(later):
                upcoming[to] = upcoming[to] - factor * tall(spread(columns[at][place:place + 1]), rank)
            pivots = jnp.where(row_at == base + at, tall(pivot, rank), pivots)
        columns = upcoming
    inverse = (both * lax.rsqrt(pivots))[:, rank:2 * rank]
    return inverse, jnp.sum(inverse * inverse * diagonal[:, :rank])


def factor_kernel(scale, parts, *refs):
    rows_refs = refs[parts:-3]
    basis_ref, coefficients_ref, amplified_ref = refs[-3:]
    snaps = coefficients_ref.shape[1]
    block = tree_sum([ref[...] for ref in refs[:parts]])
    rank = basis_ref.shape[0]
    tiles = snaps // LANES
    full = block[tiles * rank:]
    turns = [full] + [pltpu.roll(full, LANES - at, 1) for at in range(rank, LANES, rank)]
    gram = jnp.concatenate(turns, axis=0)
    inverse, amplified = lower_inverse(gram)
    sound = amplified <= BROKEN
    amplified_ref[0, 0] = jnp.where(sound, amplified, BROKEN)

    def apply(inverse):
        left = jnp.concatenate(thirds(inverse), axis=0)
        for at in range(tiles):
            part = block[at * rank:(at + 1) * rank]
            coefficients_ref[:, at * LANES:(at + 1) * LANES] = product(left, thirds(part), 0)
        left = jnp.concatenate(thirds(inverse * scale), axis=0)
        base = 0
        for ref in rows_refs:
            chunk = math.gcd(CHUNK, ref.shape[1])
            for at in range(0, ref.shape[1], chunk):
                basis_ref[:, pl.ds(base + at, chunk)] = product(left, thirds(ref[:, pl.ds(at, chunk)]), 0)
            base += ref.shape[1]

    apply(inverse)

    @pl.when(jnp.logical_not(sound))
    def _():
        row_at = lax.broadcasted_iota(jnp.int32, gram.shape, 0)
        lane_at = lax.broadcasted_iota(jnp.int32, gram.shape, 1)
        apply(lower_inverse(jnp.where(row_at == lane_at, gram * (1 + SHIFT), gram))[0])


def factor(parts, rows, scale, snaps):
    rank = rows[0].shape[0]
    cells = sum(part.shape[1] for part in rows)
    return pl.pallas_call(
        lambda *refs: factor_kernel(scale, len(parts), *refs),
        in_specs=[VMEM] * (len(parts) + len(rows)),
        out_specs=[VMEM] * 2 + [pl.BlockSpec(memory_space=pltpu.SMEM)],
        out_shape=[
            pltpu.HBM((rank, cells), jnp.float32),
            pltpu.HBM((rank, snaps), jnp.float32),
            pltpu.SMEM((1, 1), jnp.float32),
        ],
        compiler_params=limit(16),
        name="factor",
    )(*parts, *rows)


def exchange(block, axis, radix):
    count = lax.axis_size(axis)
    steps = []
    step = 1
    while step < count:
        steps.append((step, min(radix, count // step)))
        step *= steps[-1][1]
    parts = [block]
    for step, group in steps:
        order = list(range(group - 1, 0, -1))
        if step * group == count and group == 4:
            order = [2, 3, 1]
        block = tree_sum(parts)
        parts = [block] + [swap(block, axis, step * at) for at in order]
    return parts


def shards(snapshots, sketch):
    scale = math.sqrt(snapshots.shape[0] * lax.axis_size("cells"))

    columns = snapshots.shape[1]

    def again(basis):
        rows, block = project([basis], in_hbm(snapshots), 0, [])
        return factor(exchange(block, "cells", 4), [rows], scale, columns)

    early, held = sketch_rows(snapshots, sketch)
    early = exchange(early, "snaps", 2)
    late = exchange(sketch_rest(held, sketch), "snaps", 2)
    early, block = project(early, held, 0, [])
    late, block = project(late, held, first_share(held.shape[0]), [block])
    first = factor(exchange(block, "cells", 4), [early, late], scale, columns)
    basis, coefficients, _, _ = lax.while_loop(
        lambda state: jnp.logical_and(state[2][0, 0] > AMPLIFIED, state[3] < PASSES),
        lambda state: (*again(state[0]), state[3] + 1),
        (*first, jnp.int32(0)),
    )
    return (basis, coefficients)


def solution(mesh):
    return jax.shard_map(
        shards,
        mesh=mesh,
        in_specs=(P("cells", "snaps"), P("snaps", None)),
        out_specs=(P(None, "cells"), P(None, "snaps")),
        check_vma=False,
    )
```

```python
import math

import jax
import jax.numpy as jnp
from jax import lax
from jax.experimental import pallas as pl
from jax.experimental.pallas import tpu as pltpu
from jax.sharding import PartitionSpec as P

LANES = 128
CHUNK = 256
MIB = 1 << 20
AMPLIFIED = 512.0
BROKEN = 2e5
SHIFT = 3e-5
PASSES = 8
VMEM = pl.BlockSpec(memory_space=pltpu.VMEM)
HBM = pl.BlockSpec(memory_space=pltpu.HBM)


def limit(mebibytes):
    return pltpu.CompilerParams(vmem_limit_bytes=mebibytes * MIB)


def in_hbm(block):
    return pltpu.with_memory_space_constraint(block, pltpu.HBM)


def swap(block, axis, offset):
    count = lax.axis_size(axis)
    return lax.ppermute(block, axis, [(at, at ^ offset) for at in range(count)])


def tree_sum(parts):
    while len(parts) > 1:
        parts = [parts[at] + parts[at + 1] for at in range(0, len(parts), 2)]
    return parts[0]


def thirds(block):
    high, middle = halves(block)
    rest = block - high.astype(jnp.float32)
    low = (rest - middle.astype(jnp.float32)).astype(jnp.bfloat16)
    return high, middle, low


def halves(block):
    high = block.astype(jnp.bfloat16)
    return high, (block - high.astype(jnp.float32)).astype(jnp.bfloat16)


def product(left, right, right_dim):
    rank = left.shape[0] // 3
    dims = (((1,), (right_dim,)), ((), ()))
    high, middle, low = [
        lax.dot_general(left[:rank * (3 - at)], part, dims, preferred_element_type=jnp.float32)
        for at, part in enumerate(right)
    ]
    small = high[2 * rank:] + (middle[rank:] + low)
    return high[:rank] + ((high[rank:2 * rank] + middle[:rank]) + small)


def pieces(cells):
    if cells % 8:
        return [(0, cells)]
    return [(0, cells // 8), (cells // 8, cells // 8 * 3), (cells // 2, cells // 2)]


def multiply(sketch, held, out_ref, start, size, base):
    chunk = math.gcd(CHUNK, size)
    for at in range(start, start + size, chunk):
        out_ref[:, pl.ds(at - base, chunk)] = product(sketch, thirds(held[pl.ds(at, chunk), :].T), 0)


def first_kernel(sketch_ref, snapshots_ref, out_ref, held, sketch_held, arrived):
    fetches = pieces(held.shape[0])
    first = pltpu.make_async_copy(sketch_ref, sketch_held, arrived.at[len(fetches)])
    first.start()
    copies = []
    for at, (start, size) in enumerate(fetches):
        rows = pl.ds(start, size)
        copies.append(pltpu.make_async_copy(snapshots_ref.at[rows], held.at[rows], arrived.at[at]))
        copies[-1].start()
    first.wait()
    sketch = jnp.concatenate(thirds(sketch_held[...]), axis=0)
    for copy, (start, size) in zip(copies, fetches):
        if start < out_ref.shape[1]:
            copy.wait()
            multiply(sketch, held, out_ref, start, size, 0)
    copies[-1].wait()


def second_kernel(sketch_ref, held, out_ref):
    sketch = jnp.concatenate(thirds(sketch_ref[...]), axis=0)
    half = out_ref.shape[1]
    multiply(sketch, held, out_ref, half, half, half)


def sketch_rows(snapshots, sketch):
    cells, snaps = snapshots.shape
    rank = sketch.shape[1]
    return pl.pallas_call(
        first_kernel,
        in_specs=[HBM] * 2,
        out_specs=[VMEM] * 2,
        out_shape=[
            pltpu.VMEM((rank, cells // 2), jnp.float32),
            pltpu.VMEM((cells, snaps), jnp.float32),
        ],
        scratch_shapes=[
            pltpu.VMEM((rank, snaps), jnp.float32),
            pltpu.SemaphoreType.DMA((len(pieces(cells)) + 1,)),
        ],
        compiler_params=limit(16),
        name="sketch_first",
    )(in_hbm(sketch.T), in_hbm(snapshots))


def sketch_rest(held, sketch):
    cells, snaps = held.shape
    rank = sketch.shape[1]
    return pl.pallas_call(
        second_kernel,
        in_specs=[VMEM] * 2,
        out_specs=VMEM,
        out_shape=pltpu.VMEM((rank, cells // 2), jnp.float32),
        compiler_params=limit(16),
        cost_estimate=pl.CostEstimate(flops=6 * rank * cells * snaps, bytes_accessed=4 * cells * snaps, transcendentals=0),
        name="sketch_second",
    )(sketch.T, held)


def packed(gram):
    rank = gram.shape[0]
    high = rank * rank // LANES
    return jnp.concatenate([gram[at:at + high] for at in range(0, rank, high)], axis=1)


def project_kernel(parts, start, *refs):
    snapshots_ref = refs[parts]
    before = refs[parts + 1:-2]
    rows_ref, block_ref = refs[-2:]
    rank, cells = rows_ref.shape
    snaps = snapshots_ref.shape[1]
    chunk = math.gcd(CHUNK, cells)
    sums = jnp.zeros((2 * rank, snaps), jnp.float32)
    first = jnp.zeros((3 * rank, rank), jnp.float32)
    second = jnp.zeros((rank, rank), jnp.float32)
    for at in range(0, cells, chunk):
        span = pl.ds(at, chunk)
        rows = tree_sum([ref[:, span] for ref in refs[:parts]])
        rows_ref[:, span] = rows
        exact = thirds(rows)
        left = jnp.concatenate(exact, axis=0)
        for part in halves(snapshots_ref[pl.ds(start + at, chunk), :]):
            sums += jnp.dot(left[:2 * rank], part, preferred_element_type=jnp.float32)
        against = (((1,), (1,)), ((), ()))
        first += lax.dot_general(left, exact[0], against, preferred_element_type=jnp.float32)
        second += lax.dot_general(exact[1], exact[1], against, preferred_element_type=jnp.float32)
    sums = sums[:rank] + sums[rank:]
    small = first[rank:2 * rank] + first[2 * rank:]
    gram = first[:rank] + ((small + small.T) + second)
    tiles = snaps // LANES
    found = [sums[:, at * LANES:(at + 1) * LANES] for at in range(tiles)]
    found = jnp.concatenate(found + [packed(gram)], axis=0)
    for ref in before:
        found += ref[...]
    block_ref[...] = found


def project(parts, snapshots, start, before):
    snaps = snapshots.shape[1]
    rank, cells = parts[0].shape
    return pl.pallas_call(
        lambda *refs: project_kernel(len(parts), start, *refs),
        in_specs=[VMEM] * (len(parts) + 1 + len(before)),
        out_specs=[VMEM] * 2,
        out_shape=[
            pltpu.VMEM((rank, cells), jnp.float32),
            pltpu.VMEM((rank * (snaps + rank) // LANES, LANES), jnp.float32),
        ],
        compiler_params=limit(16),
        cost_estimate=pl.CostEstimate(flops=5 * rank * cells * snaps, bytes_accessed=4 * cells * snaps, transcendentals=0),
        name="project",
    )(*parts, snapshots, *before)


def spread(row):
    return jnp.broadcast_to(row, (8, row.shape[1]))


def tall(tile, rank):
    return jnp.concatenate([tile] * (rank // 8), axis=0)


def lower_inverse(gram):
    rank, lanes = gram.shape
    block = math.gcd(rank, 4)
    row_at = lax.broadcasted_iota(jnp.int32, (rank, lanes), 0)
    lane_at = lax.broadcasted_iota(jnp.int32, (rank, lanes), 1)
    both = jnp.where(lane_at < rank, gram, jnp.where(lane_at == row_at + rank, 1.0, 0.0))
    pivots = jnp.ones((rank, lanes), jnp.float32)
    diagonal = jnp.sum(jnp.where(row_at == lane_at, gram, 0.0), axis=0, keepdims=True)
    columns = [jnp.broadcast_to(both[:, at:at + 1], (rank, lanes)) for at in range(block)]
    for base in range(0, rank, block):
        later = range(base + block, min(base + 2 * block, rank))
        upcoming = [jnp.broadcast_to(both[:, at:at + 1], (rank, lanes)) for at in later]
        corner = [[spread(columns[at][base + to:base + to + 1]) for at in range(block)] for to in range(block)]
        rows = [spread(both[base + at:base + at + 1]) for at in range(block)]
        for at in range(block):
            pivot = corner[at][at]
            inverse = 1.0 / pivot
            for to in range(at + 1, block):
                ratio = corner[to][at] * inverse
                rows[to] = rows[to] - ratio * rows[at]
                columns[to] = columns[to] - tall(ratio, rank) * columns[at]
                for along in range(at + 1, block):
                    corner[to][along] = corner[to][along] - ratio * corner[at][along]
            factor = jnp.where(row_at > base + at, columns[at] * tall(inverse, rank), 0.0)
            both = both - factor * tall(rows[at], rank)
            for to, place in enumerate(later):
                upcoming[to] = upcoming[to] - factor * tall(spread(columns[at][place:place + 1]), rank)
            pivots = jnp.where(row_at == base + at, tall(pivot, rank), pivots)
        columns = upcoming
    inverse = (both * lax.rsqrt(pivots))[:, rank:2 * rank]
    return inverse, jnp.sum(inverse * inverse * diagonal[:, :rank])


def factor_kernel(scale, parts, *refs):
    rows_refs = refs[parts:-3]
    basis_ref, coefficients_ref, amplified_ref = refs[-3:]
    snaps = coefficients_ref.shape[1]
    block = tree_sum([ref[...] for ref in refs[:parts]])
    rank = basis_ref.shape[0]
    tiles = snaps // LANES
    full = block[tiles * rank:]
    turns = [full] + [pltpu.roll(full, LANES - at, 1) for at in range(rank, LANES, rank)]
    gram = jnp.concatenate(turns, axis=0)
    inverse, amplified = lower_inverse(gram)
    sound = amplified <= BROKEN
    amplified_ref[0, 0] = jnp.where(sound, amplified, BROKEN)

    def apply(inverse):
        left = jnp.concatenate(thirds(inverse), axis=0)
        for at in range(tiles):
            part = block[at * rank:(at + 1) * rank]
            coefficients_ref[:, at * LANES:(at + 1) * LANES] = product(left, thirds(part), 0)
        left = jnp.concatenate(thirds(inverse * scale), axis=0)
        base = 0
        for ref in rows_refs:
            chunk = math.gcd(CHUNK, ref.shape[1])
            for at in range(0, ref.shape[1], chunk):
                basis_ref[:, pl.ds(base + at, chunk)] = product(left, thirds(ref[:, pl.ds(at, chunk)]), 0)
            base += ref.shape[1]

    apply(inverse)

    @pl.when(jnp.logical_not(sound))
    def _():
        row_at = lax.broadcasted_iota(jnp.int32, gram.shape, 0)
        lane_at = lax.broadcasted_iota(jnp.int32, gram.shape, 1)
        apply(lower_inverse(jnp.where(row_at == lane_at, gram * (1 + SHIFT), gram))[0])


def factor(parts, rows, scale, snaps):
    rank = rows[0].shape[0]
    cells = sum(part.shape[1] for part in rows)
    return pl.pallas_call(
        lambda *refs: factor_kernel(scale, len(parts), *refs),
        in_specs=[VMEM] * (len(parts) + len(rows)),
        out_specs=[VMEM] * 2 + [pl.BlockSpec(memory_space=pltpu.SMEM)],
        out_shape=[
            pltpu.HBM((rank, cells), jnp.float32),
            pltpu.HBM((rank, snaps), jnp.float32),
            pltpu.SMEM((1, 1), jnp.float32),
        ],
        compiler_params=limit(16),
        name="factor",
    )(*parts, *rows)


def exchange(block, axis, radix):
    count = lax.axis_size(axis)
    steps = []
    step = 1
    while step < count:
        steps.append((step, min(radix, count // step)))
        step *= steps[-1][1]
    parts = [block]
    for step, group in steps:
        order = list(range(group - 1, 0, -1))
        if step * group == count and group == 4:
            order = [2, 3, 1]
        block = tree_sum(parts)
        parts = [block] + [swap(block, axis, step * at) for at in order]
    return parts


def shards(snapshots, sketch):
    scale = math.sqrt(snapshots.shape[0] * lax.axis_size("cells"))

    columns = snapshots.shape[1]

    def again(basis):
        rows, block = project([basis], in_hbm(snapshots), 0, [])
        return factor(exchange(block, "cells", 4), [rows], scale, columns)

    early, held = sketch_rows(snapshots, sketch)
    early = exchange(early, "snaps", 2)
    late = exchange(sketch_rest(held, sketch), "snaps", 2)
    early, block = project(early, held, 0, [])
    late, block = project(late, held, held.shape[0] // 2, [block])
    first = factor(exchange(block, "cells", 4), [early, late], scale, columns)
    basis, coefficients, _, _ = lax.while_loop(
        lambda state: jnp.logical_and(state[2][0, 0] > AMPLIFIED, state[3] < PASSES),
        lambda state: (*again(state[0]), state[3] + 1),
        (*first, jnp.int32(0)),
    )
    return (basis, coefficients)


def solution(mesh):
    return jax.shard_map(
        shards,
        mesh=mesh,
        in_specs=(P("cells", "snaps"), P("snaps", None)),
        out_specs=(P(None, "cells"), P(None, "snaps")),
        check_vma=False,
    )
```

```python
import math

import jax
import jax.numpy as jnp
from jax import lax
from jax.experimental import pallas as pl
from jax.experimental.pallas import tpu as pltpu
from jax.sharding import PartitionSpec as P

LANES = 128
CHUNK = 256
MIB = 1 << 20
AMPLIFIED = 512.0
BROKEN = 2e5
SHIFT = 3e-5
PASSES = 8
VMEM = pl.BlockSpec(memory_space=pltpu.VMEM)
HBM = pl.BlockSpec(memory_space=pltpu.HBM)


def limit(mebibytes):
    return pltpu.CompilerParams(vmem_limit_bytes=mebibytes * MIB)


def in_hbm(block):
    return pltpu.with_memory_space_constraint(block, pltpu.HBM)


def swap(block, axis, offset):
    count = lax.axis_size(axis)
    return lax.ppermute(block, axis, [(at, at ^ offset) for at in range(count)])


def tree_sum(parts):
    while len(parts) > 1:
        parts = [parts[at] + parts[at + 1] for at in range(0, len(parts), 2)]
    return parts[0]


def thirds(block):
    high, middle = halves(block)
    rest = block - high.astype(jnp.float32)
    low = (rest - middle.astype(jnp.float32)).astype(jnp.bfloat16)
    return high, middle, low


def halves(block):
    high = block.astype(jnp.bfloat16)
    return high, (block - high.astype(jnp.float32)).astype(jnp.bfloat16)


def product(left, right, right_dim):
    rank = left.shape[0] // 3
    dims = (((1,), (right_dim,)), ((), ()))
    high, middle, low = [
        lax.dot_general(left[:rank * (3 - at)], part, dims, preferred_element_type=jnp.float32)
        for at, part in enumerate(right)
    ]
    small = high[2 * rank:] + (middle[rank:] + low)
    return high[:rank] + ((high[rank:2 * rank] + middle[:rank]) + small)


def pieces(cells):
    if cells % 16:
        return [(0, cells)]
    return [(0, cells // 16), (cells // 16, cells // 16 * 7), (cells // 2, cells // 2)]


def multiply(sketch, held, out_ref, start, size, base):
    chunk = math.gcd(CHUNK, size)
    for at in range(start, start + size, chunk):
        out_ref[:, pl.ds(at - base, chunk)] = product(sketch, thirds(held[pl.ds(at, chunk), :].T), 0)


def first_kernel(sketch_ref, snapshots_ref, out_ref, held, sketch_held, arrived):
    fetches = pieces(held.shape[0])
    first = pltpu.make_async_copy(sketch_ref, sketch_held, arrived.at[len(fetches)])
    first.start()
    copies = []
    for at, (start, size) in enumerate(fetches):
        rows = pl.ds(start, size)
        copies.append(pltpu.make_async_copy(snapshots_ref.at[rows], held.at[rows], arrived.at[at]))
        copies[-1].start()
    first.wait()
    sketch = jnp.concatenate(thirds(sketch_held[...]), axis=0)
    for copy, (start, size) in zip(copies, fetches):
        if start < out_ref.shape[1]:
            copy.wait()
            multiply(sketch, held, out_ref, start, size, 0)
    copies[-1].wait()


def second_kernel(sketch_ref, held, out_ref):
    sketch = jnp.concatenate(thirds(sketch_ref[...]), axis=0)
    half = out_ref.shape[1]
    multiply(sketch, held, out_ref, half, half, half)


def sketch_rows(snapshots, sketch):
    cells, snaps = snapshots.shape
    rank = sketch.shape[1]
    return pl.pallas_call(
        first_kernel,
        in_specs=[HBM] * 2,
        out_specs=[VMEM] * 2,
        out_shape=[
            pltpu.VMEM((rank, cells // 2), jnp.float32),
            pltpu.VMEM((cells, snaps), jnp.float32),
        ],
        scratch_shapes=[
            pltpu.VMEM((rank, snaps), jnp.float32),
            pltpu.SemaphoreType.DMA((len(pieces(cells)) + 1,)),
        ],
        compiler_params=limit(16),
        name="sketch_first",
    )(in_hbm(sketch.T), in_hbm(snapshots))


def sketch_rest(held, sketch):
    cells, snaps = held.shape
    rank = sketch.shape[1]
    return pl.pallas_call(
        second_kernel,
        in_specs=[VMEM] * 2,
        out_specs=VMEM,
        out_shape=pltpu.VMEM((rank, cells // 2), jnp.float32),
        compiler_params=limit(16),
        cost_estimate=pl.CostEstimate(flops=6 * rank * cells * snaps, bytes_accessed=4 * cells * snaps, transcendentals=0),
        name="sketch_second",
    )(sketch.T, held)


def packed(gram):
    rank = gram.shape[0]
    high = rank * rank // LANES
    return jnp.concatenate([gram[at:at + high] for at in range(0, rank, high)], axis=1)


def project_kernel(parts, start, *refs):
    snapshots_ref = refs[parts]
    before = refs[parts + 1:-2]
    rows_ref, block_ref = refs[-2:]
    rank, cells = rows_ref.shape
    snaps = snapshots_ref.shape[1]
    chunk = math.gcd(CHUNK, cells)
    sums = jnp.zeros((2 * rank, snaps), jnp.float32)
    first = jnp.zeros((3 * rank, rank), jnp.float32)
    second = jnp.zeros((rank, rank), jnp.float32)
    for at in range(0, cells, chunk):
        span = pl.ds(at, chunk)
        rows = tree_sum([ref[:, span] for ref in refs[:parts]])
        rows_ref[:, span] = rows
        exact = thirds(rows)
        left = jnp.concatenate(exact, axis=0)
        for part in halves(snapshots_ref[pl.ds(start + at, chunk), :]):
            sums += jnp.dot(left[:2 * rank], part, preferred_element_type=jnp.float32)
        against = (((1,), (1,)), ((), ()))
        first += lax.dot_general(left, exact[0], against, preferred_element_type=jnp.float32)
        second += lax.dot_general(exact[1], exact[1], against, preferred_element_type=jnp.float32)
    sums = sums[:rank] + sums[rank:]
    small = first[rank:2 * rank] + first[2 * rank:]
    gram = first[:rank] + ((small + small.T) + second)
    tiles = snaps // LANES
    found = [sums[:, at * LANES:(at + 1) * LANES] for at in range(tiles)]
    found = jnp.concatenate(found + [packed(gram)], axis=0)
    for ref in before:
        found += ref[...]
    block_ref[...] = found


def project(parts, snapshots, start, before):
    snaps = snapshots.shape[1]
    rank, cells = parts[0].shape
    return pl.pallas_call(
        lambda *refs: project_kernel(len(parts), start, *refs),
        in_specs=[VMEM] * (len(parts) + 1 + len(before)),
        out_specs=[VMEM] * 2,
        out_shape=[
            pltpu.VMEM((rank, cells), jnp.float32),
            pltpu.VMEM((rank * (snaps + rank) // LANES, LANES), jnp.float32),
        ],
        compiler_params=limit(16),
        cost_estimate=pl.CostEstimate(flops=5 * rank * cells * snaps, bytes_accessed=4 * cells * snaps, transcendentals=0),
        name="project",
    )(*parts, snapshots, *before)


def spread(row):
    return jnp.broadcast_to(row, (8, row.shape[1]))


def tall(tile, rank):
    return jnp.concatenate([tile] * (rank // 8), axis=0)


def lower_inverse(gram):
    rank, lanes = gram.shape
    block = math.gcd(rank, 4)
    row_at = lax.broadcasted_iota(jnp.int32, (rank, lanes), 0)
    lane_at = lax.broadcasted_iota(jnp.int32, (rank, lanes), 1)
    both = jnp.where(lane_at < rank, gram, jnp.where(lane_at == row_at + rank, 1.0, 0.0))
    pivots = jnp.ones((rank, lanes), jnp.float32)
    diagonal = jnp.sum(jnp.where(row_at == lane_at, gram, 0.0), axis=0, keepdims=True)
    columns = [jnp.broadcast_to(both[:, at:at + 1], (rank, lanes)) for at in range(block)]
    for base in range(0, rank, block):
        later = range(base + block, min(base + 2 * block, rank))
        upcoming = [jnp.broadcast_to(both[:, at:at + 1], (rank, lanes)) for at in later]
        corner = [[spread(columns[at][base + to:base + to + 1]) for at in range(block)] for to in range(block)]
        rows = [spread(both[base + at:base + at + 1]) for at in range(block)]
        for at in range(block):
            pivot = corner[at][at]
            inverse = 1.0 / pivot
            for to in range(at + 1, block):
                ratio = corner[to][at] * inverse
                rows[to] = rows[to] - ratio * rows[at]
                columns[to] = columns[to] - tall(ratio, rank) * columns[at]
                for along in range(at + 1, block):
                    corner[to][along] = corner[to][along] - ratio * corner[at][along]
            factor = jnp.where(row_at > base + at, columns[at] * tall(inverse, rank), 0.0)
            both = both - factor * tall(rows[at], rank)
            for to, place in enumerate(later):
                upcoming[to] = upcoming[to] - factor * tall(spread(columns[at][place:place + 1]), rank)
            pivots = jnp.where(row_at == base + at, tall(pivot, rank), pivots)
        columns = upcoming
    inverse = (both * lax.rsqrt(pivots))[:, rank:2 * rank]
    return inverse, jnp.sum(inverse * inverse * diagonal[:, :rank])


def factor_kernel(scale, parts, *refs):
    rows_refs = refs[parts:-3]
    basis_ref, coefficients_ref, amplified_ref = refs[-3:]
    snaps = coefficients_ref.shape[1]
    block = tree_sum([ref[...] for ref in refs[:parts]])
    rank = basis_ref.shape[0]
    tiles = snaps // LANES
    full = block[tiles * rank:]
    turns = [full] + [pltpu.roll(full, LANES - at, 1) for at in range(rank, LANES, rank)]
    gram = jnp.concatenate(turns, axis=0)
    inverse, amplified = lower_inverse(gram)
    sound = amplified <= BROKEN
    amplified_ref[0, 0] = jnp.where(sound, amplified, BROKEN)

    def apply(inverse):
        left = jnp.concatenate(thirds(inverse), axis=0)
        for at in range(tiles):
            part = block[at * rank:(at + 1) * rank]
            coefficients_ref[:, at * LANES:(at + 1) * LANES] = product(left, thirds(part), 0)
        left = jnp.concatenate(thirds(inverse * scale), axis=0)
        base = 0
        for ref in rows_refs:
            chunk = math.gcd(CHUNK, ref.shape[1])
            for at in range(0, ref.shape[1], chunk):
                basis_ref[:, pl.ds(base + at, chunk)] = product(left, thirds(ref[:, pl.ds(at, chunk)]), 0)
            base += ref.shape[1]

    apply(inverse)

    @pl.when(jnp.logical_not(sound))
    def _():
        row_at = lax.broadcasted_iota(jnp.int32, gram.shape, 0)
        lane_at = lax.broadcasted_iota(jnp.int32, gram.shape, 1)
        apply(lower_inverse(jnp.where(row_at == lane_at, gram * (1 + SHIFT), gram))[0])


def factor(parts, rows, scale, snaps):
    rank = rows[0].shape[0]
    cells = sum(part.shape[1] for part in rows)
    return pl.pallas_call(
        lambda *refs: factor_kernel(scale, len(parts), *refs),
        in_specs=[VMEM] * (len(parts) + len(rows)),
        out_specs=[VMEM] * 2 + [pl.BlockSpec(memory_space=pltpu.SMEM)],
        out_shape=[
            pltpu.HBM((rank, cells), jnp.float32),
            pltpu.HBM((rank, snaps), jnp.float32),
            pltpu.SMEM((1, 1), jnp.float32),
        ],
        compiler_params=limit(16),
        name="factor",
    )(*parts, *rows)


def exchange(block, axis, radix):
    count = lax.axis_size(axis)
    steps = []
    step = 1
    while step < count:
        steps.append((step, min(radix, count // step)))
        step *= steps[-1][1]
    parts = [block]
    for step, group in steps:
        order = list(range(group - 1, 0, -1))
        if step * group == count and group == 4:
            order = [2, 3, 1]
        block = tree_sum(parts)
        parts = [block] + [swap(block, axis, step * at) for at in order]
    return parts


def shards(snapshots, sketch):
    scale = math.sqrt(snapshots.shape[0] * lax.axis_size("cells"))

    columns = snapshots.shape[1]

    def again(basis):
        rows, block = project([basis], in_hbm(snapshots), 0, [])
        return factor(exchange(block, "cells", 4), [rows], scale, columns)

    early, held = sketch_rows(snapshots, sketch)
    early = exchange(early, "snaps", 2)
    late = exchange(sketch_rest(held, sketch), "snaps", 2)
    early, block = project(early, held, 0, [])
    late, block = project(late, held, held.shape[0] // 2, [block])
    first = factor(exchange(block, "cells", 4), [early, late], scale, columns)
    basis, coefficients, _, _ = lax.while_loop(
        lambda state: jnp.logical_and(state[2][0, 0] > AMPLIFIED, state[3] < PASSES),
        lambda state: (*again(state[0]), state[3] + 1),
        (*first, jnp.int32(0)),
    )
    return (basis, coefficients)


def solution(mesh):
    return jax.shard_map(
        shards,
        mesh=mesh,
        in_specs=(P("cells", "snaps"), P("snaps", None)),
        out_specs=(P(None, "cells"), P(None, "snaps")),
        check_vma=False,
    )
```
